256 devices in a mesh: seq: 32 (over y, z), head: 8 (over x, core).
Axes of the slice: x: 4, y: 4, z: 8, core: 2. Of those that a mesh axis runs over, the one named last changes fastest.
Arguments:
- document_query: bfloat16 [8192, 8192], P('seq', 'head'), may hold values from -179.09903 to 179.09903
- document_key: bfloat16 [8192, 1024], P('seq', 'head'), may hold values from -6 to 6
- document_value: bfloat16 [8192, 1024], P('seq', 'head'), may hold values from -24 to 24
- branch_token_query: bfloat16 [512, 4, 8192], P('seq', None, 'head'), may hold values from -179.09903 to 179.09903
- branch_token_key: bfloat16 [512, 4, 1024], P('seq', None, 'head'), may hold values from -9 to 9
- branch_token_value: bfloat16 [512, 4, 1024], P('seq', None, 'head'), may hold values from -24 to 24
- branch_cached_key: bfloat16 [512, 128, 1024], P('seq', None, 'head'), may hold values from -9 to 9
- branch_cached_value: bfloat16 [512, 128, 1024], P('seq', None, 'head'), may hold values from -24 to 24
- suffix_length: int32 [512], P('seq'), may hold values from 1 to 128, as said below
- out_weight: bfloat16 [8192, 5120], P('head'), may hold values from -0.0625 to 0.0625
Outputs:
- prefix_out: bfloat16 [8192, 5120], P('seq', 'head')
- branch_out: bfloat16 [512, 4, 5120], P('seq', None, 'head')
The draws below stay inside these ranges and needn't reach their ends.
Inputs may be any that keep to these rules, and one draw needn't show every extreme that they name: `suffix_length`: slots at or past a branch's length hold stale entries.
All inputs are finite; a program needn't handle non-finite values.
Results may differ from the reference program's by a relative error of at most 0.024.
Values may be sent and summed in bfloat16 or wider, within the bound.
No kernel may reach another device: no remote copies, remote signals or barrier semaphores. Data moves between devices by JAX's collectives and lax.ppermute only.
A program may use at most 128 MiB of HBM per device.

```python
import jax
import jax.numpy as jnp
from jax import lax

D = 5120
QUERY_HEADS = 64
KEY_VALUE_HEADS = 8
HEAD_SIZE = 128
SUFFIX_SLOTS = 128
NEW_TOKENS = 4
QUERY_PER_KEY = 8
PREFIX_TOKENS = 8192
BRANCH_TOTAL = 512


def prefix_base(key):
    key = jax.random.fold_in(key, 11)
    return jnp.clip(jax.random.normal(key, (PREFIX_TOKENS, KEY_VALUE_HEADS * HEAD_SIZE), jnp.float32), -6.0, 6.0)


def branch_common(key):
    key = jax.random.fold_in(key, 12)
    return jnp.clip(jax.random.normal(key, (BRANCH_TOTAL, KEY_VALUE_HEADS * HEAD_SIZE), jnp.float32), -6.0, 6.0)


def branch_fresh(key):
    key = jax.random.fold_in(key, 13)
    return jnp.clip(jax.random.normal(key, (BRANCH_TOTAL, NEW_TOKENS, KEY_VALUE_HEADS * HEAD_SIZE), jnp.float32), -6.0, 6.0)


def per_query_head(row_tally):
    leading_dims = row_tally.shape[:-1]
    scale_factor = row_tally.reshape(leading_dims + (KEY_VALUE_HEADS, 1, HEAD_SIZE))
    return jnp.broadcast_to(scale_factor, leading_dims + (KEY_VALUE_HEADS, QUERY_PER_KEY, HEAD_SIZE)).reshape(leading_dims + (QUERY_HEADS * HEAD_SIZE,))


def draw_document_key(key, part):
    base = prefix_base(key)
    return base.astype(jnp.bfloat16)


def draw_document_query(key, part):
    key = jax.random.fold_in(key, 2)
    random_jitter = 2.0 * jnp.clip(jax.random.normal(key, (PREFIX_TOKENS, QUERY_HEADS * HEAD_SIZE), jnp.float32), -6.0, 6.0)
    return random_jitter.astype(jnp.bfloat16)


def draw_branch_cached_key(key, part):
    common = branch_common(key)
    key = jax.random.fold_in(key, 3)
    random_jitter = jnp.clip(jax.random.normal(key, (BRANCH_TOTAL, SUFFIX_SLOTS, KEY_VALUE_HEADS * HEAD_SIZE), jnp.float32), -6.0, 6.0)
    return ((random_jitter + common[:, None, :]) * 0.7071).astype(jnp.bfloat16)


def draw_branch_token_key(key, part):
    common = branch_common(key)
    fresh = branch_fresh(key)
    return ((fresh + common[:, None, :]) * 0.7071).astype(jnp.bfloat16)


def draw_branch_token_query(key, part):
    common = branch_common(key)
    fresh = branch_fresh(key)
    key = jax.random.fold_in(key, 5)
    random_jitter = 2.0 * jnp.clip(jax.random.normal(key, (BRANCH_TOTAL, NEW_TOKENS, QUERY_HEADS * HEAD_SIZE), jnp.float32), -6.0, 6.0)
    result = random_jitter + per_query_head(0.33 * common[:, None, :] + 0.55 * fresh)
    return result.astype(jnp.bfloat16)


def draw_suffix_length(key, part):
    key = jax.random.fold_in(key, 6)
    lengths = jax.random.randint(key, (BRANCH_TOTAL,), 1, SUFFIX_SLOTS + 1, dtype=jnp.int32)
    position = jnp.arange(BRANCH_TOTAL, dtype=jnp.int32)
    lengths = jnp.where(position % 7 == 3, SUFFIX_SLOTS, lengths)
    lengths = jnp.where(position % 11 == 4, 1, lengths)
    return lengths.astype(jnp.int32)


def levels(rng, shape, shards, smallest, top_value):
    level, own = 1.0, jax.random.fold_in(rng, 6)
    for axis_at, shards_of in shards:
        draws = jnp.exp(jax.random.uniform(jax.random.fold_in(own, axis_at), (shards_of,), jnp.float32, smallest / len(shards), top_value / len(shards)))
        level = level * jnp.repeat(draws, shape[axis_at] // shards_of).reshape([-1 if axis == axis_at else 1 for axis in range(len(shape))])
    return level


def normal_values(key, shape, spread, reach, pieces=(), held_as=jnp.bfloat16):
    loudness = levels(key, shape, pieces, -0.22, 0.18) if pieces else 1.0
    drawn = jax.random.normal(key, shape, jnp.float32) * spread * loudness
    return jnp.minimum(jnp.maximum(drawn, -reach), reach).astype(held_as)


def setup_inputs(seed: int = 0) -> dict:
    seeds = jax.random.split(jax.random.key(seed), 11)
    document_query = draw_document_query(jax.random.fold_in(seeds[10], 71), 0)
    document_key = draw_document_key(jax.random.fold_in(seeds[10], 71), 0)
    document_value = normal_values(seeds[2], (PREFIX_TOKENS, KEY_VALUE_HEADS * HEAD_SIZE), 4.0, 24.0, ((0, 32), (1, 8)))
    branch_token_query = draw_branch_token_query(jax.random.fold_in(seeds[10], 71), 0)
    branch_token_key = draw_branch_token_key(jax.random.fold_in(seeds[10], 71), 0)
    branch_token_value = normal_values(seeds[5], (BRANCH_TOTAL, NEW_TOKENS, KEY_VALUE_HEADS * HEAD_SIZE), 4.0, 24.0, ((0, 32), (2, 8)))
    branch_cached_key = draw_branch_cached_key(jax.random.fold_in(seeds[10], 71), 0)
    branch_cached_value = normal_values(seeds[7], (BRANCH_TOTAL, SUFFIX_SLOTS, KEY_VALUE_HEADS * HEAD_SIZE), 4.0, 24.0, ((0, 32), (2, 8)))
    suffix_length = draw_suffix_length(jax.random.fold_in(seeds[10], 71), 0)
    out_weight = normal_values(seeds[9], (QUERY_HEADS * HEAD_SIZE, D), (QUERY_HEADS * HEAD_SIZE) ** -0.5, 0.0625, ((0, 8),))
    return dict(document_query=document_query, document_key=document_key, document_value=document_value, branch_token_query=branch_token_query, branch_token_key=branch_token_key, branch_token_value=branch_token_value, branch_cached_key=branch_cached_key, branch_cached_value=branch_cached_value, suffix_length=suffix_length, out_weight=out_weight)


def prefix_attention(document_query, document_key, document_value):
    rows_per_block = min(PREFIX_TOKENS, 256)
    count_of_blocks = PREFIX_TOKENS // rows_per_block
    query_rows = document_query.reshape(count_of_blocks, rows_per_block, KEY_VALUE_HEADS, QUERY_PER_KEY, HEAD_SIZE)
    joined_keys = document_key.reshape(PREFIX_TOKENS, KEY_VALUE_HEADS, HEAD_SIZE)
    joined_values = document_value.reshape(PREFIX_TOKENS, KEY_VALUE_HEADS, HEAD_SIZE)
    key_pos = jnp.arange(PREFIX_TOKENS, dtype=jnp.int32)

    def per_block(block_index):
        chosen = lax.dynamic_index_in_dim(query_rows, block_index, 0, keepdims=False)
        query_pos = block_index * rows_per_block + jnp.arange(rows_per_block, dtype=jnp.int32)
        keep_mask = key_pos[None, :] <= query_pos[:, None]

        def each_head_output(head_index):
            one_query = lax.dynamic_index_in_dim(chosen, head_index, 1, keepdims=False).astype(jnp.float32)
            one_key = lax.dynamic_index_in_dim(joined_keys, head_index, 1, keepdims=False).astype(jnp.float32)
            one_value = lax.dynamic_index_in_dim(joined_values, head_index, 1, keepdims=False).astype(jnp.float32)
            scores = jnp.einsum("qgd,md->qgm", one_query, one_key) * HEAD_SIZE ** -0.5
            scores = jnp.where(keep_mask[:, None, :], scores, -jnp.inf)
            row_max = jnp.max(scores, axis=-1, keepdims=True)
            weights = jnp.exp(scores - row_max)
            denoms = jnp.sum(weights, axis=-1, keepdims=True)
            rounded = lax.optimization_barrier(weights.astype(jnp.bfloat16)).astype(jnp.float32)
            mixed = jnp.einsum("qgm,md->qgd", rounded, one_value)
            return (mixed / denoms).astype(jnp.bfloat16)

        head_outputs = lax.map(each_head_output, jnp.arange(KEY_VALUE_HEADS, dtype=jnp.int32))
        return jnp.transpose(head_outputs, (1, 0, 2, 3))

    result = lax.map(per_block, jnp.arange(count_of_blocks, dtype=jnp.int32))
    return result.reshape(PREFIX_TOKENS, QUERY_HEADS * HEAD_SIZE)


def branch_attention(branch_token_query, branch_token_key, branch_token_value, branch_cached_key, branch_cached_value, suffix_length, document_key, document_value):
    rows_per_group = min(BRANCH_TOTAL, 32)
    count_of_blocks = BRANCH_TOTAL // rows_per_group
    query_rows = branch_token_query.reshape(count_of_blocks, rows_per_group, NEW_TOKENS, KEY_VALUE_HEADS, QUERY_PER_KEY, HEAD_SIZE)
    appended_keys = branch_token_key.reshape(count_of_blocks, rows_per_group, NEW_TOKENS, KEY_VALUE_HEADS, HEAD_SIZE)
    appended_values = branch_token_value.reshape(count_of_blocks, rows_per_group, NEW_TOKENS, KEY_VALUE_HEADS, HEAD_SIZE)
    cached_key_rows = branch_cached_key.reshape(count_of_blocks, rows_per_group, SUFFIX_SLOTS, KEY_VALUE_HEADS, HEAD_SIZE)
    cached_value_rows = branch_cached_value.reshape(count_of_blocks, rows_per_group, SUFFIX_SLOTS, KEY_VALUE_HEADS, HEAD_SIZE)
    lengths = suffix_length.reshape(count_of_blocks, rows_per_group)
    common_key_rows = document_key.reshape(PREFIX_TOKENS, KEY_VALUE_HEADS, HEAD_SIZE)
    common_value_rows = document_value.reshape(PREFIX_TOKENS, KEY_VALUE_HEADS, HEAD_SIZE)
    step_pos = jnp.arange(NEW_TOKENS, dtype=jnp.int32)
    slot_pos = jnp.arange(SUFFIX_SLOTS, dtype=jnp.int32)

    def per_block(block_index):
        def take_block(source):
            return lax.dynamic_index_in_dim(source, block_index, 0, keepdims=False)

        block_queries = take_block(query_rows)
        block_new_keys = take_block(appended_keys)
        block_new_values = take_block(appended_values)
        block_cache_keys = take_block(cached_key_rows)
        block_cache_values = take_block(cached_value_rows)
        block_lengths = take_block(lengths)
        cache_mask = slot_pos[None, :] < block_lengths[:, None]
        new_mask = step_pos[None, :] <= step_pos[:, None]
        keep_mask = jnp.concatenate([
            jnp.ones((rows_per_group, NEW_TOKENS, PREFIX_TOKENS), jnp.bool_),
            jnp.broadcast_to(cache_mask[:, None, :], (rows_per_group, NEW_TOKENS, SUFFIX_SLOTS)),
            jnp.broadcast_to(new_mask[None, :, :], (rows_per_group, NEW_TOKENS, NEW_TOKENS))], axis=-1)

        def each_head_output(head_index):
            def head_of(source, axis):
                return lax.dynamic_index_in_dim(source, head_index, axis, keepdims=False).astype(jnp.float32)

            one_query = head_of(block_queries, 2)
            prefix_k = head_of(common_key_rows, 1)
            prefix_v = head_of(common_value_rows, 1)
            cache_k = head_of(block_cache_keys, 2)
            cache_v = head_of(block_cache_values, 2)
            fresh_k = head_of(block_new_keys, 2)
            fresh_v = head_of(block_new_values, 2)
            scores = jnp.concatenate([
                jnp.einsum("btgd,md->btgm", one_query, prefix_k),
                jnp.einsum("btgd,bcd->btgc", one_query, cache_k),
                jnp.einsum("btgd,bud->btgu", one_query, fresh_k)], axis=-1) * HEAD_SIZE ** -0.5
            scores = jnp.where(keep_mask[:, :, None, :], scores, -jnp.inf)
            row_max = jnp.max(scores, axis=-1, keepdims=True)
            weights = jnp.exp(scores - row_max)
            denoms = jnp.sum(weights, axis=-1, keepdims=True)
            rounded = lax.optimization_barrier(weights.astype(jnp.bfloat16)).astype(jnp.float32)
            mixed = jnp.einsum("btgm,md->btgd", rounded[..., :PREFIX_TOKENS], prefix_v)
            mixed = mixed + jnp.einsum("btgc,bcd->btgd", rounded[..., PREFIX_TOKENS:PREFIX_TOKENS + SUFFIX_SLOTS], cache_v)
            mixed = mixed + jnp.einsum("btgu,bud->btgd", rounded[..., PREFIX_TOKENS + SUFFIX_SLOTS:], fresh_v)
            return (mixed / denoms).astype(jnp.bfloat16)

        head_outputs = lax.map(each_head_output, jnp.arange(KEY_VALUE_HEADS, dtype=jnp.int32))
        return jnp.transpose(head_outputs, (1, 2, 0, 3, 4))

    result = lax.map(per_block, jnp.arange(count_of_blocks, dtype=jnp.int32))
    return result.reshape(BRANCH_TOTAL * NEW_TOKENS, QUERY_HEADS * HEAD_SIZE)


def reference(document_query, document_key, document_value, branch_token_query, branch_token_key, branch_token_value, branch_cached_key, branch_cached_value, suffix_length, out_weight):
    prefix_attn = prefix_attention(document_query, document_key, document_value)
    branch_attn = branch_attention(branch_token_query, branch_token_key, branch_token_value, branch_cached_key, branch_cached_value, suffix_length, document_key, document_value)
    prefix_out = jnp.dot(prefix_attn, out_weight, preferred_element_type=jnp.float32).astype(jnp.bfloat16)
    branch_out = jnp.dot(branch_attn, out_weight, preferred_element_type=jnp.float32).astype(jnp.bfloat16)
    return prefix_out, branch_out.reshape(BRANCH_TOTAL, NEW_TOKENS, D)
```

```python
import functools
import math

import jax
import jax.numpy as jnp
from jax import lax
from jax.experimental import pallas as pl
from jax.experimental.pallas import tpu as pltpu
from jax.sharding import PartitionSpec as P

HEAD_SIZE = 128
NEW_TOKENS = 4
GROUP = 8
CHUNK = 256
TILES = 10
BRANCH_ROWS = 64
NY, NZ, NX = 4, 8, 4
SCALE = HEAD_SIZE**-0.5 * math.log2(math.e)
NEG = -1e30
VMEM = pl.BlockSpec(memory_space=pltpu.VMEM)
SMEM = pl.BlockSpec(memory_space=pltpu.SMEM)
F32 = jnp.float32
BF16 = jnp.bfloat16


def y_shift(k):
    return [(y * NZ + z, ((y + k) % NY) * NZ + z) for y in range(NY) for z in range(NZ)]


def z_shift(k):
    return [(y * NZ + z, y * NZ + (z + k) % NZ) for y in range(NY) for z in range(NZ)]


def x_shift(k):
    return [(x * 2 + c, ((x + k) % NX) * 2 + c) for x in range(NX) for c in range(2)]


def core_swap():
    return [(x * 2 + c, x * 2 + 1 - c) for x in range(NX) for c in range(2)]


def dot_nt(a, b):
    return lax.dot_general(a, b, (((1,), (1,)), ((), ())), preferred_element_type=F32)


def dot(a, b):
    return jnp.dot(a, b, preferred_element_type=F32)


def row_peak(parts):
    cols = [p[:, i : i + 128] for p in parts for i in range(0, p.shape[1], 128)]
    return jnp.max(functools.reduce(jnp.maximum, cols), axis=1, keepdims=True)


def local_kernel(
    len_ref, q_ref, kv_ref, ck_ref, cv_ref, fk_ref, fv_ref, acc_ref, m_ref, va_ref, ca_ref, fa_ref
):
    ones = jnp.ones((CHUNK, HEAD_SIZE), BF16)
    va_ref[:, :HEAD_SIZE] = kv_ref[:, HEAD_SIZE:]
    va_ref[:, HEAD_SIZE:] = ones
    fa_ref[:, :HEAD_SIZE] = fv_ref[...]
    fa_ref[:, HEAD_SIZE:] = jnp.ones((128, HEAD_SIZE), BF16)
    ca_ref[:, :HEAD_SIZE] = cv_ref[...]
    ca_ref[:, HEAD_SIZE:] = jnp.ones((ca_ref.shape[0], HEAD_SIZE), BF16)
    kt = kv_ref[:, :HEAD_SIZE].T
    row = lax.broadcasted_iota(jnp.int32, (CHUNK, CHUNK), 0)
    col = lax.broadcasted_iota(jnp.int32, (CHUNK, CHUNK), 1)
    causal = col <= row

    def doc(t, _):
        s = jnp.where(causal, dot(q_ref[t], kt), NEG)
        m = row_peak([s]) * SCALE
        p = jnp.exp2(s * SCALE - m).astype(BF16)
        m_ref[t] = jnp.broadcast_to(m, (CHUNK, 128))
        acc_ref[t] = dot(p, va_ref[...])
        return 0

    lax.fori_loop(0, GROUP, doc, 0, unroll=2)

    row_branch = (row % BRANCH_ROWS) // NEW_TOKENS
    row_token = row % NEW_TOKENS
    n_cached = ca_ref.shape[0] // CHUNK
    frow = lax.broadcasted_iota(jnp.int32, (CHUNK, 128), 0)
    fcol = lax.broadcasted_iota(jnp.int32, (CHUNK, 128), 1)
    same = (frow % BRANCH_ROWS) // NEW_TOKENS == fcol // NEW_TOKENS
    fresh_keep = same & (fcol % NEW_TOKENS <= frow % NEW_TOKENS)
    del row_token
    for t in (8, 9):
        q = q_ref[t]
        parts = [dot(q, kt)]
        for c in range(n_cached):
            s = dot_nt(q, ck_ref[c * CHUNK : (c + 1) * CHUNK, :])
            low = col < 128
            length = jnp.where(low, len_ref[2 * c], len_ref[2 * c + 1])
            owner = jnp.where(low, 2 * c, 2 * c + 1)
            keep = (row_branch == owner) & (col % 128 < length)
            parts.append(jnp.where(keep, s, NEG))
        parts.append(jnp.where(fresh_keep, dot_nt(q, fk_ref[...]), NEG))
        m = row_peak(parts) * SCALE
        m_ref[t] = jnp.broadcast_to(m, (CHUNK, 128))
        p = [jnp.exp2(s * SCALE - m).astype(BF16) for s in parts]
        total = dot(p[0], va_ref[...])
        for c in range(n_cached):
            total += dot(p[1 + c], ca_ref[c * CHUNK : (c + 1) * CHUNK, :])
        total += dot(p[-1], fa_ref[...])
        acc_ref[t] = total


def attend(q_ref, kt_ref, va_ref, acc_ref, m_ref, t, n):
    q = q_ref[t]
    parts = [dot(q, kt_ref[c]) for c in range(n)]
    old = m_ref[t]
    new = jnp.maximum(old, row_peak(parts) * SCALE)
    m_ref[t] = new
    decay = jnp.exp2(old - new)
    peak = new[:, :1]
    total = None
    for c in range(n):
        p = jnp.exp2(parts[c] * SCALE - peak).astype(BF16)
        pv = dot(p, va_ref[c])
        total = pv if total is None else total + pv
    acc_ref[t, :, :HEAD_SIZE] = acc_ref[t, :, :HEAD_SIZE] * decay + total[:, :HEAD_SIZE]
    acc_ref[t, :, HEAD_SIZE:] = acc_ref[t, :, HEAD_SIZE:] * decay + total[:, HEAD_SIZE:]


def column_kernel(counts, last, table_ref, q_ref, acc_in, m_in, *rest):
    n_src = sum(len(c) for c in counts)
    srcs = rest[:n_src]
    if last:
        out_ref, acc_ref, m_ref, kt_ref, va_ref = rest[n_src:]
    else:
        acc_ref, m_ref, kt_ref, va_ref = rest[n_src:]
    acc_ref[...] = acc_in[...]
    m_ref[...] = m_in[...]
    va_ref[:, :, HEAD_SIZE:] = jnp.ones((NY, CHUNK, HEAD_SIZE), BF16)
    at = 0
    for g, sizes in enumerate(counts):
        n = sum(sizes)
        rel = 0
        for size in sizes:
            src = srcs[at]
            at += 1
            for i in range(size):
                place = table_ref[g * 8 + rel]
                kt_ref[place] = src[i, :, :HEAD_SIZE].T
                va_ref[place, :, :HEAD_SIZE] = src[i, :, HEAD_SIZE:]
                rel += 1
        allowed = table_ref[g * 8 + 4]

        def step(t, _, n):
            attend(q_ref, kt_ref, va_ref, acc_ref, m_ref, t, n)
            return 0

        @pl.when(allowed == n)
        def _():
            lax.fori_loop(0, TILES, functools.partial(step, n=n), 0, unroll=5)

        @pl.when(allowed != n)
        def _():
            lax.fori_loop(GROUP, TILES, functools.partial(step, n=n), 0, unroll=2)

        for a in range(1, n):

            @pl.when(allowed == a)
            def _():
                lax.fori_loop(0, GROUP, functools.partial(step, n=a), 0, unroll=2)

    if last:
        for t in range(GROUP):
            o = acc_ref[t, :, :HEAD_SIZE] / acc_ref[t, :, HEAD_SIZE:]
            out_ref[:CHUNK, t * 128 : (t + 1) * 128] = o.astype(BF16)
        for t in range(GROUP, TILES):
            o = (acc_ref[t, :, :HEAD_SIZE] / acc_ref[t, :, HEAD_SIZE:]).astype(BF16)
            for i in range(4):
                h = (t - GROUP) * 4 + i
                out_ref[CHUNK:, h * 128 : (h + 1) * 128] = o[i * 64 : (i + 1) * 64]


def attend_columns(q, state, columns, table, last=False):
    counts = tuple(tuple(s.shape[0] for s in column) for column in columns)
    srcs = [s for column in columns for s in column]
    keys = sum(s.shape[0] for s in srcs) * CHUNK
    scores = TILES * CHUNK * keys
    shapes = [
        jax.ShapeDtypeStruct((TILES, CHUNK, 2 * HEAD_SIZE), F32),
        jax.ShapeDtypeStruct((TILES, CHUNK, 128), F32),
    ]
    if last:
        out_shape = [jax.ShapeDtypeStruct((CHUNK + BRANCH_ROWS, GROUP * HEAD_SIZE), BF16)]
        scratch = [pltpu.VMEM(s.shape, F32) for s in shapes]
        aliases = {}
    else:
        out_shape = shapes
        scratch = []
        aliases = {2: 0, 3: 1}
    return pl.pallas_call(
        functools.partial(column_kernel, counts, last),
        out_shape=out_shape,
        in_specs=[SMEM] + [VMEM] * (3 + len(srcs)),
        out_specs=[VMEM] * len(out_shape),
        scratch_shapes=scratch
        + [
            pltpu.VMEM((NY, HEAD_SIZE, CHUNK), BF16),
            pltpu.VMEM((NY, CHUNK, 2 * HEAD_SIZE), BF16),
        ],
        input_output_aliases=aliases,
        compiler_params=pltpu.CompilerParams(vmem_limit_bytes=40 << 20),
        cost_estimate=pl.CostEstimate(
            flops=scores * 512, bytes_accessed=8 << 20, transcendentals=scores
        ),
    )(table, q, *state, *srcs)


def project_kernel(order_ref, a_ref, w_ref, o_ref):
    del order_ref
    o_ref[...] = dot(a_ref[...], w_ref[...]).astype(BF16)


def project(attn, weight, order, width):
    rows, depth = attn.shape
    steps = order.shape[0]
    return pl.pallas_call(
        project_kernel,
        out_shape=jax.ShapeDtypeStruct((steps, rows, width), BF16),
        grid_spec=pltpu.PrefetchScalarGridSpec(
            num_scalar_prefetch=1,
            grid=(steps,),
            in_specs=[
                pl.BlockSpec((rows, depth), lambda i, o: (0, 0)),
                pl.BlockSpec((depth, width), lambda i, o: (0, o[i])),
            ],
            out_specs=pl.BlockSpec((None, rows, width), lambda i, o: (i, 0, 0)),
        ),
        compiler_params=pltpu.CompilerParams(vmem_limit_bytes=32 << 20),
        cost_estimate=pl.CostEstimate(
            flops=2 * steps * rows * depth * width,
            bytes_accessed=2 * steps * depth * width,
            transcendentals=0,
        ),
    )(order, attn, weight)


def body(
    document_query,
    document_key,
    document_value,
    branch_token_query,
    branch_token_key,
    branch_token_value,
    branch_cached_key,
    branch_cached_value,
    suffix_length,
    out_weight,
):
    seq = lax.axis_index("seq")
    head = lax.axis_index("head")
    y, z = seq // NZ, seq % NZ
    x, core = head // 2, head % 2

    def send(a, pairs):
        return lax.ppermute(a, "seq", pairs)

    kv = jnp.concatenate([document_key, document_value], axis=1)
    from_down = send(kv, y_shift(1))
    from_up = send(kv, y_shift(-1))
    from_far = send(from_down, y_shift(1))

    doc_q = document_query.reshape(CHUNK, GROUP, HEAD_SIZE).transpose(1, 0, 2)
    branch_q = (
        branch_token_query.reshape(BRANCH_ROWS, GROUP, HEAD_SIZE)
        .transpose(1, 0, 2)
        .reshape(2, CHUNK, HEAD_SIZE)
    )
    q = jnp.concatenate([doc_q, branch_q], axis=0)
    pad = ((0, 128 - BRANCH_ROWS), (0, 0))
    fresh_k = jnp.pad(branch_token_key.reshape(BRANCH_ROWS, HEAD_SIZE), pad)
    fresh_v = jnp.pad(branch_token_value.reshape(BRANCH_ROWS, HEAD_SIZE), pad)
    cached_k = branch_cached_key.reshape(-1, HEAD_SIZE)
    cached_v = branch_cached_value.reshape(-1, HEAD_SIZE)
    state = pl.pallas_call(
        local_kernel,
        out_shape=[
            jax.ShapeDtypeStruct((TILES, CHUNK, 2 * HEAD_SIZE), F32),
            jax.ShapeDtypeStruct((TILES, CHUNK, 128), F32),
        ],
        in_specs=[SMEM] + [VMEM] * 6,
        out_specs=[VMEM] * 2,
        scratch_shapes=[
            pltpu.VMEM((CHUNK, 2 * HEAD_SIZE), BF16),
            pltpu.VMEM((cached_v.shape[0], 2 * HEAD_SIZE), BF16),
            pltpu.VMEM((128, 2 * HEAD_SIZE), BF16),
        ],
        compiler_params=pltpu.CompilerParams(vmem_limit_bytes=40 << 20),
        cost_estimate=pl.CostEstimate(
            flops=4 << 30, bytes_accessed=8 << 20, transcendentals=2 << 20
        ),
    )(suffix_length, q, kv, cached_k, cached_v, fresh_k, fresh_v)

    step = jnp.arange(NY, dtype=jnp.int32)
    ascending = (y + step) % NY

    def column_table(shift):
        other = (z + shift) % NZ
        allowed = y + jnp.where(other < z, 1, 0)
        return jnp.concatenate(
            [ascending, allowed[None], jnp.zeros((3,), jnp.int32)]
        ).astype(jnp.int32)

    mates = ascending[1:]
    mates = jnp.where(mates > y, mates - 1, mates)
    own_table = jnp.concatenate([mates, jnp.zeros((1,), jnp.int32), y[None], jnp.zeros((3,), jnp.int32)])

    column = jnp.stack([kv, from_up, from_far, from_down])
    right = send(column, z_shift(1))
    left = send(column, z_shift(-1))
    state = attend_columns(q, state, [[column[1:]]], own_table.astype(jnp.int32))
    for s in (1, 2, 3):
        if s < 3:
            next_right = send(right, z_shift(1))
            next_left = send(left, z_shift(-1))
        else:
            next_right = send(right[:2], z_shift(1))
            next_left = send(left[2:], z_shift(-1))
        table = jnp.concatenate([column_table(-s), column_table(s)])
        state = attend_columns(q, state, [[right], [left]], table)
        right, left = next_right, next_left
    (attn,) = attend_columns(q, state, [[right, left]], column_table(4), last=True)

    width = out_weight.shape[1] // (2 * NX)
    targets = (x + jnp.arange(NX, dtype=jnp.int32)) % NX
    theirs = project(attn, out_weight, (targets * 2 + 1 - core).astype(jnp.int32), width)
    swapped = lax.ppermute(theirs, "head", core_swap())
    mine = project(attn, out_weight, (targets * 2 + core).astype(jnp.int32), width)
    part = [
        (mine[k].astype(F32) + swapped[k].astype(F32)).astype(BF16) for k in range(NX)
    ]
    got = [lax.ppermute(part[k], "head", x_shift(k)) for k in (2, 1, 3)]
    total = part[0].astype(F32)
    for g in got:
        total = total + g.astype(F32)
    total = total.astype(BF16)
    return total[:CHUNK], total[CHUNK:].reshape(-1, NEW_TOKENS, width)


def solution(mesh):
    placed = (
        P("seq", "head"),
        P("seq", "head"),
        P("seq", "head"),
        P("seq", None, "head"),
        P("seq", None, "head"),
        P("seq", None, "head"),
        P("seq", None, "head"),
        P("seq", None, "head"),
        P("seq"),
        P("head", None),
    )
    return jax.shard_map(
        body,
        mesh=mesh,
        in_specs=placed,
        out_specs=(P("seq", "head"), P("seq", None, "head")),
        check_vma=False,
    )
```

```python
import functools
import math

import jax
import jax.numpy as jnp
from jax import lax
from jax.experimental import pallas as pl
from jax.experimental.pallas import tpu as pltpu
from jax.sharding import PartitionSpec as P

HEAD_SIZE = 128
NEW_TOKENS = 4
GROUP = 8
CHUNK = 256
TILES = 10
BRANCH_ROWS = 64
NY, NZ, NX = 4, 8, 4
SCALE = HEAD_SIZE**-0.5 * math.log2(math.e)
NEG = -1e30
VMEM = pl.BlockSpec(memory_space=pltpu.VMEM)
SMEM = pl.BlockSpec(memory_space=pltpu.SMEM)
F32 = jnp.float32
BF16 = jnp.bfloat16


def y_shift(k):
    return [(y * NZ + z, ((y + k) % NY) * NZ + z) for y in range(NY) for z in range(NZ)]


def z_shift(k):
    return [(y * NZ + z, y * NZ + (z + k) % NZ) for y in range(NY) for z in range(NZ)]


def x_shift(k):
    return [(x * 2 + c, ((x + k) % NX) * 2 + c) for x in range(NX) for c in range(2)]


def core_swap():
    return [(x * 2 + c, x * 2 + 1 - c) for x in range(NX) for c in range(2)]


def dot_nt(a, b):
    return lax.dot_general(a, b, (((1,), (1,)), ((), ())), preferred_element_type=F32)


def dot(a, b):
    return jnp.dot(a, b, preferred_element_type=F32)


def row_peak(parts):
    cols = [p[:, i : i + 128] for p in parts for i in range(0, p.shape[1], 128)]
    return jnp.max(functools.reduce(jnp.maximum, cols), axis=1, keepdims=True)


def keys_of(chunk):
    return jnp.concatenate([chunk[:HEAD_SIZE], chunk[HEAD_SIZE : 2 * HEAD_SIZE]], axis=1)


def pack_kernel(k_ref, v_ref, o_ref):
    kt = k_ref[...].T
    o_ref[:HEAD_SIZE, :] = kt[:, :HEAD_SIZE]
    o_ref[HEAD_SIZE:CHUNK, :] = kt[:, HEAD_SIZE:]
    o_ref[CHUNK:, :] = v_ref[...]


def pack(k, v):
    return pl.pallas_call(
        pack_kernel,
        out_shape=jax.ShapeDtypeStruct((2 * CHUNK, HEAD_SIZE), BF16),
        in_specs=[VMEM] * 2,
        out_specs=VMEM,
    )(k, v)


def local_kernel(
    len_ref, dq_ref, bq_ref, kv_ref, ck_ref, cv_ref, fk_ref, fv_ref, q_ref, acc_ref, m_ref, va_ref, ca_ref, fa_ref
):
    for h in range(GROUP):
        lanes = slice(h * HEAD_SIZE, (h + 1) * HEAD_SIZE)
        q_ref[h] = dq_ref[:, lanes]
        rows = slice((h % 4) * BRANCH_ROWS, (h % 4 + 1) * BRANCH_ROWS)
        q_ref[GROUP + h // 4, rows, :] = bq_ref[:, lanes]
    va_ref[:, :HEAD_SIZE] = kv_ref[CHUNK:, :]
    va_ref[:, HEAD_SIZE:] = jnp.ones((CHUNK, HEAD_SIZE), BF16)
    fa_ref[:, :HEAD_SIZE] = fv_ref[...]
    fa_ref[:, HEAD_SIZE:] = jnp.ones((128, HEAD_SIZE), BF16)
    ca_ref[:, :HEAD_SIZE] = cv_ref[...]
    ca_ref[:, HEAD_SIZE:] = jnp.ones((ca_ref.shape[0], HEAD_SIZE), BF16)
    kt = keys_of(kv_ref)
    row = lax.broadcasted_iota(jnp.int32, (CHUNK, CHUNK), 0)
    col = lax.broadcasted_iota(jnp.int32, (CHUNK, CHUNK), 1)
    causal = col <= row

    def doc(t, _):
        s = jnp.where(causal, dot(q_ref[t], kt), NEG)
        m = row_peak([s]) * SCALE
        p = jnp.exp2(s * SCALE - m).astype(BF16)
        m_ref[t] = jnp.broadcast_to(m, (CHUNK, 128))
        acc_ref[t] = dot(p, va_ref[...])
        return 0

    lax.fori_loop(0, GROUP, doc, 0, unroll=4)

    row_branch = (row % BRANCH_ROWS) // NEW_TOKENS
    n_cached = ca_ref.shape[0] // CHUNK
    frow = lax.broadcasted_iota(jnp.int32, (CHUNK, 128), 0)
    fcol = lax.broadcasted_iota(jnp.int32, (CHUNK, 128), 1)
    same = (frow % BRANCH_ROWS) // NEW_TOKENS == fcol // NEW_TOKENS
    fresh_keep = same & (fcol % NEW_TOKENS <= frow % NEW_TOKENS)
    low = col < 128
    for t in (8, 9):
        q = q_ref[t]
        parts = [dot(q, kt)]
        for c in range(n_cached):
            s = dot_nt(q, ck_ref[c * CHUNK : (c + 1) * CHUNK, :])
            length = jnp.where(low, len_ref[2 * c], len_ref[2 * c + 1])
            owner = jnp.where(low, 2 * c, 2 * c + 1)
            keep = (row_branch == owner) & (col % 128 < length)
            parts.append(jnp.where(keep, s, NEG))
        parts.append(jnp.where(fresh_keep, dot_nt(q, fk_ref[...]), NEG))
        m = row_peak(parts) * SCALE
        m_ref[t] = jnp.broadcast_to(m, (CHUNK, 128))
        p = [jnp.exp2(s * SCALE - m).astype(BF16) for s in parts]
        total = dot(p[0], va_ref[...])
        for c in range(n_cached):
            total += dot(p[1 + c], ca_ref[c * CHUNK : (c + 1) * CHUNK, :])
        total += dot(p[-1], fa_ref[...])
        acc_ref[t] = total


def accumulate(flag_ref, q_ref, m_ref, acc_in, chunks, acc_ref, va_ref):
    ones = jnp.ones((CHUNK, HEAD_SIZE), F32)
    for c, chunk in enumerate(chunks):
        flag = (ones * flag_ref[c].astype(F32)).astype(BF16)
        v = chunk[CHUNK:, :]
        va_ref[0, c, :, :HEAD_SIZE] = v * flag
        va_ref[0, c, :, HEAD_SIZE:] = flag
        va_ref[1, c, :, :HEAD_SIZE] = v
        va_ref[1, c, :, HEAD_SIZE:] = ones.astype(BF16)

    def tile(t, _):
        q = q_ref[t]
        m = m_ref[t]
        group = (t >= GROUP).astype(jnp.int32)
        total = acc_in[t]
        for c, chunk in enumerate(chunks):
            s = dot(q, keys_of(chunk))
            p = [
                jnp.exp2(s[:, i : i + 128] * SCALE - m).astype(BF16) for i in range(0, CHUNK, 128)
            ]
            total = total + dot(jnp.concatenate(p, axis=1), va_ref[group, c])
        acc_ref[t] = total
        return 0

    lax.fori_loop(0, TILES, tile, 0, unroll=5)


def block_kernel(first, flag_ref, q_ref, m_ref, acc_in, *rest):
    srcs, (acc_ref, va_ref) = rest[:-2], rest[-2:]
    chunks = [s.at[i] for s in srcs for i in range(first, s.shape[0])]
    accumulate(flag_ref, q_ref, m_ref, acc_in, chunks, acc_ref, va_ref)


def block(flags, q, m, acc, srcs, first, alias):
    n = sum(s.shape[0] - first for s in srcs)
    scores = TILES * CHUNK * n * CHUNK
    return pl.pallas_call(
        functools.partial(block_kernel, first),
        out_shape=jax.ShapeDtypeStruct(acc.shape, F32),
        in_specs=[SMEM] + [VMEM] * (3 + len(srcs)),
        out_specs=VMEM,
        scratch_shapes=[pltpu.VMEM((2, n, CHUNK, 2 * HEAD_SIZE), BF16)],
        input_output_aliases={3: 0} if alias else {},
        compiler_params=pltpu.CompilerParams(vmem_limit_bytes=40 << 20),
        cost_estimate=pl.CostEstimate(
            flops=scores * 768, bytes_accessed=8 << 20, transcendentals=scores
        ),
    )(flags, q, m, acc, *srcs)


def write_rows(out_ref, acc_ref):
    for t in range(GROUP):
        o = acc_ref[t, :, :HEAD_SIZE] / acc_ref[t, :, HEAD_SIZE:]
        out_ref[:CHUNK, t * 128 : (t + 1) * 128] = o.astype(BF16)
    for t in range(GROUP, TILES):
        o = (acc_ref[t, :, :HEAD_SIZE] / acc_ref[t, :, HEAD_SIZE:]).astype(BF16)
        for i in range(4):
            h = (t - GROUP) * 4 + i
            out_ref[CHUNK:, h * 128 : (h + 1) * 128] = o[i * BRANCH_ROWS : (i + 1) * BRANCH_ROWS]


def last_kernel(n_near, starts, flag_ref, all_ref, q_ref, m_ref, acc_in, *rest):
    near = rest[:n_near]
    acc0_ref = rest[n_near]
    out_ref, acc_ref, va_ref, run_ref, buf_ref, sem = rest[-6:]
    far = rest[n_near + 1 : -6]
    chunks = [s.at[i] for s in near for i in range(s.shape[0])]
    accumulate(flag_ref, q_ref, m_ref, acc_in, chunks, acc_ref, va_ref)
    peak = functools.reduce(jnp.maximum, [acc_ref[t, :, HEAD_SIZE:] for t in range(TILES)])
    lowest = functools.reduce(jnp.minimum, [acc_ref[t, :, HEAD_SIZE:] for t in range(TILES)])
    fine = jnp.min(jnp.where((peak < 1e30) & (lowest > 0), 1.0, 0.0)) > 0.5

    @pl.when(fine)
    def _():
        write_rows(out_ref, acc_ref)

    @pl.when(jnp.logical_not(fine))
    def _():
        copy = pltpu.make_async_copy(acc0_ref, acc_ref, sem)
        copy.start()
        copy.wait()
        run_ref[...] = m_ref[...]

        def online(allowed):
            v = jnp.concatenate(
                [buf_ref[CHUNK:, :], jnp.ones((CHUNK, HEAD_SIZE), BF16)], axis=1
            )

            def tile(t, _):
                s = dot(q_ref[t], keys_of(buf_ref))
                old = run_ref[t]
                new = jnp.maximum(old, row_peak([s]) * SCALE)
                run_ref[t] = new
                decay = jnp.exp2(old - new)
                p = jnp.exp2(s * SCALE - new[:, :1]).astype(BF16)
                acc_ref[t] = acc_ref[t] * jnp.concatenate([decay, decay], axis=1) + dot(p, v)
                return 0

            lax.fori_loop(jnp.where(allowed == 1, 0, GROUP), TILES, tile, 0)

        at = 0
        for ref, first in zip(far, starts):

            def one(i, _, ref=ref, first=first, at=at):
                copy = pltpu.make_async_copy(ref.at[i + first], buf_ref, sem)
                copy.start()
                copy.wait()
                online(all_ref[at + i])
                return 0

            lax.fori_loop(0, ref.shape[0] - first, one, 0)
            at += ref.shape[0] - first
        for ref in near:
            for i in range(ref.shape[0]):
                buf_ref[...] = ref[i]
                online(all_ref[at])
                at += 1
        write_rows(out_ref, acc_ref)


def last_block(flags, all_flags, q, m, acc, near, acc0, far, starts):
    n = sum(s.shape[0] for s in near)
    scores = TILES * CHUNK * n * CHUNK
    anywhere = pl.BlockSpec(memory_space=pl.ANY)
    return pl.pallas_call(
        functools.partial(last_kernel, len(near), starts),
        out_shape=jax.ShapeDtypeStruct((CHUNK + BRANCH_ROWS, GROUP * HEAD_SIZE), BF16),
        in_specs=[SMEM] * 2 + [VMEM] * (3 + len(near)) + [anywhere] * (1 + len(far)),
        out_specs=VMEM,
        scratch_shapes=[
            pltpu.VMEM(acc.shape, F32),
            pltpu.VMEM((2, n, CHUNK, 2 * HEAD_SIZE), BF16),
            pltpu.VMEM(m.shape, F32),
            pltpu.VMEM((2 * CHUNK, HEAD_SIZE), BF16),
            pltpu.SemaphoreType.DMA(()),
        ],
        compiler_params=pltpu.CompilerParams(vmem_limit_bytes=40 << 20),
        cost_estimate=pl.CostEstimate(
            flops=scores * 768, bytes_accessed=8 << 20, transcendentals=scores
        ),
    )(flags, all_flags, q, m, acc, *near, acc0, *far)


def copy_kernel(order_ref, w_ref, o_ref):
    del order_ref
    o_ref[...] = w_ref[...]


def take_columns(weight, order, width):
    depth = weight.shape[0]
    return pl.pallas_call(
        copy_kernel,
        out_shape=jax.ShapeDtypeStruct((depth, NX * width), BF16),
        grid_spec=pltpu.PrefetchScalarGridSpec(
            num_scalar_prefetch=1,
            grid=(NX,),
            in_specs=[pl.BlockSpec((depth, width), lambda i, o: (0, o[i]))],
            out_specs=pl.BlockSpec((depth, width), lambda i, o: (0, i)),
        ),
        compiler_params=pltpu.CompilerParams(vmem_limit_bytes=16 << 20),
        cost_estimate=pl.CostEstimate(
            flops=0, bytes_accessed=4 * depth * NX * width, transcendentals=0
        ),
    )(order, weight)


def project_kernel(n, order_ref, a_ref, b_ref, *rest):
    del order_ref
    half = a_ref.shape[0] // 2
    for i in range(n):
        w_ref, r_ref = rest[2 * i], rest[2 * i + 1]
        o = dot(a_ref[...], w_ref[...]) + dot(b_ref[...], r_ref[...])
        rest[2 * n + 2 * i][...] = o[:half].astype(BF16)
        rest[2 * n + 2 * i + 1][...] = o[half:].astype(BF16)


def project(order, attn, other, weight, received, steps, width):
    rows, depth = attn.shape
    whole = pl.BlockSpec((rows, depth), lambda i, o: (0, 0))
    specs, args = [whole, whole], [attn, other]
    for k in steps:
        specs.append(pl.BlockSpec((depth, width), lambda i, o, k=k: (0, o[k])))
        specs.append(pl.BlockSpec((depth, width), lambda i, o, k=k: (0, o[NX + k])))
        args += [weight, received]
    n = len(steps)
    half = pl.BlockSpec((rows // 2, width), lambda i, o: (0, 0))
    return pl.pallas_call(
        functools.partial(project_kernel, n),
        out_shape=[jax.ShapeDtypeStruct((rows // 2, width), BF16)] * (2 * n),
        grid_spec=pltpu.PrefetchScalarGridSpec(
            num_scalar_prefetch=1, grid=(1,), in_specs=specs, out_specs=[half] * (2 * n)
        ),
        compiler_params=pltpu.CompilerParams(vmem_limit_bytes=32 << 20),
        cost_estimate=pl.CostEstimate(
            flops=4 * n * rows * depth * width,
            bytes_accessed=4 * n * depth * width,
            transcendentals=0,
        ),
    )(order, *args)


def sum_kernel(a0, a1, b0, b1, c0, c1, doc_ref, branch_ref):
    low = a0[...].astype(F32) + b0[...].astype(F32) + c0[...].astype(F32)
    high = a1[...].astype(F32) + b1[...].astype(F32) + c1[...].astype(F32)
    rest = CHUNK - low.shape[0]
    doc_ref[: low.shape[0], :] = low.astype(BF16)
    doc_ref[low.shape[0] :, :] = high[:rest].astype(BF16)
    branch_ref[...] = high[rest:].astype(BF16)


def body(
    document_query,
    document_key,
    document_value,
    branch_token_query,
    branch_token_key,
    branch_token_value,
    branch_cached_key,
    branch_cached_value,
    suffix_length,
    out_weight,
):
    seq = lax.axis_index("seq")
    head = lax.axis_index("head")
    y, z = seq // NZ, seq % NZ
    x, core = head // 2, head % 2
    width = out_weight.shape[1] // (2 * NX)

    def send(a, pairs, axis="seq"):
        return lax.ppermute(a, axis, pairs)

    def together(*a):
        return lax.optimization_barrier(a)

    above = [((y + i) % NY < y).astype(jnp.int32) for i in range(1, NY)]

    def column_flags(shift):
        return [((z + shift) % NZ < z).astype(jnp.int32)] + above

    kv = pack(document_key, document_value)
    from_down = send(kv, y_shift(1))
    from_up = send(kv, y_shift(-1))
    from_far = send(from_down, y_shift(1))
    column = jnp.stack([kv, from_up, from_far, from_down])
    column, document_query = together(column, document_query)
    right = send(column, z_shift(1))
    left = send(column, z_shift(-1))

    branch_q = branch_token_query.reshape(BRANCH_ROWS, GROUP * HEAD_SIZE)
    pad = ((0, 128 - BRANCH_ROWS), (0, 0))
    fresh_k = jnp.pad(branch_token_key.reshape(BRANCH_ROWS, HEAD_SIZE), pad)
    fresh_v = jnp.pad(branch_token_value.reshape(BRANCH_ROWS, HEAD_SIZE), pad)
    cached_k = branch_cached_key.reshape(-1, HEAD_SIZE)
    cached_v = branch_cached_value.reshape(-1, HEAD_SIZE)
    q, acc0, m = pl.pallas_call(
        local_kernel,
        out_shape=[
            jax.ShapeDtypeStruct((TILES, CHUNK, HEAD_SIZE), BF16),
            jax.ShapeDtypeStruct((TILES, CHUNK, 2 * HEAD_SIZE), F32),
            jax.ShapeDtypeStruct((TILES, CHUNK, 128), F32),
        ],
        in_specs=[SMEM] + [VMEM] * 7,
        out_specs=[VMEM] * 3,
        scratch_shapes=[
            pltpu.VMEM((CHUNK, 2 * HEAD_SIZE), BF16),
            pltpu.VMEM((cached_v.shape[0], 2 * HEAD_SIZE), BF16),
            pltpu.VMEM((128, 2 * HEAD_SIZE), BF16),
        ],
        compiler_params=pltpu.CompilerParams(vmem_limit_bytes=40 << 20),
        cost_estimate=pl.CostEstimate(
            flops=4 << 30, bytes_accessed=8 << 20, transcendentals=2 << 20
        ),
    )(suffix_length, document_query, branch_q, kv, cached_k, cached_v, fresh_k, fresh_v)
    acc = block(jnp.stack(above), q, m, acc0, [column], first=1, alias=False)
    far, all_flags = [column], list(above)

    targets = (x + jnp.arange(NX, dtype=jnp.int32)) % NX
    order = jnp.concatenate([targets * 2 + core, targets]).astype(jnp.int32)
    others = (jnp.arange(NX, dtype=jnp.int32) * 2 + 1 - core).astype(jnp.int32)
    received = None
    for s in (1, 2, 3):
        right, left, acc = together(right, left, acc)
        if s < 3:
            next_right = send(right, z_shift(1))
            next_left = send(left, z_shift(-1))
        else:
            next_right = send(right[:2], z_shift(1))
            next_left = send(left[2:], z_shift(-1))
        if s == 1:
            right, out_weight = together(right, out_weight)
            received = send(take_columns(out_weight, others, width), core_swap(), "head")
        flags = column_flags(-s) + column_flags(s)
        acc = block(jnp.stack(flags), q, m, acc, [right, left], first=0, alias=True)
        far += [right, left]
        all_flags += flags
        right, left = next_right, next_left
    right, left, acc = together(right, left, acc)
    flags = column_flags(4)
    attn = last_block(
        jnp.stack(flags), jnp.stack(all_flags + flags), q, m, acc, [right, left], acc0, far, (1,) + (0,) * (len(far) - 1)
    )

    other = send(attn, core_swap(), "head")
    a0, a1 = project(order, attn, other, out_weight, received, (2,), width)
    via_up = send(a0, x_shift(1), "head")
    via_down = send(a1, x_shift(-1), "head")
    u0, u1, d0, d1 = project(order, attn, other, out_weight, received, (1, 3), width)
    high_up = send(u1, x_shift(1), "head")
    low_down = send(d0, x_shift(-1), "head")
    own0, own1 = project(order, attn, other, out_weight, received, (0,), width)

    def add(a, b):
        return (a.astype(F32) + b.astype(F32)).astype(BF16)

    low_up = send(add(u0, via_up), x_shift(1), "head")
    high_down = send(add(d1, via_down), x_shift(-1), "head")
    doc_out, branch_out = pl.pallas_call(
        sum_kernel,
        out_shape=[
            jax.ShapeDtypeStruct((CHUNK, width), BF16),
            jax.ShapeDtypeStruct((BRANCH_ROWS, width), BF16),
        ],
        in_specs=[VMEM] * 6,
        out_specs=[VMEM] * 2,
        compiler_params=pltpu.CompilerParams(vmem_limit_bytes=16 << 20),
    )(own0, own1, low_up, high_up, low_down, high_down)
    return doc_out, branch_out.reshape(-1, NEW_TOKENS, width)


def solution(mesh):
    placed = (
        P("seq", "head"),
        P("seq", "head"),
        P("seq", "head"),
        P("seq", None, "head"),
        P("seq", None, "head"),
        P("seq", None, "head"),
        P("seq", None, "head"),
        P("seq", None, "head"),
        P("seq"),
        P("head", None),
    )
    return jax.shard_map(
        body,
        mesh=mesh,
        in_specs=placed,
        out_specs=(P("seq", "head"), P("seq", None, "head")),
        check_vma=False,
    )
```

```python
import functools
import math

import jax
import jax.numpy as jnp
from jax import lax
from jax.experimental import pallas as pl
from jax.experimental.pallas import tpu as pltpu
from jax.sharding import PartitionSpec as P

HEAD_SIZE = 128
NEW_TOKENS = 4
GROUP = 8
CHUNK = 256
TILES = 10
BRANCH_ROWS = 64
NY, NZ, NX = 4, 8, 4
SCALE = HEAD_SIZE**-0.5 * math.log2(math.e)
NEG = -1e30
VMEM = pl.BlockSpec(memory_space=pltpu.VMEM)
SMEM = pl.BlockSpec(memory_space=pltpu.SMEM)
HBM = pl.BlockSpec(memory_space=pltpu.HBM)
F32 = jnp.float32
BF16 = jnp.bfloat16


def y_shift(k):
    return [(y * NZ + z, ((y + k) % NY) * NZ + z) for y in range(NY) for z in range(NZ)]


def z_shift(k):
    return [(y * NZ + z, y * NZ + (z + k) % NZ) for y in range(NY) for z in range(NZ)]


def x_shift(k):
    return [(x * 2 + c, ((x + k) % NX) * 2 + c) for x in range(NX) for c in range(2)]


def core_swap():
    return [(x * 2 + c, x * 2 + 1 - c) for x in range(NX) for c in range(2)]


def dot_nt(a, b):
    return lax.dot_general(a, b, (((1,), (1,)), ((), ())), preferred_element_type=F32)


def dot(a, b):
    return jnp.dot(a, b, preferred_element_type=F32)


def row_peak(parts):
    cols = [p[:, i : i + 128] for p in parts for i in range(0, p.shape[1], 128)]
    return jnp.max(functools.reduce(jnp.maximum, cols), axis=1, keepdims=True)


def keys_of(chunk):
    return jnp.concatenate([chunk[:HEAD_SIZE], chunk[HEAD_SIZE : 2 * HEAD_SIZE]], axis=1)


def pack_kernel(k_ref, v_ref, o_ref):
    kt = k_ref[...].T
    o_ref[:HEAD_SIZE, :] = kt[:, :HEAD_SIZE]
    o_ref[HEAD_SIZE:CHUNK, :] = kt[:, HEAD_SIZE:]
    o_ref[CHUNK:, :] = v_ref[...]


def pack(k, v):
    return pl.pallas_call(
        pack_kernel,
        out_shape=jax.ShapeDtypeStruct((2 * CHUNK, HEAD_SIZE), BF16),
        in_specs=[VMEM] * 2,
        out_specs=VMEM,
    )(k, v)


def local_kernel(
    len_ref, dq_hbm, bq_ref, kv_ref, ck_hbm, cv_hbm, fk_ref, fv_ref,
    q_ref, acc_ref, m_ref, va_ref, ca_ref, fa_ref, dq_ref, ck_ref, cv_ref, sems
):
    copies = [
        pltpu.make_async_copy(src, dst, sems.at[i])
        for i, (src, dst) in enumerate(((dq_hbm, dq_ref), (ck_hbm, ck_ref), (cv_hbm, cv_ref)))
    ]
    for copy in copies:
        copy.start()
    copies[0].wait()
    for h in range(GROUP):
        lanes = slice(h * HEAD_SIZE, (h + 1) * HEAD_SIZE)
        q_ref[h] = dq_ref[:, lanes]
        rows = slice((h % 4) * BRANCH_ROWS, (h % 4 + 1) * BRANCH_ROWS)
        q_ref[GROUP + h // 4, rows, :] = bq_ref[:, lanes]
    va_ref[:, :HEAD_SIZE] = kv_ref[CHUNK:, :]
    va_ref[:, HEAD_SIZE:] = jnp.ones((CHUNK, HEAD_SIZE), BF16)
    fa_ref[:, :HEAD_SIZE] = fv_ref[...]
    fa_ref[:, HEAD_SIZE:] = jnp.ones((128, HEAD_SIZE), BF16)
    ca_ref[:, HEAD_SIZE:] = jnp.ones((ca_ref.shape[0], HEAD_SIZE), BF16)
    kt = keys_of(kv_ref)
    row = lax.broadcasted_iota(jnp.int32, (CHUNK, CHUNK), 0)
    col = lax.broadcasted_iota(jnp.int32, (CHUNK, CHUNK), 1)
    causal = col <= row

    def doc(t, _):
        s = jnp.where(causal, dot(q_ref[t], kt), NEG)
        m = row_peak([s]) * SCALE
        p = jnp.exp2(s * SCALE - m).astype(BF16)
        m_ref[t] = jnp.broadcast_to(m, (CHUNK, 128))
        acc_ref[t] = dot(p, va_ref[...])
        return 0

    lax.fori_loop(0, GROUP, doc, 0, unroll=4)

    copies[1].wait()
    copies[2].wait()
    ca_ref[:, :HEAD_SIZE] = cv_ref[...]
    row_branch = (row % BRANCH_ROWS) // NEW_TOKENS
    n_cached = ca_ref.shape[0] // CHUNK
    frow = lax.broadcasted_iota(jnp.int32, (CHUNK, 128), 0)
    fcol = lax.broadcasted_iota(jnp.int32, (CHUNK, 128), 1)
    same = (frow % BRANCH_ROWS) // NEW_TOKENS == fcol // NEW_TOKENS
    fresh_keep = same & (fcol % NEW_TOKENS <= frow % NEW_TOKENS)
    low = col < 128
    for t in (8, 9):
        q = q_ref[t]
        parts = [dot(q, kt)]
        for c in range(n_cached):
            s = dot_nt(q, ck_ref[c * CHUNK : (c + 1) * CHUNK, :])
            length = jnp.where(low, len_ref[2 * c], len_ref[2 * c + 1])
            owner = jnp.where(low, 2 * c, 2 * c + 1)
            keep = (row_branch == owner) & (col % 128 < length)
            parts.append(jnp.where(keep, s, NEG))
        parts.append(jnp.where(fresh_keep, dot_nt(q, fk_ref[...]), NEG))
        m = row_peak(parts) * SCALE
        m_ref[t] = jnp.broadcast_to(m, (CHUNK, 128))
        p = [jnp.exp2(s * SCALE - m).astype(BF16) for s in parts]
        total = dot(p[0], va_ref[...])
        for c in range(n_cached):
            total += dot(p[1 + c], ca_ref[c * CHUNK : (c + 1) * CHUNK, :])
        total += dot(p[-1], fa_ref[...])
        acc_ref[t] = total


def accumulate(flag_ref, q_ref, m_ref, acc_in, chunks, acc_ref, va_ref):
    ones = jnp.ones((CHUNK, HEAD_SIZE), F32)
    for c, chunk in enumerate(chunks):
        flag = (ones * flag_ref[c].astype(F32)).astype(BF16)
        v = chunk[CHUNK:, :]
        va_ref[0, c, :, :HEAD_SIZE] = v * flag
        va_ref[0, c, :, HEAD_SIZE:] = flag
        va_ref[1, c, :, :HEAD_SIZE] = v
        va_ref[1, c, :, HEAD_SIZE:] = ones.astype(BF16)

    def tile(t, _):
        q = q_ref[t]
        m = m_ref[t]
        group = (t >= GROUP).astype(jnp.int32)
        total = acc_in[t]
        for c, chunk in enumerate(chunks):
            s = dot(q, keys_of(chunk))
            p = [
                jnp.exp2(s[:, i : i + 128] * SCALE - m).astype(BF16) for i in range(0, CHUNK, 128)
            ]
            total = total + dot(jnp.concatenate(p, axis=1), va_ref[group, c])
        acc_ref[t] = total
        return 0

    lax.fori_loop(0, TILES, tile, 0, unroll=5)


def block_kernel(first, flag_ref, q_ref, m_ref, acc_in, *rest):
    srcs, (acc_ref, va_ref) = rest[:-2], rest[-2:]
    chunks = [s.at[i] for s in srcs for i in range(first, s.shape[0])]
    accumulate(flag_ref, q_ref, m_ref, acc_in, chunks, acc_ref, va_ref)


def block(flags, q, m, acc, srcs, first, alias):
    n = sum(s.shape[0] - first for s in srcs)
    scores = TILES * CHUNK * n * CHUNK
    return pl.pallas_call(
        functools.partial(block_kernel, first),
        out_shape=jax.ShapeDtypeStruct(acc.shape, F32),
        in_specs=[SMEM] + [VMEM] * (3 + len(srcs)),
        out_specs=VMEM,
        scratch_shapes=[pltpu.VMEM((2, n, CHUNK, 2 * HEAD_SIZE), BF16)],
        input_output_aliases={3: 0} if alias else {},
        compiler_params=pltpu.CompilerParams(vmem_limit_bytes=16 << 20),
        cost_estimate=pl.CostEstimate(
            flops=scores * 768, bytes_accessed=8 << 20, transcendentals=scores
        ),
    )(flags, q, m, acc, *srcs)


def write_rows(out_ref, acc_ref):
    for t in range(GROUP):
        o = acc_ref[t, :, :HEAD_SIZE] / acc_ref[t, :, HEAD_SIZE:]
        out_ref[:CHUNK, t * 128 : (t + 1) * 128] = o.astype(BF16)
    for t in range(GROUP, TILES):
        o = (acc_ref[t, :, :HEAD_SIZE] / acc_ref[t, :, HEAD_SIZE:]).astype(BF16)
        for i in range(4):
            h = (t - GROUP) * 4 + i
            out_ref[CHUNK:, h * 128 : (h + 1) * 128] = o[i * BRANCH_ROWS : (i + 1) * BRANCH_ROWS]


def last_kernel(n_near, starts, flag_ref, all_ref, order_ref, q_ref, m_ref, acc_in, *rest):
    near = rest[:n_near]
    acc0_ref, weight_ref, received_ref = rest[n_near : n_near + 3]
    out_ref, mine_ref, theirs_ref, acc_ref, va_ref, run_ref, buf_ref, sem, sems = rest[-9:]
    far = rest[n_near + 3 : -9]
    width = mine_ref.shape[1] // NX
    fetches = [pltpu.make_async_copy(received_ref, theirs_ref, sems.at[NX])]
    for k in range(NX):
        first = pl.multiple_of(order_ref[k] * width, 128)
        fetches.append(
            pltpu.make_async_copy(
                weight_ref.at[:, pl.ds(first, width)],
                mine_ref.at[:, pl.ds(k * width, width)],
                sems.at[k],
            )
        )
    for fetch in fetches:
        fetch.start()
    chunks = [s.at[i] for s in near for i in range(s.shape[0])]
    accumulate(flag_ref, q_ref, m_ref, acc_in, chunks, acc_ref, va_ref)
    peak = functools.reduce(jnp.maximum, [acc_ref[t, :, HEAD_SIZE:] for t in range(TILES)])
    lowest = functools.reduce(jnp.minimum, [acc_ref[t, :, HEAD_SIZE:] for t in range(TILES)])
    fine = jnp.min(jnp.where((peak < 1e30) & (lowest > 0), 1.0, 0.0)) > 0.5

    @pl.when(fine)
    def _():
        write_rows(out_ref, acc_ref)

    @pl.when(jnp.logical_not(fine))
    def _():
        copy = pltpu.make_async_copy(acc0_ref, acc_ref, sem)
        copy.start()
        copy.wait()
        run_ref[...] = m_ref[...]

        def online(allowed):
            v = jnp.concatenate(
                [buf_ref[CHUNK:, :], jnp.ones((CHUNK, HEAD_SIZE), BF16)], axis=1
            )

            def tile(t, _):
                s = dot(q_ref[t], keys_of(buf_ref))
                old = run_ref[t]
                new = jnp.maximum(old, row_peak([s]) * SCALE)
                run_ref[t] = new
                decay = jnp.exp2(old - new)
                p = jnp.exp2(s * SCALE - new[:, :1]).astype(BF16)
                acc_ref[t] = acc_ref[t] * jnp.concatenate([decay, decay], axis=1) + dot(p, v)
                return 0

            lax.fori_loop(jnp.where(allowed == 1, 0, GROUP), TILES, tile, 0)

        at = 0
        for ref, first in zip(far, starts):

            def one(i, _, ref=ref, first=first, at=at):
                copy = pltpu.make_async_copy(ref.at[i + first], buf_ref, sem)
                copy.start()
                copy.wait()
                online(all_ref[at + i])
                return 0

            lax.fori_loop(0, ref.shape[0] - first, one, 0)
            at += ref.shape[0] - first
        for ref in near:
            for i in range(ref.shape[0]):
                buf_ref[...] = ref[i]
                online(all_ref[at])
                at += 1
        write_rows(out_ref, acc_ref)

    for fetch in fetches:
        fetch.wait()


def last_block(flags, all_flags, order, q, m, acc, near, acc0, weight, received, far, starts):
    n = sum(s.shape[0] for s in near)
    scores = TILES * CHUNK * n * CHUNK
    half = jax.ShapeDtypeStruct(received.shape, BF16)
    return pl.pallas_call(
        functools.partial(last_kernel, len(near), starts),
        out_shape=[jax.ShapeDtypeStruct((CHUNK + BRANCH_ROWS, GROUP * HEAD_SIZE), BF16), half, half],
        in_specs=[SMEM] * 3 + [VMEM] * (3 + len(near)) + [HBM] * (3 + len(far)),
        out_specs=[VMEM] * 3,
        scratch_shapes=[
            pltpu.VMEM(acc.shape, F32),
            pltpu.VMEM((2, n, CHUNK, 2 * HEAD_SIZE), BF16),
            pltpu.VMEM(m.shape, F32),
            pltpu.VMEM((2 * CHUNK, HEAD_SIZE), BF16),
            pltpu.SemaphoreType.DMA(()),
            pltpu.SemaphoreType.DMA((NX + 1,)),
        ],
        compiler_params=pltpu.CompilerParams(vmem_limit_bytes=32 << 20),
        cost_estimate=pl.CostEstimate(
            flops=scores * 768, bytes_accessed=8 << 20, transcendentals=scores
        ),
    )(flags, all_flags, order, q, m, acc, *near, acc0, weight, received, *far)


def columns_kernel(width, order_ref, w_ref, o_ref, sems):
    copies = []
    for k in range(NX):
        first = pl.multiple_of(order_ref[k] * width, 128)
        copies.append(
            pltpu.make_async_copy(
                w_ref.at[:, pl.ds(first, width)], o_ref.at[:, pl.ds(k * width, width)], sems.at[k]
            )
        )
    for copy in copies:
        copy.start()
    for copy in copies:
        copy.wait()


def take_columns(weight, order, width):
    depth = weight.shape[0]
    return pl.pallas_call(
        functools.partial(columns_kernel, width),
        out_shape=jax.ShapeDtypeStruct((depth, NX * width), BF16),
        in_specs=[SMEM, HBM],
        out_specs=HBM,
        scratch_shapes=[pltpu.SemaphoreType.DMA((NX,))],
        cost_estimate=pl.CostEstimate(
            flops=0, bytes_accessed=4 * depth * NX * width, transcendentals=0
        ),
    )(order, weight)


def halves_kernel(a_ref, b_ref, low_ref, high_ref, sems):
    n = low_ref.shape[0]
    copies = [
        pltpu.make_async_copy(a_ref.at[pl.ds(0, n)], low_ref, sems.at[0]),
        pltpu.make_async_copy(b_ref.at[pl.ds(n, n)], high_ref, sems.at[1]),
    ]
    for copy in copies:
        copy.start()
    for copy in copies:
        copy.wait()


def halves(a, b):
    half = jax.ShapeDtypeStruct((a.shape[0] // 2,) + a.shape[1:], a.dtype)
    return pl.pallas_call(
        halves_kernel,
        out_shape=[half, half],
        in_specs=[HBM] * 2,
        out_specs=[HBM] * 2,
        scratch_shapes=[pltpu.SemaphoreType.DMA((2,))],
    )(a, b)


def own_kernel(a_ref, w_ref, o_ref):
    width = o_ref.shape[2]

    def step(k, _):
        first = pl.multiple_of(k * width, 128)
        o_ref[k] = dot(a_ref[...], w_ref[:, pl.ds(first, width)])
        return 0

    lax.fori_loop(0, NX, step, 0)


def own_products(attn, mine, width):
    rows, depth = attn.shape
    return pl.pallas_call(
        own_kernel,
        out_shape=jax.ShapeDtypeStruct((NX, rows, width), F32),
        in_specs=[VMEM] * 2,
        out_specs=VMEM,
        compiler_params=pltpu.CompilerParams(vmem_limit_bytes=16 << 20),
        cost_estimate=pl.CostEstimate(
            flops=2 * NX * rows * depth * width, bytes_accessed=0, transcendentals=0
        ),
    )(attn, mine)


def project_kernel(steps, own_ref, b_ref, w_ref, *out_refs):
    half, width = out_refs[0].shape
    for i, k in enumerate(steps):
        o = own_ref[k] + dot(b_ref[...], w_ref[:, k * width : (k + 1) * width])
        out_refs[2 * i][...] = o[:half].astype(BF16)
        out_refs[2 * i + 1][...] = o[half:].astype(BF16)


def project(own, other, theirs, steps):
    _, rows, width = own.shape
    half = jax.ShapeDtypeStruct((rows // 2, width), BF16)
    n = len(steps)
    return pl.pallas_call(
        functools.partial(project_kernel, steps),
        out_shape=[half] * (2 * n),
        in_specs=[VMEM] * 3,
        out_specs=[VMEM] * (2 * n),
        compiler_params=pltpu.CompilerParams(vmem_limit_bytes=20 << 20),
        cost_estimate=pl.CostEstimate(
            flops=2 * n * rows * other.shape[1] * width, bytes_accessed=0, transcendentals=0
        ),
    )(own, other, theirs)


def sum_kernel(o_ref, b0, b1, c0, c1, doc_ref, branch_ref):
    half = b0.shape[0]
    low = o_ref[:half] + b0[...].astype(F32) + c0[...].astype(F32)
    high = o_ref[half:] + b1[...].astype(F32) + c1[...].astype(F32)
    rest = CHUNK - half
    doc_ref[:half, :] = low.astype(BF16)
    doc_ref[half:, :] = high[:rest].astype(BF16)
    branch_ref[...] = high[rest:].astype(BF16)


def home_kernel(own_ref, b_ref, w_ref, o_ref):
    o_ref[...] = own_ref[0] + dot(b_ref[...], w_ref[:, : o_ref.shape[1]])


def body(
    document_query,
    document_key,
    document_value,
    branch_token_query,
    branch_token_key,
    branch_token_value,
    branch_cached_key,
    branch_cached_value,
    suffix_length,
    out_weight,
):
    seq = lax.axis_index("seq")
    head = lax.axis_index("head")
    y, z = seq // NZ, seq % NZ
    x, core = head // 2, head % 2
    width = out_weight.shape[1] // (2 * NX)

    def send(a, pairs, axis="seq"):
        return lax.ppermute(a, axis, pairs)

    def together(*a):
        return lax.optimization_barrier(a)

    above = [((y + i) % NY < y).astype(jnp.int32) for i in range(1, NY)]

    def column_flags(shift):
        return [((z + shift) % NZ < z).astype(jnp.int32)] + above

    targets = (x + jnp.arange(NX, dtype=jnp.int32)) % NX
    mine_order = (targets * 2 + core).astype(jnp.int32)
    other_order = (targets * 2 + 1 - core).astype(jnp.int32)

    kv = pack(document_key, document_value)
    from_down = send(kv, y_shift(1))
    from_up = send(kv, y_shift(-1))
    kv, weight = together(kv, out_weight)
    for_other = take_columns(weight, other_order, width)
    from_down, for_other = together(from_down, for_other)
    from_far = send(from_down, y_shift(1))
    column = jnp.stack([kv, from_up, from_far, from_down])
    column, kv = together(column, kv)
    right = send(column, z_shift(1))
    left = send(column, z_shift(-1))

    branch_q = branch_token_query.reshape(BRANCH_ROWS, GROUP * HEAD_SIZE)
    pad = ((0, 128 - BRANCH_ROWS), (0, 0))
    fresh_k = jnp.pad(branch_token_key.reshape(BRANCH_ROWS, HEAD_SIZE), pad)
    fresh_v = jnp.pad(branch_token_value.reshape(BRANCH_ROWS, HEAD_SIZE), pad)
    cached_k = branch_cached_key.reshape(-1, HEAD_SIZE)
    cached_v = branch_cached_value.reshape(-1, HEAD_SIZE)
    q, acc0, m = pl.pallas_call(
        local_kernel,
        out_shape=[
            jax.ShapeDtypeStruct((TILES, CHUNK, HEAD_SIZE), BF16),
            jax.ShapeDtypeStruct((TILES, CHUNK, 2 * HEAD_SIZE), F32),
            jax.ShapeDtypeStruct((TILES, CHUNK, 128), F32),
        ],
        in_specs=[SMEM, HBM, VMEM, VMEM, HBM, HBM, VMEM, VMEM],
        out_specs=[VMEM] * 3,
        scratch_shapes=[
            pltpu.VMEM((CHUNK, 2 * HEAD_SIZE), BF16),
            pltpu.VMEM((cached_v.shape[0], 2 * HEAD_SIZE), BF16),
            pltpu.VMEM((128, 2 * HEAD_SIZE), BF16),
            pltpu.VMEM(document_query.shape, BF16),
            pltpu.VMEM(cached_k.shape, BF16),
            pltpu.VMEM(cached_v.shape, BF16),
            pltpu.SemaphoreType.DMA((3,)),
        ],
        compiler_params=pltpu.CompilerParams(vmem_limit_bytes=24 << 20),
        cost_estimate=pl.CostEstimate(
            flops=4 << 30, bytes_accessed=8 << 20, transcendentals=2 << 20
        ),
    )(suffix_length, document_query, branch_q, kv, cached_k, cached_v, fresh_k, fresh_v)
    acc = block(jnp.stack(above), q, m, acc0, [column], first=1, alias=False)
    far, all_flags = [column], list(above)

    column, for_other = together(column, for_other)
    received = send(for_other, core_swap(), "head")
    for s in (1, 2, 3):
        right, left, acc = together(right, left, acc)
        if s < 3:
            next_right = send(right, z_shift(1))
            next_left = send(left, z_shift(-1))
        else:
            low, high = halves(right, left)
            next_right = send(low, z_shift(1))
            next_left = send(high, z_shift(-1))
        flags = column_flags(-s) + column_flags(s)
        acc = block(jnp.stack(flags), q, m, acc, [right, left], first=0, alias=True)
        far += [right, left]
        all_flags += flags
        right, left = next_right, next_left
    right, left, acc = together(right, left, acc)
    flags = column_flags(4)
    attn, mine, theirs = last_block(
        jnp.stack(flags),
        jnp.stack(all_flags + flags),
        mine_order,
        q,
        m,
        acc,
        [right, left],
        acc0,
        out_weight,
        received,
        far,
        (1,) + (0,) * (len(far) - 1),
    )

    other = send(attn, core_swap(), "head")
    own = own_products(attn, mine, width)
    other, own = together(other, own)
    a0, a1 = project(own, other, theirs, (2,))
    via_up = send(a0, x_shift(1), "head")
    via_down = send(a1, x_shift(-1), "head")
    u0, u1, d0, d1 = project(own, other, theirs, (1, 3))
    high_up = send(u1, x_shift(1), "head")
    low_down = send(d0, x_shift(-1), "head")

    def add(a, b):
        return (a.astype(F32) + b.astype(F32)).astype(BF16)

    low_up = send(add(u0, via_up), x_shift(1), "head")
    high_down = send(add(d1, via_down), x_shift(-1), "head")
    home = pl.pallas_call(
        home_kernel,
        out_shape=jax.ShapeDtypeStruct(own.shape[1:], F32),
        in_specs=[VMEM] * 3,
        out_specs=VMEM,
        compiler_params=pltpu.CompilerParams(vmem_limit_bytes=20 << 20),
        cost_estimate=pl.CostEstimate(flops=1 << 29, bytes_accessed=0, transcendentals=0),
    )(own, other, theirs)
    doc_out, branch_out = pl.pallas_call(
        sum_kernel,
        out_shape=[
            jax.ShapeDtypeStruct((CHUNK, width), BF16),
            jax.ShapeDtypeStruct((BRANCH_ROWS, width), BF16),
        ],
        in_specs=[VMEM] * 5,
        out_specs=[VMEM] * 2,
        compiler_params=pltpu.CompilerParams(vmem_limit_bytes=16 << 20),
    )(home, low_up, high_up, low_down, high_down)
    return doc_out, branch_out.reshape(-1, NEW_TOKENS, width)


def solution(mesh):
    placed = (
        P("seq", "head"),
        P("seq", "head"),
        P("seq", "head"),
        P("seq", None, "head"),
        P("seq", None, "head"),
        P("seq", None, "head"),
        P("seq", None, "head"),
        P("seq", None, "head"),
        P("seq"),
        P("head", None),
    )
    return jax.shard_map(
        body,
        mesh=mesh,
        in_specs=placed,
        out_specs=(P("seq", "head"), P("seq", None, "head")),
        check_vma=False,
    )
```

```python
import functools
import math

import jax
import jax.numpy as jnp
from jax import lax
from jax.experimental import pallas as pl
from jax.experimental.pallas import tpu as pltpu
from jax.sharding import PartitionSpec as P

HEAD_SIZE = 128
NEW_TOKENS = 4
GROUP = 8
CHUNK = 256
TILES = 10
BRANCH_ROWS = 64
NY, NZ, NX = 4, 8, 4
SCALE = HEAD_SIZE**-0.5 * math.log2(math.e)
NEG = -1e30
VMEM = pl.BlockSpec(memory_space=pltpu.VMEM)
SMEM = pl.BlockSpec(memory_space=pltpu.SMEM)
HBM = pl.BlockSpec(memory_space=pltpu.HBM)
F32 = jnp.float32
BF16 = jnp.bfloat16


def y_shift(k):
    return [(y * NZ + z, ((y + k) % NY) * NZ + z) for y in range(NY) for z in range(NZ)]


def z_shift(k):
    return [(y * NZ + z, y * NZ + (z + k) % NZ) for y in range(NY) for z in range(NZ)]


def x_shift(k):
    return [(x * 2 + c, ((x + k) % NX) * 2 + c) for x in range(NX) for c in range(2)]


def core_swap():
    return [(x * 2 + c, x * 2 + 1 - c) for x in range(NX) for c in range(2)]


def in_hbm(a):
    return pltpu.with_memory_space_constraint(a, pltpu.HBM)


def in_vmem(a):
    return pltpu.with_memory_space_constraint(a, pltpu.VMEM)


def dot_nt(a, b):
    return lax.dot_general(a, b, (((1,), (1,)), ((), ())), preferred_element_type=F32)


def dot(a, b):
    return jnp.dot(a, b, preferred_element_type=F32)


def row_peak(parts):
    cols = [p[:, i : i + 128] for p in parts for i in range(0, p.shape[1], 128)]
    return jnp.max(functools.reduce(jnp.maximum, cols), axis=1, keepdims=True)


def keys_of(chunk):
    return jnp.concatenate([chunk[:HEAD_SIZE], chunk[HEAD_SIZE : 2 * HEAD_SIZE]], axis=1)


def pack_kernel(k_ref, v_ref, o_ref):
    kt = k_ref[...].T
    o_ref[:HEAD_SIZE, :] = kt[:, :HEAD_SIZE]
    o_ref[HEAD_SIZE:CHUNK, :] = kt[:, HEAD_SIZE:]
    o_ref[CHUNK:, :] = v_ref[...]


def pack(k, v):
    return pl.pallas_call(
        pack_kernel,
        out_shape=jax.ShapeDtypeStruct((2 * CHUNK, HEAD_SIZE), BF16),
        in_specs=[VMEM] * 2,
        out_specs=VMEM,
    )(k, v)


def local_kernel(
    len_ref, dq_hbm, bq_ref, kv_ref, ck_hbm, cv_hbm, fk_ref, fv_ref,
    q_ref, acc_ref, m_ref, va_ref, ca_ref, fa_ref, dq_ref, ck_ref, cv_ref, sems
):
    copies = [
        pltpu.make_async_copy(src, dst, sems.at[i])
        for i, (src, dst) in enumerate(((dq_hbm, dq_ref), (ck_hbm, ck_ref), (cv_hbm, cv_ref)))
    ]
    for copy in copies:
        copy.start()
    copies[0].wait()
    for h in range(GROUP):
        lanes = slice(h * HEAD_SIZE, (h + 1) * HEAD_SIZE)
        q_ref[h] = dq_ref[:, lanes]
        rows = slice((h % 4) * BRANCH_ROWS, (h % 4 + 1) * BRANCH_ROWS)
        q_ref[GROUP + h // 4, rows, :] = bq_ref[:, lanes]
    va_ref[:, :HEAD_SIZE] = kv_ref[CHUNK:, :]
    va_ref[:, HEAD_SIZE:] = jnp.ones((CHUNK, HEAD_SIZE), BF16)
    fa_ref[:, :HEAD_SIZE] = fv_ref[...]
    fa_ref[:, HEAD_SIZE:] = jnp.ones((128, HEAD_SIZE), BF16)
    ca_ref[:, HEAD_SIZE:] = jnp.ones((ca_ref.shape[0], HEAD_SIZE), BF16)
    kt = keys_of(kv_ref)
    row = lax.broadcasted_iota(jnp.int32, (CHUNK, CHUNK), 0)
    col = lax.broadcasted_iota(jnp.int32, (CHUNK, CHUNK), 1)
    causal = col <= row

    def doc(t, _):
        s = jnp.where(causal, dot(q_ref[t], kt), NEG)
        m = row_peak([s]) * SCALE
        p = jnp.exp2(s * SCALE - m).astype(BF16)
        m_ref[t] = jnp.broadcast_to(m, (CHUNK, 128))
        acc_ref[t] = dot(p, va_ref[...])
        return 0

    lax.fori_loop(0, GROUP, doc, 0, unroll=4)

    copies[1].wait()
    copies[2].wait()
    ca_ref[:, :HEAD_SIZE] = cv_ref[...]
    row_branch = (row % BRANCH_ROWS) // NEW_TOKENS
    n_cached = ca_ref.shape[0] // CHUNK
    frow = lax.broadcasted_iota(jnp.int32, (CHUNK, 128), 0)
    fcol = lax.broadcasted_iota(jnp.int32, (CHUNK, 128), 1)
    same = (frow % BRANCH_ROWS) // NEW_TOKENS == fcol // NEW_TOKENS
    fresh_keep = same & (fcol % NEW_TOKENS <= frow % NEW_TOKENS)
    low = col < 128
    for t in (8, 9):
        q = q_ref[t]
        parts = [dot(q, kt)]
        for c in range(n_cached):
            s = dot_nt(q, ck_ref[c * CHUNK : (c + 1) * CHUNK, :])
            length = jnp.where(low, len_ref[2 * c], len_ref[2 * c + 1])
            owner = jnp.where(low, 2 * c, 2 * c + 1)
            keep = (row_branch == owner) & (col % 128 < length)
            parts.append(jnp.where(keep, s, NEG))
        parts.append(jnp.where(fresh_keep, dot_nt(q, fk_ref[...]), NEG))
        m = row_peak(parts) * SCALE
        m_ref[t] = jnp.broadcast_to(m, (CHUNK, 128))
        p = [jnp.exp2(s * SCALE - m).astype(BF16) for s in parts]
        total = dot(p[0], va_ref[...])
        for c in range(n_cached):
            total += dot(p[1 + c], ca_ref[c * CHUNK : (c + 1) * CHUNK, :])
        total += dot(p[-1], fa_ref[...])
        acc_ref[t] = total


def accumulate(flag_ref, q_ref, m_ref, acc_in, chunks, acc_ref, va_ref):
    ones = jnp.ones((CHUNK, HEAD_SIZE), F32)
    for c, chunk in enumerate(chunks):
        flag = (ones * flag_ref[c].astype(F32)).astype(BF16)
        v = chunk[CHUNK:, :]
        va_ref[0, c, :, :HEAD_SIZE] = v * flag
        va_ref[0, c, :, HEAD_SIZE:] = flag
        va_ref[1, c, :, :HEAD_SIZE] = v
        va_ref[1, c, :, HEAD_SIZE:] = ones.astype(BF16)

    def tile(t, _):
        q = q_ref[t]
        m = m_ref[t]
        group = (t >= GROUP).astype(jnp.int32)
        total = acc_in[t]
        for c, chunk in enumerate(chunks):
            s = dot(q, keys_of(chunk))
            p = [
                jnp.exp2(s[:, i : i + 128] * SCALE - m).astype(BF16) for i in range(0, CHUNK, 128)
            ]
            total = total + dot(jnp.concatenate(p, axis=1), va_ref[group, c])
        acc_ref[t] = total
        return 0

    lax.fori_loop(0, TILES, tile, 0, unroll=5)


def block_kernel(first, flag_ref, q_ref, m_ref, acc_in, *rest):
    srcs, (acc_ref, va_ref) = rest[:-2], rest[-2:]
    chunks = [s.at[i] for s in srcs for i in range(first, s.shape[0])]
    accumulate(flag_ref, q_ref, m_ref, acc_in, chunks, acc_ref, va_ref)


def block(flags, q, m, acc, srcs, first, alias):
    n = sum(s.shape[0] - first for s in srcs)
    scores = TILES * CHUNK * n * CHUNK
    return pl.pallas_call(
        functools.partial(block_kernel, first),
        out_shape=pltpu.VMEM(acc.shape, F32),
        in_specs=[SMEM] + [VMEM] * (3 + len(srcs)),
        out_specs=VMEM,
        scratch_shapes=[pltpu.VMEM((2, n, CHUNK, 2 * HEAD_SIZE), BF16)],
        input_output_aliases={3: 0} if alias else {},
        compiler_params=pltpu.CompilerParams(vmem_limit_bytes=16 << 20),
        cost_estimate=pl.CostEstimate(
            flops=scores * 768, bytes_accessed=8 << 20, transcendentals=scores
        ),
    )(flags, in_vmem(q), in_vmem(m), in_vmem(acc), *srcs)


def write_rows(out_ref, acc_ref):
    for t in range(GROUP):
        o = acc_ref[t, :, :HEAD_SIZE] / acc_ref[t, :, HEAD_SIZE:]
        out_ref[:CHUNK, t * 128 : (t + 1) * 128] = o.astype(BF16)
    for t in range(GROUP, TILES):
        o = (acc_ref[t, :, :HEAD_SIZE] / acc_ref[t, :, HEAD_SIZE:]).astype(BF16)
        for i in range(4):
            h = (t - GROUP) * 4 + i
            out_ref[CHUNK:, h * 128 : (h + 1) * 128] = o[i * BRANCH_ROWS : (i + 1) * BRANCH_ROWS]


def last_kernel(n_near, starts, flag_ref, all_ref, order_ref, q_ref, m_ref, acc_in, *rest):
    near = rest[:n_near]
    acc0_ref, weight_ref = rest[n_near : n_near + 2]
    out_ref, mine_ref, acc_ref, va_ref, run_ref, buf_ref, sem, sems = rest[-8:]
    far = rest[n_near + 2 : -8]
    width = mine_ref.shape[1] // NX
    fetches = []
    for k in range(NX):
        first = pl.multiple_of(order_ref[k] * width, 128)
        fetches.append(
            pltpu.make_async_copy(
                weight_ref.at[:, pl.ds(first, width)],
                mine_ref.at[:, pl.ds(k * width, width)],
                sems.at[k],
            )
        )
    for fetch in fetches:
        fetch.start()
    chunks = [s.at[i] for s in near for i in range(s.shape[0])]
    accumulate(flag_ref, q_ref, m_ref, acc_in, chunks, acc_ref, va_ref)
    peak = functools.reduce(jnp.maximum, [acc_ref[t, :, HEAD_SIZE:] for t in range(TILES)])
    lowest = functools.reduce(jnp.minimum, [acc_ref[t, :, HEAD_SIZE:] for t in range(TILES)])
    fine = jnp.min(jnp.where((peak < 1e30) & (lowest > 0), 1.0, 0.0)) > 0.5

    @pl.when(fine)
    def _():
        write_rows(out_ref, acc_ref)

    @pl.when(jnp.logical_not(fine))
    def _():
        acc_ref[...] = acc0_ref[...]
        run_ref[...] = m_ref[...]

        def online(allowed):
            v = jnp.concatenate(
                [buf_ref[CHUNK:, :], jnp.ones((CHUNK, HEAD_SIZE), BF16)], axis=1
            )

            def tile(t, _):
                s = dot(q_ref[t], keys_of(buf_ref))
                old = run_ref[t]
                new = jnp.maximum(old, row_peak([s]) * SCALE)
                run_ref[t] = new
                decay = jnp.exp2(old - new)
                p = jnp.exp2(s * SCALE - new[:, :1]).astype(BF16)
                acc_ref[t] = acc_ref[t] * jnp.concatenate([decay, decay], axis=1) + dot(p, v)
                return 0

            lax.fori_loop(jnp.where(allowed == 1, 0, GROUP), TILES, tile, 0)

        at = 0
        for ref, first in zip(far, starts):

            def one(i, _, ref=ref, first=first, at=at):
                copy = pltpu.make_async_copy(ref.at[i + first], buf_ref, sem)
                copy.start()
                copy.wait()
                online(all_ref[at + i])
                return 0

            lax.fori_loop(0, ref.shape[0] - first, one, 0)
            at += ref.shape[0] - first
        for ref in near:
            for i in range(ref.shape[0]):
                buf_ref[...] = ref[i]
                online(all_ref[at])
                at += 1
        write_rows(out_ref, acc_ref)

    for fetch in fetches:
        fetch.wait()


def last_block(flags, all_flags, order, q, m, acc, near, acc0, weight, far, starts):
    n = sum(s.shape[0] for s in near)
    scores = TILES * CHUNK * n * CHUNK
    half = pltpu.VMEM((weight.shape[0], weight.shape[1] // 2), BF16)
    return pl.pallas_call(
        functools.partial(last_kernel, len(near), starts),
        out_shape=[jax.ShapeDtypeStruct((CHUNK + BRANCH_ROWS, GROUP * HEAD_SIZE), BF16), half],
        in_specs=[SMEM] * 3 + [VMEM] * (4 + len(near)) + [HBM] * (1 + len(far)),
        out_specs=[VMEM] * 2,
        scratch_shapes=[
            pltpu.VMEM(acc.shape, F32),
            pltpu.VMEM((2, n, CHUNK, 2 * HEAD_SIZE), BF16),
            pltpu.VMEM(m.shape, F32),
            pltpu.VMEM((2 * CHUNK, HEAD_SIZE), BF16),
            pltpu.SemaphoreType.DMA(()),
            pltpu.SemaphoreType.DMA((NX,)),
        ],
        compiler_params=pltpu.CompilerParams(vmem_limit_bytes=24 << 20),
        cost_estimate=pl.CostEstimate(
            flops=scores * 768, bytes_accessed=8 << 20, transcendentals=scores
        ),
    )(
        flags,
        all_flags,
        order,
        in_vmem(q),
        in_vmem(m),
        in_vmem(acc),
        *near,
        in_vmem(acc0),
        in_hbm(weight),
        *[in_hbm(a) for a in far],
    )


def copy_kernel(order_ref, w_ref, o_ref):
    del order_ref
    o_ref[...] = w_ref[...]


def take_columns(weight, order, width):
    depth = weight.shape[0]
    return pl.pallas_call(
        copy_kernel,
        out_shape=jax.ShapeDtypeStruct((depth, NX * width), BF16),
        grid_spec=pltpu.PrefetchScalarGridSpec(
            num_scalar_prefetch=1,
            grid=(NX,),
            in_specs=[pl.BlockSpec((depth, width), lambda i, o: (0, o[i]))],
            out_specs=pl.BlockSpec((depth, width), lambda i, o: (0, i)),
        ),
        compiler_params=pltpu.CompilerParams(vmem_limit_bytes=16 << 20),
        cost_estimate=pl.CostEstimate(
            flops=0, bytes_accessed=4 * depth * NX * width, transcendentals=0
        ),
    )(order, in_hbm(weight))


def own_kernel(a_ref, w_ref, o_ref):
    width = o_ref.shape[2]

    def step(k, _):
        first = pl.multiple_of(k * width, 128)
        o_ref[k] = dot(a_ref[...], w_ref[:, pl.ds(first, width)])
        return 0

    lax.fori_loop(0, NX, step, 0)


def own_products(attn, mine, width):
    rows, depth = attn.shape
    return pl.pallas_call(
        own_kernel,
        out_shape=jax.ShapeDtypeStruct((NX, rows, width), F32),
        in_specs=[VMEM] * 2,
        out_specs=VMEM,
        compiler_params=pltpu.CompilerParams(vmem_limit_bytes=16 << 20),
        cost_estimate=pl.CostEstimate(
            flops=2 * NX * rows * depth * width, bytes_accessed=0, transcendentals=0
        ),
    )(attn, in_vmem(mine))


def project_kernel(steps, own_ref, b_ref, w_ref, *out_refs):
    half, width = out_refs[0].shape
    for i, k in enumerate(steps):
        o = own_ref[k] + dot(b_ref[...], w_ref[:, k * width : (k + 1) * width])
        out_refs[2 * i][...] = o[:half].astype(BF16)
        out_refs[2 * i + 1][...] = o[half:].astype(BF16)


def project(own, other, theirs, steps):
    _, rows, width = own.shape
    half = jax.ShapeDtypeStruct((rows // 2, width), BF16)
    n = len(steps)
    return pl.pallas_call(
        functools.partial(project_kernel, steps),
        out_shape=[half] * (2 * n),
        in_specs=[VMEM] * 3,
        out_specs=[VMEM] * (2 * n),
        compiler_params=pltpu.CompilerParams(vmem_limit_bytes=20 << 20),
        cost_estimate=pl.CostEstimate(
            flops=2 * n * rows * other.shape[1] * width, bytes_accessed=0, transcendentals=0
        ),
    )(own, other, theirs)


def sum_kernel(o_ref, b0, b1, c0, c1, doc_ref, branch_ref):
    half = b0.shape[0]
    low = o_ref[:half] + b0[...].astype(F32) + c0[...].astype(F32)
    high = o_ref[half:] + b1[...].astype(F32) + c1[...].astype(F32)
    rest = CHUNK - half
    doc_ref[:half, :] = low.astype(BF16)
    doc_ref[half:, :] = high[:rest].astype(BF16)
    branch_ref[...] = high[rest:].astype(BF16)


def home_kernel(own_ref, b_ref, w_ref, o_ref):
    o_ref[...] = own_ref[0] + dot(b_ref[...], w_ref[:, : o_ref.shape[1]])


def body(
    document_query,
    document_key,
    document_value,
    branch_token_query,
    branch_token_key,
    branch_token_value,
    branch_cached_key,
    branch_cached_value,
    suffix_length,
    out_weight,
):
    seq = lax.axis_index("seq")
    head = lax.axis_index("head")
    y, z = seq // NZ, seq % NZ
    x, core = head // 2, head % 2
    width = out_weight.shape[1] // (2 * NX)

    def send(a, pairs, axis="seq"):
        return lax.ppermute(a, axis, pairs)

    def together(*a):
        return lax.optimization_barrier(a)

    above = [((y + i) % NY < y).astype(jnp.int32) for i in range(1, NY)]

    def column_flags(shift):
        return [((z + shift) % NZ < z).astype(jnp.int32)] + above

    targets = (x + jnp.arange(NX, dtype=jnp.int32)) % NX
    mine_order = (targets * 2 + core).astype(jnp.int32)
    other_order = (targets * 2 + 1 - core).astype(jnp.int32)

    kv = pack(document_key, document_value)
    from_down = send(kv, y_shift(1))
    from_up = send(kv, y_shift(-1))
    kv, weight = together(kv, out_weight)
    for_other = take_columns(weight, other_order, width)
    from_down, for_other = together(from_down, for_other)
    from_far = send(from_down, y_shift(1))
    column = jnp.stack([kv, from_up, from_far, from_down])
    column, kv = together(column, kv)
    right = send(column, z_shift(1))
    left = send(column, z_shift(-1))

    branch_q = branch_token_query.reshape(BRANCH_ROWS, GROUP * HEAD_SIZE)
    pad = ((0, 128 - BRANCH_ROWS), (0, 0))
    fresh_k = jnp.pad(branch_token_key.reshape(BRANCH_ROWS, HEAD_SIZE), pad)
    fresh_v = jnp.pad(branch_token_value.reshape(BRANCH_ROWS, HEAD_SIZE), pad)
    cached_k = branch_cached_key.reshape(-1, HEAD_SIZE)
    cached_v = branch_cached_value.reshape(-1, HEAD_SIZE)
    q, acc0, m = pl.pallas_call(
        local_kernel,
        out_shape=[
            pltpu.VMEM((TILES, CHUNK, HEAD_SIZE), BF16),
            pltpu.VMEM((TILES, CHUNK, 2 * HEAD_SIZE), F32),
            pltpu.VMEM((TILES, CHUNK, 128), F32),
        ],
        in_specs=[SMEM, HBM, VMEM, VMEM, HBM, HBM, VMEM, VMEM],
        out_specs=[VMEM] * 3,
        scratch_shapes=[
            pltpu.VMEM((CHUNK, 2 * HEAD_SIZE), BF16),
            pltpu.VMEM((cached_v.shape[0], 2 * HEAD_SIZE), BF16),
            pltpu.VMEM((128, 2 * HEAD_SIZE), BF16),
            pltpu.VMEM(document_query.shape, BF16),
            pltpu.VMEM(cached_k.shape, BF16),
            pltpu.VMEM(cached_v.shape, BF16),
            pltpu.SemaphoreType.DMA((3,)),
        ],
        compiler_params=pltpu.CompilerParams(vmem_limit_bytes=24 << 20),
        cost_estimate=pl.CostEstimate(
            flops=4 << 30, bytes_accessed=8 << 20, transcendentals=2 << 20
        ),
    )(
        suffix_length,
        in_hbm(document_query),
        branch_q,
        kv,
        in_hbm(cached_k),
        in_hbm(cached_v),
        fresh_k,
        fresh_v,
    )
    acc = block(jnp.stack(above), q, m, acc0, [column], first=1, alias=False)
    far, all_flags = [column], list(above)

    column, for_other = together(column, for_other)
    received = send(for_other, core_swap(), "head")
    for s in (1, 2, 3):
        right, left, acc = together(right, left, acc)
        if s < 3:
            next_right = send(right, z_shift(1))
            next_left = send(left, z_shift(-1))
        else:
            next_right = send(right[:2], z_shift(1))
            next_left = send(left[2:], z_shift(-1))
        flags = column_flags(-s) + column_flags(s)
        acc = block(jnp.stack(flags), q, m, acc, [right, left], first=0, alias=True)
        far += [right, left]
        all_flags += flags
        right, left = next_right, next_left
    right, left, acc = together(right, left, acc)
    flags = column_flags(4)
    attn, mine = last_block(
        jnp.stack(flags),
        jnp.stack(all_flags + flags),
        mine_order,
        q,
        m,
        acc,
        [right, left],
        acc0,
        out_weight,
        far,
        (1,) + (0,) * (len(far) - 1),
    )

    other = send(attn, core_swap(), "head")
    own = own_products(attn, mine, width)
    theirs = in_vmem(received)
    other, own = together(other, own)
    a0, a1 = project(own, other, theirs, (2,))
    via_up = send(a0, x_shift(1), "head")
    via_down = send(a1, x_shift(-1), "head")
    u0, u1, d0, d1 = project(own, other, theirs, (1, 3))
    high_up = send(u1, x_shift(1), "head")
    low_down = send(d0, x_shift(-1), "head")

    def add(a, b):
        return (a.astype(F32) + b.astype(F32)).astype(BF16)

    low_up = send(add(u0, via_up), x_shift(1), "head")
    high_down = send(add(d1, via_down), x_shift(-1), "head")
    home = pl.pallas_call(
        home_kernel,
        out_shape=jax.ShapeDtypeStruct(own.shape[1:], F32),
        in_specs=[VMEM] * 3,
        out_specs=VMEM,
        compiler_params=pltpu.CompilerParams(vmem_limit_bytes=20 << 20),
        cost_estimate=pl.CostEstimate(flops=1 << 29, bytes_accessed=0, transcendentals=0),
    )(own, other, theirs)
    doc_out, branch_out = pl.pallas_call(
        sum_kernel,
        out_shape=[
            jax.ShapeDtypeStruct((CHUNK, width), BF16),
            jax.ShapeDtypeStruct((BRANCH_ROWS, width), BF16),
        ],
        in_specs=[VMEM] * 5,
        out_specs=[VMEM] * 2,
        compiler_params=pltpu.CompilerParams(vmem_limit_bytes=16 << 20),
    )(home, low_up, high_up, low_down, high_down)
    return doc_out, branch_out.reshape(-1, NEW_TOKENS, width)


def solution(mesh):
    placed = (
        P("seq", "head"),
        P("seq", "head"),
        P("seq", "head"),
        P("seq", None, "head"),
        P("seq", None, "head"),
        P("seq", None, "head"),
        P("seq", None, "head"),
        P("seq", None, "head"),
        P("seq"),
        P("head", None),
    )
    return jax.shard_map(
        body,
        mesh=mesh,
        in_specs=placed,
        out_specs=(P("seq", "head"), P("seq", None, "head")),
        check_vma=False,
    )
```

```python
import functools
import math

import jax
import jax.numpy as jnp
from jax import lax
from jax.experimental import pallas as pl
from jax.experimental.pallas import tpu as pltpu
from jax.sharding import PartitionSpec as P

HEAD_SIZE = 128
NEW_TOKENS = 4
GROUP = 8
CHUNK = 256
TILES = 10
BRANCH_ROWS = 64
NY, NZ, NX = 4, 8, 4
SCALE = HEAD_SIZE**-0.5 * math.log2(math.e)
NEG = -1e30
VMEM = pl.BlockSpec(memory_space=pltpu.VMEM)
SMEM = pl.BlockSpec(memory_space=pltpu.SMEM)
HBM = pl.BlockSpec(memory_space=pltpu.HBM)
F32 = jnp.float32
BF16 = jnp.bfloat16


def y_shift(k):
    return [(y * NZ + z, ((y + k) % NY) * NZ + z) for y in range(NY) for z in range(NZ)]


def z_shift(k):
    return [(y * NZ + z, y * NZ + (z + k) % NZ) for y in range(NY) for z in range(NZ)]


def x_shift(k):
    return [(x * 2 + c, ((x + k) % NX) * 2 + c) for x in range(NX) for c in range(2)]


def core_swap():
    return [(x * 2 + c, x * 2 + 1 - c) for x in range(NX) for c in range(2)]


def in_hbm(a):
    return pltpu.with_memory_space_constraint(a, pltpu.HBM)


def in_vmem(a):
    return pltpu.with_memory_space_constraint(a, pltpu.VMEM)


def dot_nt(a, b):
    return lax.dot_general(a, b, (((1,), (1,)), ((), ())), preferred_element_type=F32)


def dot(a, b):
    return jnp.dot(a, b, preferred_element_type=F32)


def row_peak(parts):
    cols = [p[:, i : i + 128] for p in parts for i in range(0, p.shape[1], 128)]
    return jnp.max(functools.reduce(jnp.maximum, cols), axis=1, keepdims=True)


def keys_of(chunk):
    return jnp.concatenate([chunk[:HEAD_SIZE], chunk[HEAD_SIZE : 2 * HEAD_SIZE]], axis=1)


def pack_kernel(k_ref, v_ref, o_ref):
    kt = k_ref[...].T
    o_ref[:HEAD_SIZE, :] = kt[:, :HEAD_SIZE]
    o_ref[HEAD_SIZE:CHUNK, :] = kt[:, HEAD_SIZE:]
    o_ref[CHUNK:, :] = v_ref[...]


def pack(k, v):
    return pl.pallas_call(
        pack_kernel,
        out_shape=jax.ShapeDtypeStruct((2 * CHUNK, HEAD_SIZE), BF16),
        in_specs=[VMEM] * 2,
        out_specs=VMEM,
    )(k, v)


def local_kernel(
    len_ref, dq_hbm, bq_ref, kv_ref, ck_hbm, cv_hbm, fk_ref, fv_ref,
    q_ref, acc_ref, m_ref, va_ref, ca_ref, fa_ref, dq_ref, ck_ref, cv_ref, sems
):
    copies = [
        pltpu.make_async_copy(src, dst, sems.at[i])
        for i, (src, dst) in enumerate(((dq_hbm, dq_ref), (ck_hbm, ck_ref), (cv_hbm, cv_ref)))
    ]
    for copy in copies:
        copy.start()
    copies[0].wait()
    for h in range(GROUP):
        lanes = slice(h * HEAD_SIZE, (h + 1) * HEAD_SIZE)
        q_ref[h] = dq_ref[:, lanes]
        rows = slice((h % 4) * BRANCH_ROWS, (h % 4 + 1) * BRANCH_ROWS)
        q_ref[GROUP + h // 4, rows, :] = bq_ref[:, lanes]
    va_ref[:, :HEAD_SIZE] = kv_ref[CHUNK:, :]
    va_ref[:, HEAD_SIZE:] = jnp.ones((CHUNK, HEAD_SIZE), BF16)
    fa_ref[:, :HEAD_SIZE] = fv_ref[...]
    fa_ref[:, HEAD_SIZE:] = jnp.ones((128, HEAD_SIZE), BF16)
    ca_ref[:, HEAD_SIZE:] = jnp.ones((ca_ref.shape[0], HEAD_SIZE), BF16)
    kt = keys_of(kv_ref)
    row = lax.broadcasted_iota(jnp.int32, (CHUNK, CHUNK), 0)
    col = lax.broadcasted_iota(jnp.int32, (CHUNK, CHUNK), 1)
    causal = col <= row

    def doc(t, _):
        s = jnp.where(causal, dot(q_ref[t], kt), NEG)
        m = row_peak([s]) * SCALE
        p = jnp.exp2(s * SCALE - m).astype(BF16)
        m_ref[t] = jnp.broadcast_to(m, (CHUNK, 128))
        acc_ref[t] = dot(p, va_ref[...])
        return 0

    lax.fori_loop(0, GROUP, doc, 0, unroll=4)

    copies[1].wait()
    copies[2].wait()
    ca_ref[:, :HEAD_SIZE] = cv_ref[...]
    row_branch = (row % BRANCH_ROWS) // NEW_TOKENS
    n_cached = ca_ref.shape[0] // CHUNK
    frow = lax.broadcasted_iota(jnp.int32, (CHUNK, 128), 0)
    fcol = lax.broadcasted_iota(jnp.int32, (CHUNK, 128), 1)
    same = (frow % BRANCH_ROWS) // NEW_TOKENS == fcol // NEW_TOKENS
    fresh_keep = same & (fcol % NEW_TOKENS <= frow % NEW_TOKENS)
    low = col < 128
    for t in (8, 9):
        q = q_ref[t]
        parts = [dot(q, kt)]
        for c in range(n_cached):
            s = dot_nt(q, ck_ref[c * CHUNK : (c + 1) * CHUNK, :])
            length = jnp.where(low, len_ref[2 * c], len_ref[2 * c + 1])
            owner = jnp.where(low, 2 * c, 2 * c + 1)
            keep = (row_branch == owner) & (col % 128 < length)
            parts.append(jnp.where(keep, s, NEG))
        parts.append(jnp.where(fresh_keep, dot_nt(q, fk_ref[...]), NEG))
        m = row_peak(parts) * SCALE
        m_ref[t] = jnp.broadcast_to(m, (CHUNK, 128))
        p = [jnp.exp2(s * SCALE - m).astype(BF16) for s in parts]
        total = dot(p[0], va_ref[...])
        for c in range(n_cached):
            total += dot(p[1 + c], ca_ref[c * CHUNK : (c + 1) * CHUNK, :])
        total += dot(p[-1], fa_ref[...])
        acc_ref[t] = total


def seen(place_ref, shift, rel):
    y, z = place_ref[0], place_ref[1]
    if rel:
        return ((y + rel) % NY < y).astype(jnp.int32)
    return ((z + shift) % NZ < z).astype(jnp.int32)


def accumulate(flags, q_ref, m_ref, acc_in, chunks, acc_ref, va_ref):
    ones = jnp.ones((CHUNK, HEAD_SIZE), F32)
    for c, chunk in enumerate(chunks):
        flag = (ones * flags[c].astype(F32)).astype(BF16)
        v = chunk[CHUNK:, :]
        va_ref[0, c, :, :HEAD_SIZE] = v * flag
        va_ref[0, c, :, HEAD_SIZE:] = flag
        va_ref[1, c, :, :HEAD_SIZE] = v
        va_ref[1, c, :, HEAD_SIZE:] = ones.astype(BF16)

    def tile(t, _):
        q = q_ref[t]
        m = m_ref[t]
        group = (t >= GROUP).astype(jnp.int32)
        total = acc_in[t]
        for c, chunk in enumerate(chunks):
            s = dot(q, keys_of(chunk))
            p = [
                jnp.exp2(s[:, i : i + 128] * SCALE - m).astype(BF16) for i in range(0, CHUNK, 128)
            ]
            total = total + dot(jnp.concatenate(p, axis=1), va_ref[group, c])
        acc_ref[t] = total
        return 0

    lax.fori_loop(0, TILES, tile, 0, unroll=5)


def block_kernel(first, shifts, place_ref, q_ref, m_ref, acc_in, *rest):
    srcs, (acc_ref, va_ref) = rest[:-2], rest[-2:]
    chunks = [s.at[i] for s in srcs for i in range(first, NY)]
    flags = [seen(place_ref, shift, i) for shift in shifts for i in range(first, NY)]
    accumulate(flags, q_ref, m_ref, acc_in, chunks, acc_ref, va_ref)


def block(place, q, m, acc, srcs, shifts, first, alias):
    n = sum(s.shape[0] - first for s in srcs)
    scores = TILES * CHUNK * n * CHUNK
    return pl.pallas_call(
        functools.partial(block_kernel, first, shifts),
        out_shape=pltpu.VMEM(acc.shape, F32),
        in_specs=[SMEM] + [VMEM] * (3 + len(srcs)),
        out_specs=VMEM,
        scratch_shapes=[pltpu.VMEM((2, n, CHUNK, 2 * HEAD_SIZE), BF16)],
        input_output_aliases={3: 0} if alias else {},
        compiler_params=pltpu.CompilerParams(vmem_limit_bytes=16 << 20),
        cost_estimate=pl.CostEstimate(
            flops=scores * 768, bytes_accessed=8 << 20, transcendentals=scores
        ),
    )(place, in_vmem(q), in_vmem(m), in_vmem(acc), *srcs)


def write_rows(out_ref, acc_ref):
    for t in range(GROUP):
        o = acc_ref[t, :, :HEAD_SIZE] / acc_ref[t, :, HEAD_SIZE:]
        out_ref[:CHUNK, t * 128 : (t + 1) * 128] = o.astype(BF16)
    for t in range(GROUP, TILES):
        o = (acc_ref[t, :, :HEAD_SIZE] / acc_ref[t, :, HEAD_SIZE:]).astype(BF16)
        for i in range(4):
            h = (t - GROUP) * 4 + i
            out_ref[CHUNK:, h * 128 : (h + 1) * 128] = o[i * BRANCH_ROWS : (i + 1) * BRANCH_ROWS]


def last_kernel(n_near, shifts, place_ref, q_ref, m_ref, acc_in, *rest):
    near = rest[:n_near]
    acc0_ref, weight_ref, received_ref = rest[n_near : n_near + 3]
    out_ref, mine_ref, theirs_ref, acc_ref, va_ref, run_ref, buf_ref, sem, sems = rest[-9:]
    far = rest[n_near + 3 : -9]
    width = mine_ref.shape[1] // NX
    fetches = [pltpu.make_async_copy(received_ref, theirs_ref, sems.at[NX])]
    for k in range(NX):
        chip = (place_ref[2] + k) % NX
        first = pl.multiple_of((chip * 2 + place_ref[3]) * width, 128)
        fetches.append(
            pltpu.make_async_copy(
                weight_ref.at[:, pl.ds(first, width)],
                mine_ref.at[:, pl.ds(k * width, width)],
                sems.at[k],
            )
        )
    for fetch in fetches:
        fetch.start()
    chunks = [s.at[i] for s in near for i in range(s.shape[0])]
    last_flags = [seen(place_ref, NZ // 2, i) for i in range(NY)]
    accumulate(last_flags, q_ref, m_ref, acc_in, chunks, acc_ref, va_ref)
    peak = functools.reduce(jnp.maximum, [acc_ref[t, :, HEAD_SIZE:] for t in range(TILES)])
    lowest = functools.reduce(jnp.minimum, [acc_ref[t, :, HEAD_SIZE:] for t in range(TILES)])
    fine = jnp.min(jnp.where((peak < 1e30) & (lowest > 0), 1.0, 0.0)) > 0.5

    @pl.when(fine)
    def _():
        write_rows(out_ref, acc_ref)

    @pl.when(jnp.logical_not(fine))
    def _():
        acc_ref[...] = acc0_ref[...]
        run_ref[...] = m_ref[...]

        def online(allowed):
            v = jnp.concatenate(
                [buf_ref[CHUNK:, :], jnp.ones((CHUNK, HEAD_SIZE), BF16)], axis=1
            )

            def tile(t, _):
                s = dot(q_ref[t], keys_of(buf_ref))
                old = run_ref[t]
                new = jnp.maximum(old, row_peak([s]) * SCALE)
                run_ref[t] = new
                decay = jnp.exp2(old - new)
                p = jnp.exp2(s * SCALE - new[:, :1]).astype(BF16)
                acc_ref[t] = acc_ref[t] * jnp.concatenate([decay, decay], axis=1) + dot(p, v)
                return 0

            lax.fori_loop(jnp.where(allowed == 1, 0, GROUP), TILES, tile, 0)

        for ref, shift in zip(far, shifts):
            for i in range(1 if shift == 0 else 0, NY):
                copy = pltpu.make_async_copy(ref.at[i], buf_ref, sem)
                copy.start()
                copy.wait()
                online(seen(place_ref, shift, i))
        for i, chunk in enumerate(chunks):
            buf_ref[...] = chunk[...]
            online(last_flags[i])
        write_rows(out_ref, acc_ref)

    for fetch in fetches:
        fetch.wait()


def last_block(place, q, m, acc, near, acc0, weight, received, far, shifts):
    n = sum(s.shape[0] for s in near)
    scores = TILES * CHUNK * n * CHUNK
    half = pltpu.VMEM((weight.shape[0], weight.shape[1] // 2), BF16)
    return pl.pallas_call(
        functools.partial(last_kernel, len(near), shifts),
        out_shape=[jax.ShapeDtypeStruct((CHUNK + BRANCH_ROWS, GROUP * HEAD_SIZE), BF16), half, half],
        in_specs=[SMEM]
        + [VMEM] * (4 + len(near))
        + [HBM, pl.BlockSpec(memory_space=pl.ANY)]
        + [HBM] * len(far),
        out_specs=[VMEM] * 3,
        scratch_shapes=[
            pltpu.VMEM(acc.shape, F32),
            pltpu.VMEM((2, n, CHUNK, 2 * HEAD_SIZE), BF16),
            pltpu.VMEM(m.shape, F32),
            pltpu.VMEM((2 * CHUNK, HEAD_SIZE), BF16),
            pltpu.SemaphoreType.DMA(()),
            pltpu.SemaphoreType.DMA((NX + 1,)),
        ],
        compiler_params=pltpu.CompilerParams(vmem_limit_bytes=24 << 20),
        cost_estimate=pl.CostEstimate(
            flops=scores * 768, bytes_accessed=8 << 20, transcendentals=scores
        ),
    )(
        place,
        in_vmem(q),
        in_vmem(m),
        in_vmem(acc),
        *near,
        in_vmem(acc0),
        in_hbm(weight),
        received,
        *[in_hbm(a) for a in far],
    )


def copy_kernel(place_ref, w_ref, o_ref):
    del place_ref
    o_ref[...] = w_ref[...]


def columns_for_other(weight, place, width):
    depth = weight.shape[0]
    rows = depth // 4

    def source(i, j, p):
        return j, (p[2] + i) % NX * 2 + 1 - p[3]

    return pl.pallas_call(
        copy_kernel,
        out_shape=jax.ShapeDtypeStruct((depth, NX * width), BF16),
        grid_spec=pltpu.PrefetchScalarGridSpec(
            num_scalar_prefetch=1,
            grid=(NX, 4),
            in_specs=[pl.BlockSpec((rows, width), source)],
            out_specs=pl.BlockSpec((rows, width), lambda i, j, p: (j, i)),
        ),
        compiler_params=pltpu.CompilerParams(vmem_limit_bytes=8 << 20),
        cost_estimate=pl.CostEstimate(
            flops=0, bytes_accessed=4 * depth * NX * width, transcendentals=0
        ),
    )(place, in_hbm(weight))


def own_kernel(a_ref, w_ref, o_ref):
    width = o_ref.shape[2]

    def step(k, _):
        first = pl.multiple_of(k * width, 128)
        o_ref[k] = dot(a_ref[...], w_ref[:, pl.ds(first, width)])
        return 0

    lax.fori_loop(0, NX, step, 0)


def own_products(attn, mine, width):
    rows, depth = attn.shape
    return pl.pallas_call(
        own_kernel,
        out_shape=jax.ShapeDtypeStruct((NX, rows, width), F32),
        in_specs=[VMEM] * 2,
        out_specs=VMEM,
        compiler_params=pltpu.CompilerParams(vmem_limit_bytes=16 << 20),
        cost_estimate=pl.CostEstimate(
            flops=2 * NX * rows * depth * width, bytes_accessed=0, transcendentals=0
        ),
    )(attn, in_vmem(mine))


def project_kernel(steps, own_ref, b_ref, w_ref, *out_refs):
    half, width = out_refs[0].shape
    for i, k in enumerate(steps):
        o = own_ref[k] + dot(b_ref[...], w_ref[:, k * width : (k + 1) * width])
        out_refs[2 * i][...] = o[:half].astype(BF16)
        out_refs[2 * i + 1][...] = o[half:].astype(BF16)


def project(own, other, theirs, steps):
    _, rows, width = own.shape
    half = jax.ShapeDtypeStruct((rows // 2, width), BF16)
    n = len(steps)
    return pl.pallas_call(
        functools.partial(project_kernel, steps),
        out_shape=[half] * (2 * n),
        in_specs=[VMEM] * 3,
        out_specs=[VMEM] * (2 * n),
        compiler_params=pltpu.CompilerParams(vmem_limit_bytes=20 << 20),
        cost_estimate=pl.CostEstimate(
            flops=2 * n * rows * other.shape[1] * width, bytes_accessed=0, transcendentals=0
        ),
    )(in_vmem(own), other, in_vmem(theirs))


def sum_kernel(o_ref, b0, b1, c0, c1, doc_ref, branch_ref):
    half = b0.shape[0]
    low = o_ref[:half] + b0[...].astype(F32) + c0[...].astype(F32)
    high = o_ref[half:] + b1[...].astype(F32) + c1[...].astype(F32)
    rest = CHUNK - half
    doc_ref[:half, :] = low.astype(BF16)
    doc_ref[half:, :] = high[:rest].astype(BF16)
    branch_ref[...] = high[rest:].astype(BF16)


def home_kernel(own_ref, b_ref, w_ref, o_ref):
    o_ref[...] = own_ref[0] + dot(b_ref[...], w_ref[:, : o_ref.shape[1]])


def body(
    document_query,
    document_key,
    document_value,
    branch_token_query,
    branch_token_key,
    branch_token_value,
    branch_cached_key,
    branch_cached_value,
    suffix_length,
    out_weight,
):
    seq = lax.axis_index("seq")
    head = lax.axis_index("head")
    y, z = seq // NZ, seq % NZ
    x, core = head // 2, head % 2
    width = out_weight.shape[1] // (2 * NX)

    def send(a, pairs, axis="seq"):
        return lax.ppermute(a, axis, pairs)

    def together(*a):
        return lax.optimization_barrier(a)

    place = jnp.stack([y, z, x, core]).astype(jnp.int32)
    kv = pack(document_key, document_value)
    from_down = send(kv, y_shift(1))
    from_up = send(kv, y_shift(-1))
    kv, weight = together(kv, out_weight)
    for_other = columns_for_other(weight, place, width)
    from_down, for_other = together(from_down, for_other)
    from_far = send(from_down, y_shift(1))
    column = jnp.stack([kv, from_up, from_far, from_down])
    column, kv = together(column, kv)
    right = send(column, z_shift(1))
    left = send(column, z_shift(-1))

    branch_q = branch_token_query.reshape(BRANCH_ROWS, GROUP * HEAD_SIZE)
    pad = ((0, 128 - BRANCH_ROWS), (0, 0))
    fresh_k = jnp.pad(branch_token_key.reshape(BRANCH_ROWS, HEAD_SIZE), pad)
    fresh_v = jnp.pad(branch_token_value.reshape(BRANCH_ROWS, HEAD_SIZE), pad)
    cached_k = branch_cached_key.reshape(-1, HEAD_SIZE)
    cached_v = branch_cached_value.reshape(-1, HEAD_SIZE)
    q, acc0, m = pl.pallas_call(
        local_kernel,
        out_shape=[
            pltpu.VMEM((TILES, CHUNK, HEAD_SIZE), BF16),
            pltpu.VMEM((TILES, CHUNK, 2 * HEAD_SIZE), F32),
            pltpu.VMEM((TILES, CHUNK, 128), F32),
        ],
        in_specs=[SMEM, HBM, VMEM, VMEM, HBM, HBM, VMEM, VMEM],
        out_specs=[VMEM] * 3,
        scratch_shapes=[
            pltpu.VMEM((CHUNK, 2 * HEAD_SIZE), BF16),
            pltpu.VMEM((cached_v.shape[0], 2 * HEAD_SIZE), BF16),
            pltpu.VMEM((128, 2 * HEAD_SIZE), BF16),
            pltpu.VMEM(document_query.shape, BF16),
            pltpu.VMEM(cached_k.shape, BF16),
            pltpu.VMEM(cached_v.shape, BF16),
            pltpu.SemaphoreType.DMA((3,)),
        ],
        compiler_params=pltpu.CompilerParams(vmem_limit_bytes=24 << 20),
        cost_estimate=pl.CostEstimate(
            flops=4 << 30, bytes_accessed=8 << 20, transcendentals=2 << 20
        ),
    )(
        suffix_length,
        in_hbm(document_query),
        branch_q,
        kv,
        in_hbm(cached_k),
        in_hbm(cached_v),
        fresh_k,
        fresh_v,
    )
    acc = block(place, q, m, acc0, [column], (0,), first=1, alias=False)
    far, shifts = [column], [0]

    column, for_other = together(column, for_other)
    received = send(for_other, core_swap(), "head")
    for s in (1, 2, 3):
        right, left, acc = together(right, left, acc)
        if s < 3:
            next_right = send(right, z_shift(1))
            next_left = send(left, z_shift(-1))
        else:
            next_right = send(right[:2], z_shift(1))
            next_left = send(left[2:], z_shift(-1))
        acc = block(place, q, m, acc, [right, left], (-s, s), first=0, alias=True)
        far += [right, left]
        shifts += [-s, s]
        right, left = next_right, next_left
    right, left, acc = together(right, left, acc)
    attn, mine, theirs = last_block(
        place, q, m, acc, [right, left], acc0, out_weight, received, far, tuple(shifts)
    )

    other = send(attn, core_swap(), "head")
    own = own_products(attn, mine, width)
    other, own = together(other, own)
    a0, a1 = project(own, other, theirs, (2,))
    via_up = send(a0, x_shift(1), "head")
    via_down = send(a1, x_shift(-1), "head")
    u0, u1, d0, d1 = project(own, other, theirs, (1, 3))
    high_up = send(u1, x_shift(1), "head")
    low_down = send(d0, x_shift(-1), "head")

    def add(a, b):
        return (a.astype(F32) + b.astype(F32)).astype(BF16)

    low_up = send(add(u0, via_up), x_shift(1), "head")
    high_down = send(add(d1, via_down), x_shift(-1), "head")
    home = pl.pallas_call(
        home_kernel,
        out_shape=jax.ShapeDtypeStruct(own.shape[1:], F32),
        in_specs=[VMEM] * 3,
        out_specs=VMEM,
        compiler_params=pltpu.CompilerParams(vmem_limit_bytes=20 << 20),
        cost_estimate=pl.CostEstimate(flops=1 << 29, bytes_accessed=0, transcendentals=0),
    )(own, other, theirs)
    doc_out, branch_out = pl.pallas_call(
        sum_kernel,
        out_shape=[
            jax.ShapeDtypeStruct((CHUNK, width), BF16),
            jax.ShapeDtypeStruct((BRANCH_ROWS, width), BF16),
        ],
        in_specs=[VMEM] * 5,
        out_specs=[VMEM] * 2,
        compiler_params=pltpu.CompilerParams(vmem_limit_bytes=16 << 20),
    )(home, low_up, high_up, low_down, high_down)
    return doc_out, branch_out.reshape(-1, NEW_TOKENS, width)


def solution(mesh):
    placed = (
        P("seq", "head"),
        P("seq", "head"),
        P("seq", "head"),
        P("seq", None, "head"),
        P("seq", None, "head"),
        P("seq", None, "head"),
        P("seq", None, "head"),
        P("seq", None, "head"),
        P("seq"),
        P("head", None),
    )
    return jax.shard_map(
        body,
        mesh=mesh,
        in_specs=placed,
        out_specs=(P("seq", "head"), P("seq", None, "head")),
        check_vma=False,
    )
```

```python
import functools
import math

import jax
import jax.numpy as jnp
from jax import lax
from jax.experimental import pallas as pl
from jax.experimental.pallas import tpu as pltpu
from jax.sharding import PartitionSpec as P

HEAD_SIZE = 128
NEW_TOKENS = 4
GROUP = 8
CHUNK = 256
TILES = 10
BRANCH_ROWS = 64
NY, NZ, NX = 4, 8, 4
SCALE = HEAD_SIZE**-0.5 * math.log2(math.e)
NEG = -1e30
VMEM = pl.BlockSpec(memory_space=pltpu.VMEM)
SMEM = pl.BlockSpec(memory_space=pltpu.SMEM)
HBM = pl.BlockSpec(memory_space=pltpu.HBM)
F32 = jnp.float32
BF16 = jnp.bfloat16


def y_shift(k):
    return [(y * NZ + z, ((y + k) % NY) * NZ + z) for y in range(NY) for z in range(NZ)]


def z_shift(k):
    return [(y * NZ + z, y * NZ + (z + k) % NZ) for y in range(NY) for z in range(NZ)]


def x_shift(k):
    return [(x * 2 + c, ((x + k) % NX) * 2 + c) for x in range(NX) for c in range(2)]


def core_swap():
    return [(x * 2 + c, x * 2 + 1 - c) for x in range(NX) for c in range(2)]


def in_hbm(a):
    return pltpu.with_memory_space_constraint(a, pltpu.HBM)


def in_vmem(a):
    return pltpu.with_memory_space_constraint(a, pltpu.VMEM)


def dot_nt(a, b):
    return lax.dot_general(a, b, (((1,), (1,)), ((), ())), preferred_element_type=F32)


def dot(a, b):
    return jnp.dot(a, b, preferred_element_type=F32)


def row_peak(parts):
    cols = [p[:, i : i + 128] for p in parts for i in range(0, p.shape[1], 128)]
    return jnp.max(functools.reduce(jnp.maximum, cols), axis=1, keepdims=True)


def keys_of(chunk):
    return jnp.concatenate([chunk[:HEAD_SIZE], chunk[HEAD_SIZE : 2 * HEAD_SIZE]], axis=1)


def pack_kernel(k_ref, v_ref, o_ref):
    kt = k_ref[...].T
    o_ref[:HEAD_SIZE, :] = kt[:, :HEAD_SIZE]
    o_ref[HEAD_SIZE:CHUNK, :] = kt[:, HEAD_SIZE:]
    o_ref[CHUNK:, :] = v_ref[...]


def pack(k, v):
    return pl.pallas_call(
        pack_kernel,
        out_shape=jax.ShapeDtypeStruct((2 * CHUNK, HEAD_SIZE), BF16),
        in_specs=[VMEM] * 2,
        out_specs=VMEM,
    )(k, v)


def local_kernel(
    len_ref, dq_hbm, bq_ref, kv_ref, ck_hbm, cv_hbm, fk_ref, fv_ref,
    q_ref, acc_ref, m_ref, va_ref, ca_ref, fa_ref, dq_ref, ck_ref, cv_ref, sems
):
    copies = [
        pltpu.make_async_copy(src, dst, sems.at[i])
        for i, (src, dst) in enumerate(((dq_hbm, dq_ref), (ck_hbm, ck_ref), (cv_hbm, cv_ref)))
    ]
    for copy in copies:
        copy.start()
    copies[0].wait()
    for h in range(GROUP):
        lanes = slice(h * HEAD_SIZE, (h + 1) * HEAD_SIZE)
        q_ref[h] = dq_ref[:, lanes]
        rows = slice((h % 4) * BRANCH_ROWS, (h % 4 + 1) * BRANCH_ROWS)
        q_ref[GROUP + h // 4, rows, :] = bq_ref[:, lanes]
    va_ref[:, :HEAD_SIZE] = kv_ref[CHUNK:, :]
    va_ref[:, HEAD_SIZE:] = jnp.ones((CHUNK, HEAD_SIZE), BF16)
    fa_ref[:, :HEAD_SIZE] = fv_ref[...]
    fa_ref[:, HEAD_SIZE:] = jnp.ones((128, HEAD_SIZE), BF16)
    ca_ref[:, HEAD_SIZE:] = jnp.ones((ca_ref.shape[0], HEAD_SIZE), BF16)
    kt = keys_of(kv_ref)
    row = lax.broadcasted_iota(jnp.int32, (CHUNK, CHUNK), 0)
    col = lax.broadcasted_iota(jnp.int32, (CHUNK, CHUNK), 1)
    causal = col <= row

    def doc(t, _):
        s = jnp.where(causal, dot(q_ref[t], kt), NEG)
        m = row_peak([s]) * SCALE
        p = jnp.exp2(s * SCALE - m).astype(BF16)
        m_ref[t] = jnp.broadcast_to(m, (CHUNK, 128))
        acc_ref[t] = dot(p, va_ref[...])
        return 0

    lax.fori_loop(0, GROUP, doc, 0, unroll=4)

    copies[1].wait()
    copies[2].wait()
    ca_ref[:, :HEAD_SIZE] = cv_ref[...]
    row_branch = (row % BRANCH_ROWS) // NEW_TOKENS
    n_cached = ca_ref.shape[0] // CHUNK
    frow = lax.broadcasted_iota(jnp.int32, (CHUNK, 128), 0)
    fcol = lax.broadcasted_iota(jnp.int32, (CHUNK, 128), 1)
    same = (frow % BRANCH_ROWS) // NEW_TOKENS == fcol // NEW_TOKENS
    fresh_keep = same & (fcol % NEW_TOKENS <= frow % NEW_TOKENS)
    low = col < 128
    for t in (8, 9):
        q = q_ref[t]
        parts = [dot(q, kt)]
        for c in range(n_cached):
            s = dot_nt(q, ck_ref[c * CHUNK : (c + 1) * CHUNK, :])
            length = jnp.where(low, len_ref[2 * c], len_ref[2 * c + 1])
            owner = jnp.where(low, 2 * c, 2 * c + 1)
            keep = (row_branch == owner) & (col % 128 < length)
            parts.append(jnp.where(keep, s, NEG))
        parts.append(jnp.where(fresh_keep, dot_nt(q, fk_ref[...]), NEG))
        m = row_peak(parts) * SCALE
        m_ref[t] = jnp.broadcast_to(m, (CHUNK, 128))
        p = [jnp.exp2(s * SCALE - m).astype(BF16) for s in parts]
        total = dot(p[0], va_ref[...])
        for c in range(n_cached):
            total += dot(p[1 + c], ca_ref[c * CHUNK : (c + 1) * CHUNK, :])
        total += dot(p[-1], fa_ref[...])
        acc_ref[t] = total


def seen(place_ref, shift, rel):
    y, z = place_ref[0], place_ref[1]
    if rel:
        return ((y + rel) % NY < y).astype(jnp.int32)
    return ((z + shift) % NZ < z).astype(jnp.int32)


def accumulate(flags, q_ref, m_ref, acc_in, chunks, acc_ref, va_ref):
    ones = jnp.ones((CHUNK, HEAD_SIZE), F32)
    for c, chunk in enumerate(chunks):
        flag = (ones * flags[c].astype(F32)).astype(BF16)
        v = chunk[CHUNK:, :]
        va_ref[0, c, :, :HEAD_SIZE] = v * flag
        va_ref[0, c, :, HEAD_SIZE:] = flag
        va_ref[1, c, :, :HEAD_SIZE] = v
        va_ref[1, c, :, HEAD_SIZE:] = ones.astype(BF16)

    def tile(t, _):
        q = q_ref[t]
        m = m_ref[t]
        group = (t >= GROUP).astype(jnp.int32)
        total = acc_in[t]
        for c, chunk in enumerate(chunks):
            s = dot(q, keys_of(chunk))
            p = [
                jnp.exp2(s[:, i : i + 128] * SCALE - m).astype(BF16) for i in range(0, CHUNK, 128)
            ]
            total = total + dot(jnp.concatenate(p, axis=1), va_ref[group, c])
        acc_ref[t] = total
        return 0

    lax.fori_loop(0, TILES, tile, 0, unroll=5)


def block_kernel(first, shifts, place_ref, q_ref, m_ref, acc_in, *rest):
    srcs, (acc_ref, va_ref) = rest[:-2], rest[-2:]
    chunks = [s.at[i] for s in srcs for i in range(first, NY)]
    flags = [seen(place_ref, shift, i) for shift in shifts for i in range(first, NY)]
    accumulate(flags, q_ref, m_ref, acc_in, chunks, acc_ref, va_ref)


def block(place, q, m, acc, srcs, shifts, first, alias):
    n = sum(s.shape[0] - first for s in srcs)
    scores = TILES * CHUNK * n * CHUNK
    return pl.pallas_call(
        functools.partial(block_kernel, first, shifts),
        out_shape=pltpu.VMEM(acc.shape, F32),
        in_specs=[SMEM] + [VMEM] * (3 + len(srcs)),
        out_specs=VMEM,
        scratch_shapes=[pltpu.VMEM((2, n, CHUNK, 2 * HEAD_SIZE), BF16)],
        input_output_aliases={3: 0} if alias else {},
        compiler_params=pltpu.CompilerParams(vmem_limit_bytes=16 << 20),
        cost_estimate=pl.CostEstimate(
            flops=scores * 768, bytes_accessed=8 << 20, transcendentals=scores
        ),
    )(place, in_vmem(q), in_vmem(m), in_vmem(acc), *srcs)


def write_rows(out_ref, acc_ref):
    for t in range(GROUP):
        o = acc_ref[t, :, :HEAD_SIZE] / acc_ref[t, :, HEAD_SIZE:]
        out_ref[:CHUNK, t * 128 : (t + 1) * 128] = o.astype(BF16)
    for t in range(GROUP, TILES):
        o = (acc_ref[t, :, :HEAD_SIZE] / acc_ref[t, :, HEAD_SIZE:]).astype(BF16)
        for i in range(4):
            h = (t - GROUP) * 4 + i
            out_ref[CHUNK:, h * 128 : (h + 1) * 128] = o[i * BRANCH_ROWS : (i + 1) * BRANCH_ROWS]


def last_kernel(n_near, shifts, place_ref, q_ref, m_ref, acc_in, *rest):
    near = rest[:n_near]
    acc0_ref, weight_ref, received_ref = rest[n_near : n_near + 3]
    out_ref, mine_ref, theirs_ref, acc_ref, va_ref, run_ref, buf_ref, sem, sems = rest[-9:]
    far = rest[n_near + 3 : -9]
    width = mine_ref.shape[1] // NX
    fetches = [pltpu.make_async_copy(received_ref, theirs_ref, sems.at[NX])]
    for k in range(NX):
        chip = (place_ref[2] + k) % NX
        first = pl.multiple_of((chip * 2 + place_ref[3]) * width, 128)
        fetches.append(
            pltpu.make_async_copy(
                weight_ref.at[:, pl.ds(first, width)],
                mine_ref.at[:, pl.ds(k * width, width)],
                sems.at[k],
            )
        )
    for fetch in fetches:
        fetch.start()
    chunks = [s.at[i] for s in near for i in range(s.shape[0])]
    last_flags = [seen(place_ref, NZ // 2, i) for i in range(NY)]
    accumulate(last_flags, q_ref, m_ref, acc_in, chunks, acc_ref, va_ref)
    peak = functools.reduce(jnp.maximum, [acc_ref[t, :, HEAD_SIZE:] for t in range(TILES)])
    lowest = functools.reduce(jnp.minimum, [acc_ref[t, :, HEAD_SIZE:] for t in range(TILES)])
    fine = jnp.min(jnp.where((peak < 1e30) & (lowest > 0), 1.0, 0.0)) > 0.5

    @pl.when(fine)
    def _():
        write_rows(out_ref, acc_ref)

    @pl.when(jnp.logical_not(fine))
    def _():
        acc_ref[...] = acc0_ref[...]
        run_ref[...] = m_ref[...]

        def online(allowed):
            v = jnp.concatenate(
                [buf_ref[CHUNK:, :], jnp.ones((CHUNK, HEAD_SIZE), BF16)], axis=1
            )

            def tile(t, _):
                s = dot(q_ref[t], keys_of(buf_ref))
                old = run_ref[t]
                new = jnp.maximum(old, row_peak([s]) * SCALE)
                run_ref[t] = new
                decay = jnp.exp2(old - new)
                p = jnp.exp2(s * SCALE - new[:, :1]).astype(BF16)
                acc_ref[t] = acc_ref[t] * jnp.concatenate([decay, decay], axis=1) + dot(p, v)
                return 0

            lax.fori_loop(jnp.where(allowed == 1, 0, GROUP), TILES, tile, 0)

        for ref, shift in zip(far, shifts):
            for i in range(1 if shift == 0 else 0, NY):
                copy = pltpu.make_async_copy(ref.at[i], buf_ref, sem)
                copy.start()
                copy.wait()
                online(seen(place_ref, shift, i))
        for i, chunk in enumerate(chunks):
            buf_ref[...] = chunk[...]
            online(last_flags[i])
        write_rows(out_ref, acc_ref)

    for fetch in fetches:
        fetch.wait()


def last_block(place, q, m, acc, near, acc0, weight, received, far, shifts):
    n = sum(s.shape[0] for s in near)
    scores = TILES * CHUNK * n * CHUNK
    half = pltpu.VMEM((weight.shape[0], weight.shape[1] // 2), BF16)
    return pl.pallas_call(
        functools.partial(last_kernel, len(near), shifts),
        out_shape=[jax.ShapeDtypeStruct((CHUNK + BRANCH_ROWS, GROUP * HEAD_SIZE), BF16), half, half],
        in_specs=[SMEM]
        + [VMEM] * (4 + len(near))
        + [HBM, pl.BlockSpec(memory_space=pl.ANY)]
        + [HBM] * len(far),
        out_specs=[VMEM] * 3,
        scratch_shapes=[
            pltpu.VMEM(acc.shape, F32),
            pltpu.VMEM((2, n, CHUNK, 2 * HEAD_SIZE), BF16),
            pltpu.VMEM(m.shape, F32),
            pltpu.VMEM((2 * CHUNK, HEAD_SIZE), BF16),
            pltpu.SemaphoreType.DMA(()),
            pltpu.SemaphoreType.DMA((NX + 1,)),
        ],
        compiler_params=pltpu.CompilerParams(vmem_limit_bytes=24 << 20),
        cost_estimate=pl.CostEstimate(
            flops=scores * 768, bytes_accessed=8 << 20, transcendentals=scores
        ),
    )(
        place,
        in_vmem(q),
        in_vmem(m),
        in_vmem(acc),
        *near,
        in_vmem(acc0),
        in_hbm(weight),
        received,
        *[in_hbm(a) for a in far],
    )


def columns_kernel(place_ref, w_ref, o_ref, sems):
    width = o_ref.shape[1] // NX
    copies = []
    for k in range(NX):
        chip = (place_ref[2] + k) % NX
        first = pl.multiple_of((chip * 2 + 1 - place_ref[3]) * width, 128)
        copies.append(
            pltpu.make_async_copy(
                w_ref.at[:, pl.ds(first, width)], o_ref.at[:, pl.ds(k * width, width)], sems.at[k]
            )
        )
    for copy in copies:
        copy.start()
    for copy in copies:
        copy.wait()


def columns_for_other(weight, place):
    return pl.pallas_call(
        columns_kernel,
        out_shape=pltpu.VMEM((weight.shape[0], weight.shape[1] // 2), BF16),
        in_specs=[SMEM, HBM],
        out_specs=VMEM,
        scratch_shapes=[pltpu.SemaphoreType.DMA((NX,))],
        compiler_params=pltpu.CompilerParams(vmem_limit_bytes=8 << 20),
        cost_estimate=pl.CostEstimate(
            flops=0, bytes_accessed=2 * weight.size, transcendentals=0
        ),
    )(place, in_hbm(weight))


def own_kernel(a_ref, w_ref, o_ref):
    width = o_ref.shape[2]

    def step(k, _):
        first = pl.multiple_of(k * width, 128)
        o_ref[k] = dot(a_ref[...], w_ref[:, pl.ds(first, width)])
        return 0

    lax.fori_loop(0, NX, step, 0)


def own_products(attn, mine, width):
    rows, depth = attn.shape
    return pl.pallas_call(
        own_kernel,
        out_shape=jax.ShapeDtypeStruct((NX, rows, width), F32),
        in_specs=[VMEM] * 2,
        out_specs=VMEM,
        compiler_params=pltpu.CompilerParams(vmem_limit_bytes=16 << 20),
        cost_estimate=pl.CostEstimate(
            flops=2 * NX * rows * depth * width, bytes_accessed=0, transcendentals=0
        ),
    )(attn, in_vmem(mine))


def project_kernel(steps, own_ref, b_ref, w_ref, *out_refs):
    half, width = out_refs[0].shape
    for i, k in enumerate(steps):
        o = own_ref[k] + dot(b_ref[...], w_ref[:, k * width : (k + 1) * width])
        out_refs[2 * i][...] = o[:half].astype(BF16)
        out_refs[2 * i + 1][...] = o[half:].astype(BF16)


def project(own, other, theirs, steps):
    _, rows, width = own.shape
    half = jax.ShapeDtypeStruct((rows // 2, width), BF16)
    n = len(steps)
    return pl.pallas_call(
        functools.partial(project_kernel, steps),
        out_shape=[half] * (2 * n),
        in_specs=[VMEM] * 3,
        out_specs=[VMEM] * (2 * n),
        compiler_params=pltpu.CompilerParams(vmem_limit_bytes=20 << 20),
        cost_estimate=pl.CostEstimate(
            flops=2 * n * rows * other.shape[1] * width, bytes_accessed=0, transcendentals=0
        ),
    )(in_vmem(own), other, in_vmem(theirs))


def sum_kernel(o_ref, b0, b1, c0, c1, doc_ref, branch_ref):
    half = b0.shape[0]
    low = o_ref[:half] + b0[...].astype(F32) + c0[...].astype(F32)
    high = o_ref[half:] + b1[...].astype(F32) + c1[...].astype(F32)
    rest = CHUNK - half
    doc_ref[:half, :] = low.astype(BF16)
    doc_ref[half:, :] = high[:rest].astype(BF16)
    branch_ref[...] = high[rest:].astype(BF16)


def home_kernel(own_ref, b_ref, w_ref, o_ref):
    o_ref[...] = own_ref[0] + dot(b_ref[...], w_ref[:, : o_ref.shape[1]])


def body(
    document_query,
    document_key,
    document_value,
    branch_token_query,
    branch_token_key,
    branch_token_value,
    branch_cached_key,
    branch_cached_value,
    suffix_length,
    out_weight,
):
    seq = lax.axis_index("seq")
    head = lax.axis_index("head")
    y, z = seq // NZ, seq % NZ
    x, core = head // 2, head % 2
    width = out_weight.shape[1] // (2 * NX)

    def send(a, pairs, axis="seq"):
        return lax.ppermute(a, axis, pairs)

    def together(*a):
        return lax.optimization_barrier(a)

    place = jnp.stack([y, z, x, core]).astype(jnp.int32)
    kv = pack(document_key, document_value)
    from_down = send(kv, y_shift(1))
    from_up = send(kv, y_shift(-1))
    kv, weight = together(kv, out_weight)
    for_other = columns_for_other(weight, place)
    from_down, for_other = together(from_down, for_other)
    from_far = send(from_down, y_shift(1))
    column = jnp.stack([kv, from_up, from_far, from_down])
    column, kv = together(column, kv)
    right = send(column, z_shift(1))
    left = send(column, z_shift(-1))

    branch_q = branch_token_query.reshape(BRANCH_ROWS, GROUP * HEAD_SIZE)
    pad = ((0, 128 - BRANCH_ROWS), (0, 0))
    fresh_k = jnp.pad(branch_token_key.reshape(BRANCH_ROWS, HEAD_SIZE), pad)
    fresh_v = jnp.pad(branch_token_value.reshape(BRANCH_ROWS, HEAD_SIZE), pad)
    cached_k = branch_cached_key.reshape(-1, HEAD_SIZE)
    cached_v = branch_cached_value.reshape(-1, HEAD_SIZE)
    q, acc0, m = pl.pallas_call(
        local_kernel,
        out_shape=[
            pltpu.VMEM((TILES, CHUNK, HEAD_SIZE), BF16),
            pltpu.VMEM((TILES, CHUNK, 2 * HEAD_SIZE), F32),
            pltpu.VMEM((TILES, CHUNK, 128), F32),
        ],
        in_specs=[SMEM, HBM, VMEM, VMEM, HBM, HBM, VMEM, VMEM],
        out_specs=[VMEM] * 3,
        scratch_shapes=[
            pltpu.VMEM((CHUNK, 2 * HEAD_SIZE), BF16),
            pltpu.VMEM((cached_v.shape[0], 2 * HEAD_SIZE), BF16),
            pltpu.VMEM((128, 2 * HEAD_SIZE), BF16),
            pltpu.VMEM(document_query.shape, BF16),
            pltpu.VMEM(cached_k.shape, BF16),
            pltpu.VMEM(cached_v.shape, BF16),
            pltpu.SemaphoreType.DMA((3,)),
        ],
        compiler_params=pltpu.CompilerParams(vmem_limit_bytes=24 << 20),
        cost_estimate=pl.CostEstimate(
            flops=4 << 30, bytes_accessed=8 << 20, transcendentals=2 << 20
        ),
    )(
        suffix_length,
        in_hbm(document_query),
        branch_q,
        kv,
        in_hbm(cached_k),
        in_hbm(cached_v),
        fresh_k,
        fresh_v,
    )
    acc = block(place, q, m, acc0, [column], (0,), first=1, alias=False)
    far, shifts = [column], [0]

    acc, for_other = together(acc, for_other)
    received = send(for_other, core_swap(), "head")
    for s in (1, 2, 3):
        right, left, acc = together(right, left, acc)
        if s < 3:
            next_right = send(right, z_shift(1))
            next_left = send(left, z_shift(-1))
        else:
            next_right = send(right[:2], z_shift(1))
            next_left = send(left[2:], z_shift(-1))
        acc = block(place, q, m, acc, [right, left], (-s, s), first=0, alias=True)
        far += [right, left]
        shifts += [-s, s]
        right, left = next_right, next_left
    right, left, acc = together(right, left, acc)
    attn, mine, theirs = last_block(
        place, q, m, acc, [right, left], acc0, out_weight, received, far, tuple(shifts)
    )

    other = send(attn, core_swap(), "head")
    own = own_products(attn, mine, width)
    other, own = together(other, own)
    a0, a1 = project(own, other, theirs, (2,))
    via_up = send(a0, x_shift(1), "head")
    via_down = send(a1, x_shift(-1), "head")
    u0, u1, d0, d1 = project(own, other, theirs, (1, 3))
    high_up = send(u1, x_shift(1), "head")
    low_down = send(d0, x_shift(-1), "head")

    def add(a, b):
        return (a.astype(F32) + b.astype(F32)).astype(BF16)

    low_up = send(add(u0, via_up), x_shift(1), "head")
    high_down = send(add(d1, via_down), x_shift(-1), "head")
    home = pl.pallas_call(
        home_kernel,
        out_shape=jax.ShapeDtypeStruct(own.shape[1:], F32),
        in_specs=[VMEM] * 3,
        out_specs=VMEM,
        compiler_params=pltpu.CompilerParams(vmem_limit_bytes=20 << 20),
        cost_estimate=pl.CostEstimate(flops=1 << 29, bytes_accessed=0, transcendentals=0),
    )(own, other, theirs)
    doc_out, branch_out = pl.pallas_call(
        sum_kernel,
        out_shape=[
            jax.ShapeDtypeStruct((CHUNK, width), BF16),
            jax.ShapeDtypeStruct((BRANCH_ROWS, width), BF16),
        ],
        in_specs=[VMEM] * 5,
        out_specs=[VMEM] * 2,
        compiler_params=pltpu.CompilerParams(vmem_limit_bytes=16 << 20),
    )(home, low_up, high_up, low_down, high_down)
    return doc_out, branch_out.reshape(-1, NEW_TOKENS, width)


def solution(mesh):
    placed = (
        P("seq", "head"),
        P("seq", "head"),
        P("seq", "head"),
        P("seq", None, "head"),
        P("seq", None, "head"),
        P("seq", None, "head"),
        P("seq", None, "head"),
        P("seq", None, "head"),
        P("seq"),
        P("head", None),
    )
    return jax.shard_map(
        body,
        mesh=mesh,
        in_specs=placed,
        out_specs=(P("seq", "head"), P("seq", None, "head")),
        check_vma=False,
    )
```

```python
import functools
import math

import jax
import jax.numpy as jnp
from jax import lax
from jax.experimental import pallas as pl
from jax.experimental.pallas import tpu as pltpu
from jax.sharding import PartitionSpec as P

HEAD_SIZE = 128
NEW_TOKENS = 4
GROUP = 8
CHUNK = 256
TILES = 10
BRANCH_ROWS = 64
NY, NZ, NX = 4, 8, 4
SCALE = HEAD_SIZE**-0.5 * math.log2(math.e)
NEG = -1e30
VMEM = pl.BlockSpec(memory_space=pltpu.VMEM)
SMEM = pl.BlockSpec(memory_space=pltpu.SMEM)
HBM = pl.BlockSpec(memory_space=pltpu.HBM)
F32 = jnp.float32
BF16 = jnp.bfloat16


def y_shift(k):
    return [(y * NZ + z, ((y + k) % NY) * NZ + z) for y in range(NY) for z in range(NZ)]


def z_shift(k):
    return [(y * NZ + z, y * NZ + (z + k) % NZ) for y in range(NY) for z in range(NZ)]


def x_shift(k):
    return [(x * 2 + c, ((x + k) % NX) * 2 + c) for x in range(NX) for c in range(2)]


def core_swap():
    return [(x * 2 + c, x * 2 + 1 - c) for x in range(NX) for c in range(2)]


def in_hbm(a):
    return pltpu.with_memory_space_constraint(a, pltpu.HBM)


def in_vmem(a):
    return pltpu.with_memory_space_constraint(a, pltpu.VMEM)


def dot_nt(a, b):
    return lax.dot_general(a, b, (((1,), (1,)), ((), ())), preferred_element_type=F32)


def dot(a, b):
    return jnp.dot(a, b, preferred_element_type=F32)


def row_peak(parts):
    cols = [p[:, i : i + 128] for p in parts for i in range(0, p.shape[1], 128)]
    return jnp.max(functools.reduce(jnp.maximum, cols), axis=1, keepdims=True)


def keys_of(chunk):
    return jnp.concatenate([chunk[:HEAD_SIZE], chunk[HEAD_SIZE : 2 * HEAD_SIZE]], axis=1)


def pack_kernel(k_ref, v_ref, o_ref):
    kt = k_ref[...].T
    o_ref[:HEAD_SIZE, :] = kt[:, :HEAD_SIZE]
    o_ref[HEAD_SIZE:CHUNK, :] = kt[:, HEAD_SIZE:]
    o_ref[CHUNK:, :] = v_ref[...]


def pack(k, v):
    return pl.pallas_call(
        pack_kernel,
        out_shape=jax.ShapeDtypeStruct((2 * CHUNK, HEAD_SIZE), BF16),
        in_specs=[VMEM] * 2,
        out_specs=VMEM,
    )(k, v)


def local_kernel(
    len_ref, dq_hbm, bq_ref, kv_ref, ck_hbm, cv_hbm, fk_ref, fv_ref,
    q_ref, acc_ref, m_ref, va_ref, ca_ref, fa_ref, dq_ref, ck_ref, cv_ref, sems
):
    copies = [
        pltpu.make_async_copy(src, dst, sems.at[i])
        for i, (src, dst) in enumerate(((dq_hbm, dq_ref), (ck_hbm, ck_ref), (cv_hbm, cv_ref)))
    ]
    for copy in copies:
        copy.start()
    copies[0].wait()
    for h in range(GROUP):
        lanes = slice(h * HEAD_SIZE, (h + 1) * HEAD_SIZE)
        q_ref[h] = dq_ref[:, lanes]
        rows = slice((h % 4) * BRANCH_ROWS, (h % 4 + 1) * BRANCH_ROWS)
        q_ref[GROUP + h // 4, rows, :] = bq_ref[:, lanes]
    va_ref[:, :HEAD_SIZE] = kv_ref[CHUNK:, :]
    va_ref[:, HEAD_SIZE:] = jnp.ones((CHUNK, HEAD_SIZE), BF16)
    fa_ref[:, :HEAD_SIZE] = fv_ref[...]
    fa_ref[:, HEAD_SIZE:] = jnp.ones((128, HEAD_SIZE), BF16)
    ca_ref[:, HEAD_SIZE:] = jnp.ones((ca_ref.shape[0], HEAD_SIZE), BF16)
    kt = keys_of(kv_ref)
    row = lax.broadcasted_iota(jnp.int32, (CHUNK, CHUNK), 0)
    col = lax.broadcasted_iota(jnp.int32, (CHUNK, CHUNK), 1)
    causal = col <= row

    def doc(t, _):
        s = jnp.where(causal, dot(q_ref[t], kt), NEG)
        m = row_peak([s]) * SCALE
        p = jnp.exp2(s * SCALE - m).astype(BF16)
        m_ref[t] = jnp.broadcast_to(m, (CHUNK, 128))
        acc_ref[t] = dot(p, va_ref[...])
        return 0

    lax.fori_loop(0, GROUP, doc, 0, unroll=4)

    copies[1].wait()
    copies[2].wait()
    ca_ref[:, :HEAD_SIZE] = cv_ref[...]
    row_branch = (row % BRANCH_ROWS) // NEW_TOKENS
    n_cached = ca_ref.shape[0] // CHUNK
    frow = lax.broadcasted_iota(jnp.int32, (CHUNK, 128), 0)
    fcol = lax.broadcasted_iota(jnp.int32, (CHUNK, 128), 1)
    same = (frow % BRANCH_ROWS) // NEW_TOKENS == fcol // NEW_TOKENS
    fresh_keep = same & (fcol % NEW_TOKENS <= frow % NEW_TOKENS)
    low = col < 128
    for t in (8, 9):
        q = q_ref[t]
        parts = [dot(q, kt)]
        for c in range(n_cached):
            s = dot_nt(q, ck_ref[c * CHUNK : (c + 1) * CHUNK, :])
            length = jnp.where(low, len_ref[2 * c], len_ref[2 * c + 1])
            owner = jnp.where(low, 2 * c, 2 * c + 1)
            keep = (row_branch == owner) & (col % 128 < length)
            parts.append(jnp.where(keep, s, NEG))
        parts.append(jnp.where(fresh_keep, dot_nt(q, fk_ref[...]), NEG))
        m = row_peak(parts) * SCALE
        m_ref[t] = jnp.broadcast_to(m, (CHUNK, 128))
        p = [jnp.exp2(s * SCALE - m).astype(BF16) for s in parts]
        total = dot(p[0], va_ref[...])
        for c in range(n_cached):
            total += dot(p[1 + c], ca_ref[c * CHUNK : (c + 1) * CHUNK, :])
        total += dot(p[-1], fa_ref[...])
        acc_ref[t] = total


def seen(place_ref, shift, rel):
    y, z = place_ref[0], place_ref[1]
    if rel:
        return ((y + rel) % NY < y).astype(jnp.int32)
    return ((z + shift) % NZ < z).astype(jnp.int32)


def accumulate(flags, q_ref, m_ref, acc_in, chunks, acc_ref, va_ref):
    ones = jnp.ones((CHUNK, HEAD_SIZE), F32)
    for c, chunk in enumerate(chunks):
        flag = (ones * flags[c].astype(F32)).astype(BF16)
        v = chunk[CHUNK:, :]
        va_ref[0, c, :, :HEAD_SIZE] = v * flag
        va_ref[0, c, :, HEAD_SIZE:] = flag
        va_ref[1, c, :, :HEAD_SIZE] = v
        va_ref[1, c, :, HEAD_SIZE:] = ones.astype(BF16)

    def tile(t, _):
        q = q_ref[t]
        m = m_ref[t]
        group = (t >= GROUP).astype(jnp.int32)
        total = acc_in[t]
        for c, chunk in enumerate(chunks):
            s = dot(q, keys_of(chunk))
            p = [
                jnp.exp2(s[:, i : i + 128] * SCALE - m).astype(BF16) for i in range(0, CHUNK, 128)
            ]
            total = total + dot(jnp.concatenate(p, axis=1), va_ref[group, c])
        acc_ref[t] = total
        return 0

    lax.fori_loop(0, TILES, tile, 0, unroll=5)


def block_kernel(first, shifts, place_ref, q_ref, m_ref, acc_in, *rest):
    srcs, (acc_ref, va_ref) = rest[:-2], rest[-2:]
    chunks = [s.at[i] for s in srcs for i in range(first, NY)]
    flags = [seen(place_ref, shift, i) for shift in shifts for i in range(first, NY)]
    accumulate(flags, q_ref, m_ref, acc_in, chunks, acc_ref, va_ref)


def block(place, q, m, acc, srcs, shifts, first, alias):
    n = sum(s.shape[0] - first for s in srcs)
    scores = TILES * CHUNK * n * CHUNK
    return pl.pallas_call(
        functools.partial(block_kernel, first, shifts),
        out_shape=pltpu.VMEM(acc.shape, F32),
        in_specs=[SMEM] + [VMEM] * (3 + len(srcs)),
        out_specs=VMEM,
        scratch_shapes=[pltpu.VMEM((2, n, CHUNK, 2 * HEAD_SIZE), BF16)],
        input_output_aliases={3: 0} if alias else {},
        compiler_params=pltpu.CompilerParams(vmem_limit_bytes=16 << 20),
        cost_estimate=pl.CostEstimate(
            flops=scores * 768, bytes_accessed=8 << 20, transcendentals=scores
        ),
    )(place, in_vmem(q), in_vmem(m), in_vmem(acc), *srcs)


def write_rows(out_ref, acc_ref):
    for t in range(GROUP):
        o = acc_ref[t, :, :HEAD_SIZE] / acc_ref[t, :, HEAD_SIZE:]
        out_ref[:CHUNK, t * 128 : (t + 1) * 128] = o.astype(BF16)
    for t in range(GROUP, TILES):
        o = (acc_ref[t, :, :HEAD_SIZE] / acc_ref[t, :, HEAD_SIZE:]).astype(BF16)
        for i in range(4):
            h = (t - GROUP) * 4 + i
            out_ref[CHUNK:, h * 128 : (h + 1) * 128] = o[i * BRANCH_ROWS : (i + 1) * BRANCH_ROWS]


def last_kernel(n_near, shifts, place_ref, q_ref, m_ref, acc_in, *rest):
    near = rest[:n_near]
    acc0_ref, weight_ref, received_ref = rest[n_near : n_near + 3]
    out_ref, mine_ref, theirs_ref, acc_ref, va_ref, run_ref, buf_ref, sem, sems = rest[-9:]
    far = rest[n_near + 3 : -9]
    width = mine_ref.shape[1] // NX
    fetches = [pltpu.make_async_copy(received_ref, theirs_ref, sems.at[NX])]
    for k in range(NX):
        chip = (place_ref[2] + k) % NX
        first = pl.multiple_of((chip * 2 + place_ref[3]) * width, 128)
        fetches.append(
            pltpu.make_async_copy(
                weight_ref.at[:, pl.ds(first, width)],
                mine_ref.at[:, pl.ds(k * width, width)],
                sems.at[k],
            )
        )
    for fetch in fetches:
        fetch.start()
    chunks = [s.at[i] for s in near for i in range(s.shape[0])]
    last_flags = [seen(place_ref, NZ // 2, i) for i in range(NY)]
    accumulate(last_flags, q_ref, m_ref, acc_in, chunks, acc_ref, va_ref)
    peak = functools.reduce(jnp.maximum, [acc_ref[t, :, HEAD_SIZE:] for t in range(TILES)])
    lowest = functools.reduce(jnp.minimum, [acc_ref[t, :, HEAD_SIZE:] for t in range(TILES)])
    fine = jnp.min(jnp.where((peak < 1e30) & (lowest > 0), 1.0, 0.0)) > 0.5

    @pl.when(fine)
    def _():
        write_rows(out_ref, acc_ref)

    @pl.when(jnp.logical_not(fine))
    def _():
        acc_ref[...] = acc0_ref[...]
        run_ref[...] = m_ref[...]

        def online(allowed):
            v = jnp.concatenate(
                [buf_ref[CHUNK:, :], jnp.ones((CHUNK, HEAD_SIZE), BF16)], axis=1
            )

            def tile(t, _):
                s = dot(q_ref[t], keys_of(buf_ref))
                old = run_ref[t]
                new = jnp.maximum(old, row_peak([s]) * SCALE)
                run_ref[t] = new
                decay = jnp.exp2(old - new)
                p = jnp.exp2(s * SCALE - new[:, :1]).astype(BF16)
                acc_ref[t] = acc_ref[t] * jnp.concatenate([decay, decay], axis=1) + dot(p, v)
                return 0

            lax.fori_loop(jnp.where(allowed == 1, 0, GROUP), TILES, tile, 0)

        for ref, shift in zip(far, shifts):
            for i in range(1 if shift == 0 else 0, NY):
                copy = pltpu.make_async_copy(ref.at[i], buf_ref, sem)
                copy.start()
                copy.wait()
                online(seen(place_ref, shift, i))
        for i, chunk in enumerate(chunks):
            buf_ref[...] = chunk[...]
            online(last_flags[i])
        write_rows(out_ref, acc_ref)

    for fetch in fetches:
        fetch.wait()


def last_block(place, q, m, acc, near, acc0, weight, received, far, shifts):
    n = sum(s.shape[0] for s in near)
    scores = TILES * CHUNK * n * CHUNK
    half = pltpu.VMEM((weight.shape[0], weight.shape[1] // 2), BF16)
    return pl.pallas_call(
        functools.partial(last_kernel, len(near), shifts),
        out_shape=[jax.ShapeDtypeStruct((CHUNK + BRANCH_ROWS, GROUP * HEAD_SIZE), BF16), half, half],
        in_specs=[SMEM]
        + [VMEM] * (4 + len(near))
        + [HBM, pl.BlockSpec(memory_space=pl.ANY)]
        + [HBM] * len(far),
        out_specs=[VMEM] * 3,
        scratch_shapes=[
            pltpu.VMEM(acc.shape, F32),
            pltpu.VMEM((2, n, CHUNK, 2 * HEAD_SIZE), BF16),
            pltpu.VMEM(m.shape, F32),
            pltpu.VMEM((2 * CHUNK, HEAD_SIZE), BF16),
            pltpu.SemaphoreType.DMA(()),
            pltpu.SemaphoreType.DMA((NX + 1,)),
        ],
        compiler_params=pltpu.CompilerParams(vmem_limit_bytes=24 << 20),
        cost_estimate=pl.CostEstimate(
            flops=scores * 768, bytes_accessed=8 << 20, transcendentals=scores
        ),
    )(
        place,
        in_vmem(q),
        in_vmem(m),
        in_vmem(acc),
        *near,
        in_vmem(acc0),
        in_hbm(weight),
        received,
        *[in_hbm(a) for a in far],
    )


def columns_kernel(place_ref, w_ref, o_ref, sems):
    width = o_ref.shape[1] // NX
    copies = []
    for k in range(NX):
        chip = (place_ref[2] + k) % NX
        first = pl.multiple_of((chip * 2 + 1 - place_ref[3]) * width, 128)
        copies.append(
            pltpu.make_async_copy(
                w_ref.at[:, pl.ds(first, width)], o_ref.at[:, pl.ds(k * width, width)], sems.at[k]
            )
        )
    for copy in copies:
        copy.start()
    for copy in copies:
        copy.wait()


def columns_for_other(weight, place):
    return pl.pallas_call(
        columns_kernel,
        out_shape=pltpu.VMEM((weight.shape[0], weight.shape[1] // 2), BF16),
        in_specs=[SMEM, HBM],
        out_specs=VMEM,
        scratch_shapes=[pltpu.SemaphoreType.DMA((NX,))],
        compiler_params=pltpu.CompilerParams(vmem_limit_bytes=8 << 20),
        cost_estimate=pl.CostEstimate(
            flops=0, bytes_accessed=2 * weight.size, transcendentals=0
        ),
    )(place, in_hbm(weight))


def own_kernel(a_ref, w_ref, o_ref):
    width = o_ref.shape[2]

    def step(k, _):
        first = pl.multiple_of(k * width, 128)
        o_ref[k] = dot(a_ref[...], w_ref[:, pl.ds(first, width)])
        return 0

    lax.fori_loop(0, NX, step, 0)


def own_products(attn, mine, width):
    rows, depth = attn.shape
    return pl.pallas_call(
        own_kernel,
        out_shape=jax.ShapeDtypeStruct((NX, rows, width), F32),
        in_specs=[VMEM] * 2,
        out_specs=VMEM,
        compiler_params=pltpu.CompilerParams(vmem_limit_bytes=16 << 20),
        cost_estimate=pl.CostEstimate(
            flops=2 * NX * rows * depth * width, bytes_accessed=0, transcendentals=0
        ),
    )(attn, in_vmem(mine))


def project_kernel(steps, own_ref, b_ref, w_ref, *out_refs):
    half, width = out_refs[0].shape
    for i, k in enumerate(steps):
        o = own_ref[k] + dot(b_ref[...], w_ref[:, k * width : (k + 1) * width])
        out_refs[2 * i][...] = o[:half].astype(BF16)
        out_refs[2 * i + 1][...] = o[half:].astype(BF16)


def project(own, other, theirs, steps):
    _, rows, width = own.shape
    half = jax.ShapeDtypeStruct((rows // 2, width), BF16)
    n = len(steps)
    return pl.pallas_call(
        functools.partial(project_kernel, steps),
        out_shape=[half] * (2 * n),
        in_specs=[VMEM] * 3,
        out_specs=[VMEM] * (2 * n),
        compiler_params=pltpu.CompilerParams(vmem_limit_bytes=20 << 20),
        cost_estimate=pl.CostEstimate(
            flops=2 * n * rows * other.shape[1] * width, bytes_accessed=0, transcendentals=0
        ),
    )(in_vmem(own), other, in_vmem(theirs))


def sum_kernel(o_ref, b0, b1, c0, c1, doc_ref, branch_ref):
    half = b0.shape[0]
    low = o_ref[:half] + b0[...].astype(F32) + c0[...].astype(F32)
    high = o_ref[half:] + b1[...].astype(F32) + c1[...].astype(F32)
    rest = CHUNK - half
    doc_ref[:half, :] = low.astype(BF16)
    doc_ref[half:, :] = high[:rest].astype(BF16)
    branch_ref[...] = high[rest:].astype(BF16)


def home_kernel(own_ref, b_ref, w_ref, o_ref):
    o_ref[...] = own_ref[0] + dot(b_ref[...], w_ref[:, : o_ref.shape[1]])


def body(
    document_query,
    document_key,
    document_value,
    branch_token_query,
    branch_token_key,
    branch_token_value,
    branch_cached_key,
    branch_cached_value,
    suffix_length,
    out_weight,
):
    seq = lax.axis_index("seq")
    head = lax.axis_index("head")
    y, z = seq // NZ, seq % NZ
    x, core = head // 2, head % 2
    width = out_weight.shape[1] // (2 * NX)

    def send(a, pairs, axis="seq"):
        return lax.ppermute(a, axis, pairs)

    def together(*a):
        return lax.optimization_barrier(a)

    place = jnp.stack([y, z, x, core]).astype(jnp.int32)
    kv = pack(document_key, document_value)
    from_down = send(kv, y_shift(1))
    from_up = send(kv, y_shift(-1))
    kv, weight = together(kv, out_weight)
    for_other = columns_for_other(weight, place)
    from_down, for_other = together(from_down, for_other)
    from_far = send(from_down, y_shift(1))
    from_up, for_other = together(from_up, for_other)
    received = send(for_other, core_swap(), "head")
    column = jnp.stack([kv, from_up, from_far, from_down])
    column, kv = together(column, kv)
    right = send(column, z_shift(1))
    left = send(column, z_shift(-1))

    branch_q = branch_token_query.reshape(BRANCH_ROWS, GROUP * HEAD_SIZE)
    pad = ((0, 128 - BRANCH_ROWS), (0, 0))
    fresh_k = jnp.pad(branch_token_key.reshape(BRANCH_ROWS, HEAD_SIZE), pad)
    fresh_v = jnp.pad(branch_token_value.reshape(BRANCH_ROWS, HEAD_SIZE), pad)
    cached_k = branch_cached_key.reshape(-1, HEAD_SIZE)
    cached_v = branch_cached_value.reshape(-1, HEAD_SIZE)
    q, acc0, m = pl.pallas_call(
        local_kernel,
        out_shape=[
            pltpu.VMEM((TILES, CHUNK, HEAD_SIZE), BF16),
            pltpu.VMEM((TILES, CHUNK, 2 * HEAD_SIZE), F32),
            pltpu.VMEM((TILES, CHUNK, 128), F32),
        ],
        in_specs=[SMEM, HBM, VMEM, VMEM, HBM, HBM, VMEM, VMEM],
        out_specs=[VMEM] * 3,
        scratch_shapes=[
            pltpu.VMEM((CHUNK, 2 * HEAD_SIZE), BF16),
            pltpu.VMEM((cached_v.shape[0], 2 * HEAD_SIZE), BF16),
            pltpu.VMEM((128, 2 * HEAD_SIZE), BF16),
            pltpu.VMEM(document_query.shape, BF16),
            pltpu.VMEM(cached_k.shape, BF16),
            pltpu.VMEM(cached_v.shape, BF16),
            pltpu.SemaphoreType.DMA((3,)),
        ],
        compiler_params=pltpu.CompilerParams(vmem_limit_bytes=24 << 20),
        cost_estimate=pl.CostEstimate(
            flops=4 << 30, bytes_accessed=8 << 20, transcendentals=2 << 20
        ),
    )(
        suffix_length,
        in_hbm(document_query),
        branch_q,
        kv,
        in_hbm(cached_k),
        in_hbm(cached_v),
        fresh_k,
        fresh_v,
    )
    acc = block(place, q, m, acc0, [column], (0,), first=1, alias=False)
    far, shifts = [column], [0]

    for s in (1, 2, 3):
        right, left, acc = together(right, left, acc)
        if s < 3:
            next_right = send(right, z_shift(1))
            next_left = send(left, z_shift(-1))
        else:
            next_right = send(right[:2], z_shift(1))
            next_left = send(left[2:], z_shift(-1))
        acc = block(place, q, m, acc, [right, left], (-s, s), first=0, alias=True)
        far += [right, left]
        shifts += [-s, s]
        right, left = next_right, next_left
    right, left, acc = together(right, left, acc)
    attn, mine, theirs = last_block(
        place, q, m, acc, [right, left], acc0, out_weight, received, far, tuple(shifts)
    )

    other = send(attn, core_swap(), "head")
    own = own_products(attn, mine, width)
    other, own = together(other, own)
    a0, a1 = project(own, other, theirs, (2,))
    via_up = send(a0, x_shift(1), "head")
    via_down = send(a1, x_shift(-1), "head")
    u0, u1, d0, d1 = project(own, other, theirs, (1, 3))
    high_up = send(u1, x_shift(1), "head")
    low_down = send(d0, x_shift(-1), "head")

    def add(a, b):
        return (a.astype(F32) + b.astype(F32)).astype(BF16)

    low_up = send(add(u0, via_up), x_shift(1), "head")
    high_down = send(add(d1, via_down), x_shift(-1), "head")
    home = pl.pallas_call(
        home_kernel,
        out_shape=jax.ShapeDtypeStruct(own.shape[1:], F32),
        in_specs=[VMEM] * 3,
        out_specs=VMEM,
        compiler_params=pltpu.CompilerParams(vmem_limit_bytes=20 << 20),
        cost_estimate=pl.CostEstimate(flops=1 << 29, bytes_accessed=0, transcendentals=0),
    )(own, other, theirs)
    doc_out, branch_out = pl.pallas_call(
        sum_kernel,
        out_shape=[
            jax.ShapeDtypeStruct((CHUNK, width), BF16),
            jax.ShapeDtypeStruct((BRANCH_ROWS, width), BF16),
        ],
        in_specs=[VMEM] * 5,
        out_specs=[VMEM] * 2,
        compiler_params=pltpu.CompilerParams(vmem_limit_bytes=16 << 20),
    )(home, low_up, high_up, low_down, high_down)
    return doc_out, branch_out.reshape(-1, NEW_TOKENS, width)


def solution(mesh):
    placed = (
        P("seq", "head"),
        P("seq", "head"),
        P("seq", "head"),
        P("seq", None, "head"),
        P("seq", None, "head"),
        P("seq", None, "head"),
        P("seq", None, "head"),
        P("seq", None, "head"),
        P("seq"),
        P("head", None),
    )
    return jax.shard_map(
        body,
        mesh=mesh,
        in_specs=placed,
        out_specs=(P("seq", "head"), P("seq", None, "head")),
        check_vma=False,
    )
```

```python
import functools
import math

import jax
import jax.numpy as jnp
from jax import lax
from jax.experimental import pallas as pl
from jax.experimental.pallas import tpu as pltpu
from jax.sharding import PartitionSpec as P

HEAD_SIZE = 128
NEW_TOKENS = 4
GROUP = 8
CHUNK = 256
TILES = 10
BRANCH_ROWS = 64
NY, NZ, NX = 4, 8, 4
SCALE = HEAD_SIZE**-0.5 * math.log2(math.e)
NEG = -1e30
VMEM = pl.BlockSpec(memory_space=pltpu.VMEM)
SMEM = pl.BlockSpec(memory_space=pltpu.SMEM)
HBM = pl.BlockSpec(memory_space=pltpu.HBM)
F32 = jnp.float32
BF16 = jnp.bfloat16


def y_shift(k):
    return [(y * NZ + z, ((y + k) % NY) * NZ + z) for y in range(NY) for z in range(NZ)]


def z_shift(k):
    return [(y * NZ + z, y * NZ + (z + k) % NZ) for y in range(NY) for z in range(NZ)]


def x_shift(k):
    return [(x * 2 + c, ((x + k) % NX) * 2 + c) for x in range(NX) for c in range(2)]


def core_swap():
    return [(x * 2 + c, x * 2 + 1 - c) for x in range(NX) for c in range(2)]


def in_hbm(a):
    return pltpu.with_memory_space_constraint(a, pltpu.HBM)


def in_vmem(a):
    return pltpu.with_memory_space_constraint(a, pltpu.VMEM)


def dot_nt(a, b):
    return lax.dot_general(a, b, (((1,), (1,)), ((), ())), preferred_element_type=F32)


def dot(a, b):
    return jnp.dot(a, b, preferred_element_type=F32)


def row_peak(parts):
    cols = [p[:, i : i + 128] for p in parts for i in range(0, p.shape[1], 128)]
    return jnp.max(functools.reduce(jnp.maximum, cols), axis=1, keepdims=True)


def keys_of(chunk):
    return jnp.concatenate([chunk[:HEAD_SIZE], chunk[HEAD_SIZE : 2 * HEAD_SIZE]], axis=1)


def pack_kernel(k_ref, v_ref, o_ref):
    kt = k_ref[...].T
    o_ref[:HEAD_SIZE, :] = kt[:, :HEAD_SIZE]
    o_ref[HEAD_SIZE:CHUNK, :] = kt[:, HEAD_SIZE:]
    o_ref[CHUNK:, :] = v_ref[...]


def pack(k, v):
    return pl.pallas_call(
        pack_kernel,
        out_shape=jax.ShapeDtypeStruct((2 * CHUNK, HEAD_SIZE), BF16),
        in_specs=[VMEM] * 2,
        out_specs=VMEM,
    )(k, v)


def local_kernel(
    len_ref, dq_hbm, bq_ref, kv_ref, ck_hbm, cv_hbm, fk_ref, fv_ref,
    q_ref, acc_ref, m_ref, va_ref, ca_ref, fa_ref, dq_ref, ck_ref, cv_ref, sems
):
    copies = [
        pltpu.make_async_copy(src, dst, sems.at[i])
        for i, (src, dst) in enumerate(((dq_hbm, dq_ref), (ck_hbm, ck_ref), (cv_hbm, cv_ref)))
    ]
    for copy in copies:
        copy.start()
    copies[0].wait()
    for h in range(GROUP):
        lanes = slice(h * HEAD_SIZE, (h + 1) * HEAD_SIZE)
        q_ref[h] = dq_ref[:, lanes]
        rows = slice((h % 4) * BRANCH_ROWS, (h % 4 + 1) * BRANCH_ROWS)
        q_ref[GROUP + h // 4, rows, :] = bq_ref[:, lanes]
    va_ref[:, :HEAD_SIZE] = kv_ref[CHUNK:, :]
    va_ref[:, HEAD_SIZE:] = jnp.ones((CHUNK, HEAD_SIZE), BF16)
    fa_ref[:, :HEAD_SIZE] = fv_ref[...]
    fa_ref[:, HEAD_SIZE:] = jnp.ones((128, HEAD_SIZE), BF16)
    ca_ref[:, HEAD_SIZE:] = jnp.ones((ca_ref.shape[0], HEAD_SIZE), BF16)
    kt = keys_of(kv_ref)
    row = lax.broadcasted_iota(jnp.int32, (CHUNK, CHUNK), 0)
    col = lax.broadcasted_iota(jnp.int32, (CHUNK, CHUNK), 1)
    causal = col <= row

    def doc(t, _):
        s = jnp.where(causal, dot(q_ref[t], kt), NEG)
        m = row_peak([s]) * SCALE
        p = jnp.exp2(s * SCALE - m).astype(BF16)
        m_ref[t] = jnp.broadcast_to(m, (CHUNK, 128))
        acc_ref[t] = dot(p, va_ref[...])
        return 0

    lax.fori_loop(0, GROUP, doc, 0, unroll=4)

    copies[1].wait()
    copies[2].wait()
    ca_ref[:, :HEAD_SIZE] = cv_ref[...]
    row_branch = (row % BRANCH_ROWS) // NEW_TOKENS
    n_cached = ca_ref.shape[0] // CHUNK
    frow = lax.broadcasted_iota(jnp.int32, (CHUNK, 128), 0)
    fcol = lax.broadcasted_iota(jnp.int32, (CHUNK, 128), 1)
    same = (frow % BRANCH_ROWS) // NEW_TOKENS == fcol // NEW_TOKENS
    fresh_keep = same & (fcol % NEW_TOKENS <= frow % NEW_TOKENS)
    low = col < 128
    for t in (8, 9):
        q = q_ref[t]
        parts = [dot(q, kt)]
        for c in range(n_cached):
            s = dot_nt(q, ck_ref[c * CHUNK : (c + 1) * CHUNK, :])
            length = jnp.where(low, len_ref[2 * c], len_ref[2 * c + 1])
            owner = jnp.where(low, 2 * c, 2 * c + 1)
            keep = (row_branch == owner) & (col % 128 < length)
            parts.append(jnp.where(keep, s, NEG))
        parts.append(jnp.where(fresh_keep, dot_nt(q, fk_ref[...]), NEG))
        m = row_peak(parts) * SCALE
        m_ref[t] = jnp.broadcast_to(m, (CHUNK, 128))
        p = [jnp.exp2(s * SCALE - m).astype(BF16) for s in parts]
        total = dot(p[0], va_ref[...])
        for c in range(n_cached):
            total += dot(p[1 + c], ca_ref[c * CHUNK : (c + 1) * CHUNK, :])
        total += dot(p[-1], fa_ref[...])
        acc_ref[t] = total


def seen(place_ref, shift, rel):
    y, z = place_ref[0], place_ref[1]
    if rel:
        return ((y + rel) % NY < y).astype(jnp.int32)
    return ((z + shift) % NZ < z).astype(jnp.int32)


def accumulate(flags, q_ref, m_ref, acc_in, chunks, acc_ref, va_ref):
    ones = jnp.ones((CHUNK, HEAD_SIZE), F32)
    for c, chunk in enumerate(chunks):
        flag = (ones * flags[c].astype(F32)).astype(BF16)
        v = chunk[CHUNK:, :]
        va_ref[0, c, :, :HEAD_SIZE] = v * flag
        va_ref[0, c, :, HEAD_SIZE:] = flag
        va_ref[1, c, :, :HEAD_SIZE] = v
        va_ref[1, c, :, HEAD_SIZE:] = ones.astype(BF16)

    def tile(t, _):
        q = q_ref[t]
        m = m_ref[t]
        group = (t >= GROUP).astype(jnp.int32)
        total = acc_in[t]
        for c, chunk in enumerate(chunks):
            s = dot(q, keys_of(chunk))
            p = [
                jnp.exp2(s[:, i : i + 128] * SCALE - m).astype(BF16) for i in range(0, CHUNK, 128)
            ]
            total = total + dot(jnp.concatenate(p, axis=1), va_ref[group, c])
        acc_ref[t] = total
        return 0

    lax.fori_loop(0, TILES, tile, 0, unroll=5)


def held(pieces):
    return [
        (n, i, shift, first + i)
        for n, (shift, first) in enumerate(pieces)
        for i in range(2)
        if (shift, first + i) != (0, 0)
    ]


def block_kernel(pieces, place_ref, q_ref, m_ref, acc_in, *rest):
    srcs, (acc_ref, va_ref) = rest[:-2], rest[-2:]
    chunks = [srcs[n].at[i] for n, i, _, _ in held(pieces)]
    flags = [seen(place_ref, shift, rel) for _, _, shift, rel in held(pieces)]
    accumulate(flags, q_ref, m_ref, acc_in, chunks, acc_ref, va_ref)


def block(place, q, m, acc, srcs, pieces, alias):
    n = len(held(pieces))
    scores = TILES * CHUNK * n * CHUNK
    return pl.pallas_call(
        functools.partial(block_kernel, pieces),
        out_shape=pltpu.VMEM(acc.shape, F32),
        in_specs=[SMEM] + [VMEM] * (3 + len(srcs)),
        out_specs=VMEM,
        scratch_shapes=[pltpu.VMEM((2, n, CHUNK, 2 * HEAD_SIZE), BF16)],
        input_output_aliases={3: 0} if alias else {},
        compiler_params=pltpu.CompilerParams(vmem_limit_bytes=16 << 20),
        cost_estimate=pl.CostEstimate(
            flops=scores * 768, bytes_accessed=8 << 20, transcendentals=scores
        ),
    )(place, in_vmem(q), in_vmem(m), in_vmem(acc), *srcs)


def write_rows(out_ref, acc_ref):
    for t in range(GROUP):
        o = acc_ref[t, :, :HEAD_SIZE] / acc_ref[t, :, HEAD_SIZE:]
        out_ref[:CHUNK, t * 128 : (t + 1) * 128] = o.astype(BF16)
    for t in range(GROUP, TILES):
        o = (acc_ref[t, :, :HEAD_SIZE] / acc_ref[t, :, HEAD_SIZE:]).astype(BF16)
        for i in range(4):
            h = (t - GROUP) * 4 + i
            out_ref[CHUNK:, h * 128 : (h + 1) * 128] = o[i * BRANCH_ROWS : (i + 1) * BRANCH_ROWS]


def last_kernel(n_near, pieces, place_ref, q_ref, m_ref, acc_in, *rest):
    near = rest[:n_near]
    acc0_ref, weight_ref, received_ref = rest[n_near : n_near + 3]
    out_ref, mine_ref, theirs_ref, acc_ref, va_ref, run_ref, buf_ref, sem, sems = rest[-9:]
    far = rest[n_near + 3 : -9]
    width = mine_ref.shape[1] // NX
    fetches = []
    for k in range(NX):
        chip = (place_ref[2] + k) % NX
        first = pl.multiple_of((chip * 2 + place_ref[3]) * width, 128)
        for i, (src, dst) in enumerate(((weight_ref, mine_ref), (received_ref, theirs_ref))):
            fetches.append(
                pltpu.make_async_copy(
                    src.at[:, pl.ds(first, width)],
                    dst.at[:, pl.ds(k * width, width)],
                    sems.at[2 * k + i],
                )
            )
    for fetch in fetches:
        fetch.start()
    chunks = [s.at[i] for s in near for i in range(s.shape[0])]
    last_flags = [seen(place_ref, NZ // 2, i) for i in range(NY)]
    accumulate(last_flags, q_ref, m_ref, acc_in, chunks, acc_ref, va_ref)
    peak = functools.reduce(jnp.maximum, [acc_ref[t, :, HEAD_SIZE:] for t in range(TILES)])
    lowest = functools.reduce(jnp.minimum, [acc_ref[t, :, HEAD_SIZE:] for t in range(TILES)])
    fine = jnp.min(jnp.where((peak < 1e30) & (lowest > 0), 1.0, 0.0)) > 0.5

    @pl.when(fine)
    def _():
        write_rows(out_ref, acc_ref)

    @pl.when(jnp.logical_not(fine))
    def _():
        acc_ref[...] = acc0_ref[...]
        run_ref[...] = m_ref[...]

        def online(allowed):
            v = jnp.concatenate(
                [buf_ref[CHUNK:, :], jnp.ones((CHUNK, HEAD_SIZE), BF16)], axis=1
            )

            def tile(t, _):
                s = dot(q_ref[t], keys_of(buf_ref))
                old = run_ref[t]
                new = jnp.maximum(old, row_peak([s]) * SCALE)
                run_ref[t] = new
                decay = jnp.exp2(old - new)
                p = jnp.exp2(s * SCALE - new[:, :1]).astype(BF16)
                acc_ref[t] = acc_ref[t] * jnp.concatenate([decay, decay], axis=1) + dot(p, v)
                return 0

            lax.fori_loop(jnp.where(allowed == 1, 0, GROUP), TILES, tile, 0)

        for n, i, shift, rel in held(pieces):
            copy = pltpu.make_async_copy(far[n].at[i], buf_ref, sem)
            copy.start()
            copy.wait()
            online(seen(place_ref, shift, rel))
        for i, chunk in enumerate(chunks):
            buf_ref[...] = chunk[...]
            online(last_flags[i])
        write_rows(out_ref, acc_ref)

    for fetch in fetches:
        fetch.wait()


def last_block(place, q, m, acc, near, acc0, weight, received, far, pieces):
    n = sum(s.shape[0] for s in near)
    scores = TILES * CHUNK * n * CHUNK
    half = pltpu.VMEM((weight.shape[0], weight.shape[1] // 2), BF16)
    return pl.pallas_call(
        functools.partial(last_kernel, len(near), pieces),
        out_shape=[jax.ShapeDtypeStruct((CHUNK + BRANCH_ROWS, GROUP * HEAD_SIZE), BF16), half, half],
        in_specs=[SMEM]
        + [VMEM] * (4 + len(near))
        + [HBM, HBM]
        + [HBM] * len(far),
        out_specs=[VMEM] * 3,
        scratch_shapes=[
            pltpu.VMEM(acc.shape, F32),
            pltpu.VMEM((2, n, CHUNK, 2 * HEAD_SIZE), BF16),
            pltpu.VMEM(m.shape, F32),
            pltpu.VMEM((2 * CHUNK, HEAD_SIZE), BF16),
            pltpu.SemaphoreType.DMA(()),
            pltpu.SemaphoreType.DMA((2 * NX,)),
        ],
        compiler_params=pltpu.CompilerParams(vmem_limit_bytes=24 << 20),
        cost_estimate=pl.CostEstimate(
            flops=scores * 768, bytes_accessed=8 << 20, transcendentals=scores
        ),
    )(
        place,
        in_vmem(q),
        in_vmem(m),
        in_vmem(acc),
        *near,
        in_vmem(acc0),
        in_hbm(weight),
        in_hbm(received),
        *[in_hbm(a) for a in far],
    )


def own_kernel(a_ref, w_ref, o_ref):
    width = o_ref.shape[2]

    def step(k, _):
        first = pl.multiple_of(k * width, 128)
        o_ref[k] = dot(a_ref[...], w_ref[:, pl.ds(first, width)])
        return 0

    lax.fori_loop(0, NX, step, 0)


def own_products(attn, mine, width):
    rows, depth = attn.shape
    return pl.pallas_call(
        own_kernel,
        out_shape=jax.ShapeDtypeStruct((NX, rows, width), F32),
        in_specs=[VMEM] * 2,
        out_specs=VMEM,
        compiler_params=pltpu.CompilerParams(vmem_limit_bytes=16 << 20),
        cost_estimate=pl.CostEstimate(
            flops=2 * NX * rows * depth * width, bytes_accessed=0, transcendentals=0
        ),
    )(attn, in_vmem(mine))


def project_kernel(steps, own_ref, b_ref, w_ref, *out_refs):
    half, width = out_refs[0].shape
    for i, k in enumerate(steps):
        o = own_ref[k] + dot(b_ref[...], w_ref[:, k * width : (k + 1) * width])
        out_refs[2 * i][...] = o[:half].astype(BF16)
        out_refs[2 * i + 1][...] = o[half:].astype(BF16)


def project(own, other, theirs, steps):
    _, rows, width = own.shape
    half = jax.ShapeDtypeStruct((rows // 2, width), BF16)
    n = len(steps)
    return pl.pallas_call(
        functools.partial(project_kernel, steps),
        out_shape=[half] * (2 * n),
        in_specs=[VMEM] * 3,
        out_specs=[VMEM] * (2 * n),
        compiler_params=pltpu.CompilerParams(vmem_limit_bytes=20 << 20),
        cost_estimate=pl.CostEstimate(
            flops=2 * n * rows * other.shape[1] * width, bytes_accessed=0, transcendentals=0
        ),
    )(in_vmem(own), other, in_vmem(theirs))


def sum_kernel(o_ref, b0, b1, c0, c1, doc_ref, branch_ref):
    half = b0.shape[0]
    low = o_ref[:half] + b0[...].astype(F32) + c0[...].astype(F32)
    high = o_ref[half:] + b1[...].astype(F32) + c1[...].astype(F32)
    rest = CHUNK - half
    doc_ref[:half, :] = low.astype(BF16)
    doc_ref[half:, :] = high[:rest].astype(BF16)
    branch_ref[...] = high[rest:].astype(BF16)


def home_kernel(own_ref, b_ref, w_ref, o_ref):
    o_ref[...] = own_ref[0] + dot(b_ref[...], w_ref[:, : o_ref.shape[1]])


def body(
    document_query,
    document_key,
    document_value,
    branch_token_query,
    branch_token_key,
    branch_token_value,
    branch_cached_key,
    branch_cached_value,
    suffix_length,
    out_weight,
):
    seq = lax.axis_index("seq")
    head = lax.axis_index("head")
    y, z = seq // NZ, seq % NZ
    x, core = head // 2, head % 2
    width = out_weight.shape[1] // (2 * NX)

    def send(a, pairs, axis="seq"):
        return lax.ppermute(a, axis, pairs)

    def together(*a):
        return lax.optimization_barrier(a)

    place = jnp.stack([y, z, x, core]).astype(jnp.int32)
    kv = pack(document_key, document_value)
    from_down = send(kv, y_shift(1))
    from_up = send(kv, y_shift(-1))
    from_far = send(from_down, y_shift(1))
    received = send(out_weight, core_swap(), "head")
    own_a = jnp.stack([kv, from_up])
    own_a, kv = together(own_a, kv)
    right_a = send(own_a, z_shift(1))
    left_a = send(own_a, z_shift(-1))

    branch_q = branch_token_query.reshape(BRANCH_ROWS, GROUP * HEAD_SIZE)
    pad = ((0, 128 - BRANCH_ROWS), (0, 0))
    fresh_k = jnp.pad(branch_token_key.reshape(BRANCH_ROWS, HEAD_SIZE), pad)
    fresh_v = jnp.pad(branch_token_value.reshape(BRANCH_ROWS, HEAD_SIZE), pad)
    cached_k = branch_cached_key.reshape(-1, HEAD_SIZE)
    cached_v = branch_cached_value.reshape(-1, HEAD_SIZE)
    q, acc0, m = pl.pallas_call(
        local_kernel,
        out_shape=[
            pltpu.VMEM((TILES, CHUNK, HEAD_SIZE), BF16),
            pltpu.VMEM((TILES, CHUNK, 2 * HEAD_SIZE), F32),
            pltpu.VMEM((TILES, CHUNK, 128), F32),
        ],
        in_specs=[SMEM, HBM, VMEM, VMEM, HBM, HBM, VMEM, VMEM],
        out_specs=[VMEM] * 3,
        scratch_shapes=[
            pltpu.VMEM((CHUNK, 2 * HEAD_SIZE), BF16),
            pltpu.VMEM((cached_v.shape[0], 2 * HEAD_SIZE), BF16),
            pltpu.VMEM((128, 2 * HEAD_SIZE), BF16),
            pltpu.VMEM(document_query.shape, BF16),
            pltpu.VMEM(cached_k.shape, BF16),
            pltpu.VMEM(cached_v.shape, BF16),
            pltpu.SemaphoreType.DMA((3,)),
        ],
        compiler_params=pltpu.CompilerParams(vmem_limit_bytes=24 << 20),
        cost_estimate=pl.CostEstimate(
            flops=4 << 30, bytes_accessed=8 << 20, transcendentals=2 << 20
        ),
    )(
        suffix_length,
        in_hbm(document_query),
        branch_q,
        kv,
        in_hbm(cached_k),
        in_hbm(cached_v),
        fresh_k,
        fresh_v,
    )
    from_far, m = together(from_far, m)
    own_b = jnp.stack([from_far, from_down])
    right_b = send(own_b, z_shift(1))
    left_b = send(own_b, z_shift(-1))
    far, pieces = [own_a, own_b], [(0, 0), (0, 2)]
    acc = block(place, q, m, acc0, far, tuple(pieces), alias=False)
    for s in (1, 2, 3):
        here = ((-s, 0), (s, 0)), ((-s, 2), (s, 2))
        right_a, left_a, acc = together(right_a, left_a, acc)
        next_right_a = send(right_a, z_shift(1))
        if s < 3:
            next_left_a = send(left_a, z_shift(-1))
        acc = block(place, q, m, acc, [right_a, left_a], here[0], alias=True)
        right_b, left_b, acc = together(right_b, left_b, acc)
        next_left_b = send(left_b, z_shift(-1))
        if s < 3:
            next_right_b = send(right_b, z_shift(1))
        acc = block(place, q, m, acc, [right_b, left_b], here[1], alias=True)
        far += [right_a, left_a, right_b, left_b]
        pieces += here[0] + here[1]
        right_a, left_b = next_right_a, next_left_b
        left_a, right_b = next_left_a, next_right_b
    right_a, left_b, acc = together(right_a, left_b, acc)
    attn, mine, theirs = last_block(
        place, q, m, acc, [right_a, left_b], acc0, out_weight, received, far, tuple(pieces)
    )

    other = send(attn, core_swap(), "head")
    own = own_products(attn, mine, width)
    other, own = together(other, own)
    a0, a1 = project(own, other, theirs, (2,))
    via_up = send(a0, x_shift(1), "head")
    via_down = send(a1, x_shift(-1), "head")
    u0, u1, d0, d1 = project(own, other, theirs, (1, 3))
    high_up = send(u1, x_shift(1), "head")
    low_down = send(d0, x_shift(-1), "head")

    def add(a, b):
        return (a.astype(F32) + b.astype(F32)).astype(BF16)

    low_up = send(add(u0, via_up), x_shift(1), "head")
    high_down = send(add(d1, via_down), x_shift(-1), "head")
    home = pl.pallas_call(
        home_kernel,
        out_shape=jax.ShapeDtypeStruct(own.shape[1:], F32),
        in_specs=[VMEM] * 3,
        out_specs=VMEM,
        compiler_params=pltpu.CompilerParams(vmem_limit_bytes=20 << 20),
        cost_estimate=pl.CostEstimate(flops=1 << 29, bytes_accessed=0, transcendentals=0),
    )(own, other, theirs)
    doc_out, branch_out = pl.pallas_call(
        sum_kernel,
        out_shape=[
            jax.ShapeDtypeStruct((CHUNK, width), BF16),
            jax.ShapeDtypeStruct((BRANCH_ROWS, width), BF16),
        ],
        in_specs=[VMEM] * 5,
        out_specs=[VMEM] * 2,
        compiler_params=pltpu.CompilerParams(vmem_limit_bytes=16 << 20),
    )(home, low_up, high_up, low_down, high_down)
    return doc_out, branch_out.reshape(-1, NEW_TOKENS, width)


def solution(mesh):
    placed = (
        P("seq", "head"),
        P("seq", "head"),
        P("seq", "head"),
        P("seq", None, "head"),
        P("seq", None, "head"),
        P("seq", None, "head"),
        P("seq", None, "head"),
        P("seq", None, "head"),
        P("seq"),
        P("head", None),
    )
    return jax.shard_map(
        body,
        mesh=mesh,
        in_specs=placed,
        out_specs=(P("seq", "head"), P("seq", None, "head")),
        check_vma=False,
    )
```

```python
import functools
import math

import jax
import jax.numpy as jnp
from jax import lax
from jax.experimental import pallas as pl
from jax.experimental.pallas import tpu as pltpu
from jax.sharding import PartitionSpec as P

HEAD_SIZE = 128
NEW_TOKENS = 4
GROUP = 8
CHUNK = 256
TILES = 10
BRANCH_ROWS = 64
NY, NZ, NX = 4, 8, 4
SCALE = HEAD_SIZE**-0.5 * math.log2(math.e)
NEG = -1e30
VMEM = pl.BlockSpec(memory_space=pltpu.VMEM)
SMEM = pl.BlockSpec(memory_space=pltpu.SMEM)
HBM = pl.BlockSpec(memory_space=pltpu.HBM)
F32 = jnp.float32
BF16 = jnp.bfloat16


def y_shift(k):
    return [(y * NZ + z, ((y + k) % NY) * NZ + z) for y in range(NY) for z in range(NZ)]


def z_shift(k):
    return [(y * NZ + z, y * NZ + (z + k) % NZ) for y in range(NY) for z in range(NZ)]


def x_shift(k):
    return [(x * 2 + c, ((x + k) % NX) * 2 + c) for x in range(NX) for c in range(2)]


def core_swap():
    return [(x * 2 + c, x * 2 + 1 - c) for x in range(NX) for c in range(2)]


def in_hbm(a):
    return pltpu.with_memory_space_constraint(a, pltpu.HBM)


def in_vmem(a):
    return pltpu.with_memory_space_constraint(a, pltpu.VMEM)


def dot_nt(a, b):
    return lax.dot_general(a, b, (((1,), (1,)), ((), ())), preferred_element_type=F32)


def dot(a, b):
    return jnp.dot(a, b, preferred_element_type=F32)


def row_peak(parts):
    cols = [p[:, i : i + 128] for p in parts for i in range(0, p.shape[1], 128)]
    return jnp.max(functools.reduce(jnp.maximum, cols), axis=1, keepdims=True)


def keys_of(chunk):
    return jnp.concatenate([chunk[:HEAD_SIZE], chunk[HEAD_SIZE : 2 * HEAD_SIZE]], axis=1)


def pack_kernel(k_ref, v_ref, o_ref):
    kt = k_ref[...].T
    o_ref[:HEAD_SIZE, :] = kt[:, :HEAD_SIZE]
    o_ref[HEAD_SIZE:CHUNK, :] = kt[:, HEAD_SIZE:]
    o_ref[CHUNK:, :] = v_ref[...]


def pack(k, v):
    return pl.pallas_call(
        pack_kernel,
        out_shape=jax.ShapeDtypeStruct((2 * CHUNK, HEAD_SIZE), BF16),
        in_specs=[VMEM] * 2,
        out_specs=VMEM,
    )(k, v)


def local_kernel(
    len_ref, dq_hbm, bq_ref, kv_ref, ck_hbm, cv_hbm, fk_ref, fv_ref,
    q_ref, acc_ref, m_ref, va_ref, ca_ref, fa_ref, dq_ref, ck_ref, cv_ref, sems
):
    copies = [
        pltpu.make_async_copy(src, dst, sems.at[i])
        for i, (src, dst) in enumerate(((dq_hbm, dq_ref), (ck_hbm, ck_ref), (cv_hbm, cv_ref)))
    ]
    for copy in copies:
        copy.start()
    copies[0].wait()
    for h in range(GROUP):
        lanes = slice(h * HEAD_SIZE, (h + 1) * HEAD_SIZE)
        q_ref[h] = dq_ref[:, lanes]
        rows = slice((h % 4) * BRANCH_ROWS, (h % 4 + 1) * BRANCH_ROWS)
        q_ref[GROUP + h // 4, rows, :] = bq_ref[:, lanes]
    va_ref[:, :HEAD_SIZE] = kv_ref[CHUNK:, :]
    va_ref[:, HEAD_SIZE:] = jnp.ones((CHUNK, HEAD_SIZE), BF16)
    fa_ref[:, :HEAD_SIZE] = fv_ref[...]
    fa_ref[:, HEAD_SIZE:] = jnp.ones((128, HEAD_SIZE), BF16)
    ca_ref[:, HEAD_SIZE:] = jnp.ones((ca_ref.shape[0], HEAD_SIZE), BF16)
    kt = keys_of(kv_ref)
    row = lax.broadcasted_iota(jnp.int32, (CHUNK, CHUNK), 0)
    col = lax.broadcasted_iota(jnp.int32, (CHUNK, CHUNK), 1)
    causal = col <= row

    def doc(t, _):
        s = jnp.where(causal, dot(q_ref[t], kt), NEG)
        m = row_peak([s]) * SCALE
        p = jnp.exp2(s * SCALE - m).astype(BF16)
        m_ref[t] = jnp.broadcast_to(m, (CHUNK, 128))
        acc_ref[t] = dot(p, va_ref[...])
        return 0

    lax.fori_loop(0, GROUP, doc, 0, unroll=4)

    copies[1].wait()
    copies[2].wait()
    ca_ref[:, :HEAD_SIZE] = cv_ref[...]
    row_branch = (row % BRANCH_ROWS) // NEW_TOKENS
    n_cached = ca_ref.shape[0] // CHUNK
    frow = lax.broadcasted_iota(jnp.int32, (CHUNK, 128), 0)
    fcol = lax.broadcasted_iota(jnp.int32, (CHUNK, 128), 1)
    same = (frow % BRANCH_ROWS) // NEW_TOKENS == fcol // NEW_TOKENS
    fresh_keep = same & (fcol % NEW_TOKENS <= frow % NEW_TOKENS)
    low = col < 128
    for t in (8, 9):
        q = q_ref[t]
        parts = [dot(q, kt)]
        for c in range(n_cached):
            s = dot_nt(q, ck_ref[c * CHUNK : (c + 1) * CHUNK, :])
            length = jnp.where(low, len_ref[2 * c], len_ref[2 * c + 1])
            owner = jnp.where(low, 2 * c, 2 * c + 1)
            keep = (row_branch == owner) & (col % 128 < length)
            parts.append(jnp.where(keep, s, NEG))
        parts.append(jnp.where(fresh_keep, dot_nt(q, fk_ref[...]), NEG))
        m = row_peak(parts) * SCALE
        m_ref[t] = jnp.broadcast_to(m, (CHUNK, 128))
        p = [jnp.exp2(s * SCALE - m).astype(BF16) for s in parts]
        total = dot(p[0], va_ref[...])
        for c in range(n_cached):
            total += dot(p[1 + c], ca_ref[c * CHUNK : (c + 1) * CHUNK, :])
        total += dot(p[-1], fa_ref[...])
        acc_ref[t] = total


def seen(place_ref, shift, rel):
    y, z = place_ref[0], place_ref[1]
    if rel:
        return ((y + rel) % NY < y).astype(jnp.int32)
    return ((z + shift) % NZ < z).astype(jnp.int32)


def accumulate(flags, q_ref, m_ref, acc_in, chunks, acc_ref, va_ref):
    ones = jnp.ones((CHUNK, HEAD_SIZE), F32)
    for c, chunk in enumerate(chunks):
        flag = (ones * flags[c].astype(F32)).astype(BF16)
        v = chunk[CHUNK:, :]
        va_ref[0, c, :, :HEAD_SIZE] = v * flag
        va_ref[0, c, :, HEAD_SIZE:] = flag
        va_ref[1, c, :, :HEAD_SIZE] = v
        va_ref[1, c, :, HEAD_SIZE:] = ones.astype(BF16)

    def tile(t, _):
        q = q_ref[t]
        m = m_ref[t]
        group = (t >= GROUP).astype(jnp.int32)
        total = acc_in[t]
        for c, chunk in enumerate(chunks):
            s = dot(q, keys_of(chunk))
            p = [
                jnp.exp2(s[:, i : i + 128] * SCALE - m).astype(BF16) for i in range(0, CHUNK, 128)
            ]
            total = total + dot(jnp.concatenate(p, axis=1), va_ref[group, c])
        acc_ref[t] = total
        return 0

    lax.fori_loop(0, TILES, tile, 0, unroll=5)


def block_kernel(first, shifts, place_ref, q_ref, m_ref, acc_in, *rest):
    srcs, (acc_ref, va_ref) = rest[:-2], rest[-2:]
    chunks = [s.at[i] for s in srcs for i in range(first, NY)]
    flags = [seen(place_ref, shift, i) for shift in shifts for i in range(first, NY)]
    accumulate(flags, q_ref, m_ref, acc_in, chunks, acc_ref, va_ref)


def block(place, q, m, acc, srcs, shifts, first, alias):
    n = sum(s.shape[0] - first for s in srcs)
    scores = TILES * CHUNK * n * CHUNK
    return pl.pallas_call(
        functools.partial(block_kernel, first, shifts),
        out_shape=pltpu.VMEM(acc.shape, F32),
        in_specs=[SMEM] + [VMEM] * (3 + len(srcs)),
        out_specs=VMEM,
        scratch_shapes=[pltpu.VMEM((2, n, CHUNK, 2 * HEAD_SIZE), BF16)],
        input_output_aliases={3: 0} if alias else {},
        compiler_params=pltpu.CompilerParams(vmem_limit_bytes=16 << 20),
        cost_estimate=pl.CostEstimate(
            flops=scores * 768, bytes_accessed=8 << 20, transcendentals=scores
        ),
    )(place, in_vmem(q), in_vmem(m), in_vmem(acc), *srcs)


def write_rows(out_ref, acc_ref):
    for t in range(GROUP):
        o = acc_ref[t, :, :HEAD_SIZE] / acc_ref[t, :, HEAD_SIZE:]
        out_ref[:CHUNK, t * 128 : (t + 1) * 128] = o.astype(BF16)
    for t in range(GROUP, TILES):
        o = (acc_ref[t, :, :HEAD_SIZE] / acc_ref[t, :, HEAD_SIZE:]).astype(BF16)
        for i in range(4):
            h = (t - GROUP) * 4 + i
            out_ref[CHUNK:, h * 128 : (h + 1) * 128] = o[i * BRANCH_ROWS : (i + 1) * BRANCH_ROWS]


def last_kernel(n_near, shifts, place_ref, q_ref, m_ref, acc_in, *rest):
    near = rest[:n_near]
    acc0_ref, weight_ref, received_ref = rest[n_near : n_near + 3]
    out_ref, mine_ref, theirs_ref, acc_ref, va_ref, run_ref, buf_ref, sem, sems = rest[-9:]
    far = rest[n_near + 3 : -9]
    width = mine_ref.shape[1] // NX
    fetches = []
    for k in range(NX):
        chip = (place_ref[2] + k) % NX
        first = pl.multiple_of((chip * 2 + place_ref[3]) * width, 128)
        for i, (src, dst) in enumerate(((weight_ref, mine_ref), (received_ref, theirs_ref))):
            fetches.append(
                pltpu.make_async_copy(
                    src.at[:, pl.ds(first, width)],
                    dst.at[:, pl.ds(k * width, width)],
                    sems.at[2 * k + i],
                )
            )
    for fetch in fetches:
        fetch.start()
    chunks = [s.at[i] for s in near for i in range(s.shape[0])]
    last_flags = [seen(place_ref, NZ // 2, i) for i in range(NY)]
    accumulate(last_flags, q_ref, m_ref, acc_in, chunks, acc_ref, va_ref)
    peak = functools.reduce(jnp.maximum, [acc_ref[t, :, HEAD_SIZE:] for t in range(TILES)])
    lowest = functools.reduce(jnp.minimum, [acc_ref[t, :, HEAD_SIZE:] for t in range(TILES)])
    fine = jnp.min(jnp.where((peak < 1e30) & (lowest > 0), 1.0, 0.0)) > 0.5

    @pl.when(fine)
    def _():
        write_rows(out_ref, acc_ref)

    @pl.when(jnp.logical_not(fine))
    def _():
        acc_ref[...] = acc0_ref[...]
        run_ref[...] = m_ref[...]

        def online(allowed):
            v = jnp.concatenate(
                [buf_ref[CHUNK:, :], jnp.ones((CHUNK, HEAD_SIZE), BF16)], axis=1
            )

            def tile(t, _):
                s = dot(q_ref[t], keys_of(buf_ref))
                old = run_ref[t]
                new = jnp.maximum(old, row_peak([s]) * SCALE)
                run_ref[t] = new
                decay = jnp.exp2(old - new)
                p = jnp.exp2(s * SCALE - new[:, :1]).astype(BF16)
                acc_ref[t] = acc_ref[t] * jnp.concatenate([decay, decay], axis=1) + dot(p, v)
                return 0

            lax.fori_loop(jnp.where(allowed == 1, 0, GROUP), TILES, tile, 0)

        for ref, shift in zip(far, shifts):
            for i in range(1 if shift == 0 else 0, NY):
                copy = pltpu.make_async_copy(ref.at[i], buf_ref, sem)
                copy.start()
                copy.wait()
                online(seen(place_ref, shift, i))
        for i, chunk in enumerate(chunks):
            buf_ref[...] = chunk[...]
            online(last_flags[i])
        write_rows(out_ref, acc_ref)

    for fetch in fetches:
        fetch.wait()


def last_block(place, q, m, acc, near, acc0, weight, received, far, shifts):
    n = sum(s.shape[0] for s in near)
    scores = TILES * CHUNK * n * CHUNK
    half = pltpu.VMEM((weight.shape[0], weight.shape[1] // 2), BF16)
    return pl.pallas_call(
        functools.partial(last_kernel, len(near), shifts),
        out_shape=[jax.ShapeDtypeStruct((CHUNK + BRANCH_ROWS, GROUP * HEAD_SIZE), BF16), half, half],
        in_specs=[SMEM]
        + [VMEM] * (4 + len(near))
        + [HBM, HBM]
        + [HBM] * len(far),
        out_specs=[VMEM] * 3,
        scratch_shapes=[
            pltpu.VMEM(acc.shape, F32),
            pltpu.VMEM((2, n, CHUNK, 2 * HEAD_SIZE), BF16),
            pltpu.VMEM(m.shape, F32),
            pltpu.VMEM((2 * CHUNK, HEAD_SIZE), BF16),
            pltpu.SemaphoreType.DMA(()),
            pltpu.SemaphoreType.DMA((2 * NX,)),
        ],
        compiler_params=pltpu.CompilerParams(vmem_limit_bytes=24 << 20),
        cost_estimate=pl.CostEstimate(
            flops=scores * 768, bytes_accessed=8 << 20, transcendentals=scores
        ),
    )(
        place,
        in_vmem(q),
        in_vmem(m),
        in_vmem(acc),
        *near,
        in_vmem(acc0),
        in_hbm(weight),
        in_hbm(received),
        *[in_hbm(a) for a in far],
    )


def own_kernel(a_ref, w_ref, o_ref):
    width = o_ref.shape[2]

    def step(k, _):
        first = pl.multiple_of(k * width, 128)
        o_ref[k] = dot(a_ref[...], w_ref[:, pl.ds(first, width)])
        return 0

    lax.fori_loop(0, NX, step, 0)


def own_products(attn, mine, width):
    rows, depth = attn.shape
    return pl.pallas_call(
        own_kernel,
        out_shape=jax.ShapeDtypeStruct((NX, rows, width), F32),
        in_specs=[VMEM] * 2,
        out_specs=VMEM,
        compiler_params=pltpu.CompilerParams(vmem_limit_bytes=16 << 20),
        cost_estimate=pl.CostEstimate(
            flops=2 * NX * rows * depth * width, bytes_accessed=0, transcendentals=0
        ),
    )(attn, in_vmem(mine))


def project_kernel(steps, own_ref, b_ref, w_ref, *out_refs):
    half, width = out_refs[0].shape
    for i, k in enumerate(steps):
        o = own_ref[k] + dot(b_ref[...], w_ref[:, k * width : (k + 1) * width])
        out_refs[2 * i][...] = o[:half].astype(BF16)
        out_refs[2 * i + 1][...] = o[half:].astype(BF16)


def project(own, other, theirs, steps):
    _, rows, width = own.shape
    half = jax.ShapeDtypeStruct((rows // 2, width), BF16)
    n = len(steps)
    return pl.pallas_call(
        functools.partial(project_kernel, steps),
        out_shape=[half] * (2 * n),
        in_specs=[VMEM] * 3,
        out_specs=[VMEM] * (2 * n),
        compiler_params=pltpu.CompilerParams(vmem_limit_bytes=20 << 20),
        cost_estimate=pl.CostEstimate(
            flops=2 * n * rows * other.shape[1] * width, bytes_accessed=0, transcendentals=0
        ),
    )(in_vmem(own), other, in_vmem(theirs))


def sum_kernel(o_ref, b0, b1, c0, c1, doc_ref, branch_ref):
    half = b0.shape[0]
    low = o_ref[:half] + b0[...].astype(F32) + c0[...].astype(F32)
    high = o_ref[half:] + b1[...].astype(F32) + c1[...].astype(F32)
    rest = CHUNK - half
    doc_ref[:half, :] = low.astype(BF16)
    doc_ref[half:, :] = high[:rest].astype(BF16)
    branch_ref[...] = high[rest:].astype(BF16)


def home_kernel(own_ref, b_ref, w_ref, o_ref):
    o_ref[...] = own_ref[0] + dot(b_ref[...], w_ref[:, : o_ref.shape[1]])


def body(
    document_query,
    document_key,
    document_value,
    branch_token_query,
    branch_token_key,
    branch_token_value,
    branch_cached_key,
    branch_cached_value,
    suffix_length,
    out_weight,
):
    seq = lax.axis_index("seq")
    head = lax.axis_index("head")
    y, z = seq // NZ, seq % NZ
    x, core = head // 2, head % 2
    width = out_weight.shape[1] // (2 * NX)

    def send(a, pairs, axis="seq"):
        return lax.ppermute(a, axis, pairs)

    def together(*a):
        return lax.optimization_barrier(a)

    place = jnp.stack([y, z, x, core]).astype(jnp.int32)
    kv = pack(document_key, document_value)
    from_down = send(kv, y_shift(1))
    from_up = send(kv, y_shift(-1))
    from_far = send(from_down, y_shift(1))
    received = send(out_weight, core_swap(), "head")
    column = jnp.stack([kv, from_up, from_far, from_down])
    column, kv = together(column, kv)
    right = send(column, z_shift(1))
    left = send(column, z_shift(-1))

    branch_q = branch_token_query.reshape(BRANCH_ROWS, GROUP * HEAD_SIZE)
    pad = ((0, 128 - BRANCH_ROWS), (0, 0))
    fresh_k = jnp.pad(branch_token_key.reshape(BRANCH_ROWS, HEAD_SIZE), pad)
    fresh_v = jnp.pad(branch_token_value.reshape(BRANCH_ROWS, HEAD_SIZE), pad)
    cached_k = branch_cached_key.reshape(-1, HEAD_SIZE)
    cached_v = branch_cached_value.reshape(-1, HEAD_SIZE)
    q, acc0, m = pl.pallas_call(
        local_kernel,
        out_shape=[
            pltpu.VMEM((TILES, CHUNK, HEAD_SIZE), BF16),
            pltpu.VMEM((TILES, CHUNK, 2 * HEAD_SIZE), F32),
            pltpu.VMEM((TILES, CHUNK, 128), F32),
        ],
        in_specs=[SMEM, HBM, VMEM, VMEM, HBM, HBM, VMEM, VMEM],
        out_specs=[VMEM] * 3,
        scratch_shapes=[
            pltpu.VMEM((CHUNK, 2 * HEAD_SIZE), BF16),
            pltpu.VMEM((cached_v.shape[0], 2 * HEAD_SIZE), BF16),
            pltpu.VMEM((128, 2 * HEAD_SIZE), BF16),
            pltpu.VMEM(document_query.shape, BF16),
            pltpu.VMEM(cached_k.shape, BF16),
            pltpu.VMEM(cached_v.shape, BF16),
            pltpu.SemaphoreType.DMA((3,)),
        ],
        compiler_params=pltpu.CompilerParams(vmem_limit_bytes=24 << 20),
        cost_estimate=pl.CostEstimate(
            flops=4 << 30, bytes_accessed=8 << 20, transcendentals=2 << 20
        ),
    )(
        suffix_length,
        in_hbm(document_query),
        branch_q,
        kv,
        in_hbm(cached_k),
        in_hbm(cached_v),
        fresh_k,
        fresh_v,
    )
    acc = block(place, q, m, acc0, [column], (0,), first=1, alias=False)
    far, shifts = [column], [0]

    for s in (1, 2, 3):
        right, left, acc = together(right, left, acc)
        if s < 3:
            next_right = send(right, z_shift(1))
            next_left = send(left, z_shift(-1))
        else:
            next_right = send(right[:2], z_shift(1))
            next_left = send(left[2:], z_shift(-1))
        acc = block(place, q, m, acc, [right, left], (-s, s), first=0, alias=True)
        far += [right, left]
        shifts += [-s, s]
        right, left = next_right, next_left
    right, left, acc = together(right, left, acc)
    attn, mine, theirs = last_block(
        place, q, m, acc, [right, left], acc0, out_weight, received, far, tuple(shifts)
    )

    other = send(attn, core_swap(), "head")
    own = own_products(attn, mine, width)
    other, own = together(other, own)
    a0, a1 = project(own, other, theirs, (2,))
    via_up = send(a0, x_shift(1), "head")
    via_down = send(a1, x_shift(-1), "head")
    u0, u1, d0, d1 = project(own, other, theirs, (1, 3))
    high_up = send(u1, x_shift(1), "head")
    low_down = send(d0, x_shift(-1), "head")

    def add(a, b):
        return (a.astype(F32) + b.astype(F32)).astype(BF16)

    low_up = send(add(u0, via_up), x_shift(1), "head")
    high_down = send(add(d1, via_down), x_shift(-1), "head")
    home = pl.pallas_call(
        home_kernel,
        out_shape=jax.ShapeDtypeStruct(own.shape[1:], F32),
        in_specs=[VMEM] * 3,
        out_specs=VMEM,
        compiler_params=pltpu.CompilerParams(vmem_limit_bytes=20 << 20),
        cost_estimate=pl.CostEstimate(flops=1 << 29, bytes_accessed=0, transcendentals=0),
    )(own, other, theirs)
    doc_out, branch_out = pl.pallas_call(
        sum_kernel,
        out_shape=[
            jax.ShapeDtypeStruct((CHUNK, width), BF16),
            jax.ShapeDtypeStruct((BRANCH_ROWS, width), BF16),
        ],
        in_specs=[VMEM] * 5,
        out_specs=[VMEM] * 2,
        compiler_params=pltpu.CompilerParams(vmem_limit_bytes=16 << 20),
    )(home, low_up, high_up, low_down, high_down)
    return doc_out, branch_out.reshape(-1, NEW_TOKENS, width)


def solution(mesh):
    placed = (
        P("seq", "head"),
        P("seq", "head"),
        P("seq", "head"),
        P("seq", None, "head"),
        P("seq", None, "head"),
        P("seq", None, "head"),
        P("seq", None, "head"),
        P("seq", None, "head"),
        P("seq"),
        P("head", None),
    )
    return jax.shard_map(
        body,
        mesh=mesh,
        in_specs=placed,
        out_specs=(P("seq", "head"), P("seq", None, "head")),
        check_vma=False,
    )
```
